32 devices in a mesh: rep: 4 (over y, x), blk: 8 (over z, core).
Axes of the slice: x: 2, y: 2, z: 4, core: 2. Of those that a mesh axis runs over, the one named last changes fastest.
Arguments:
- features: bfloat16 [8, 1024, 128], P('blk', 'rep'), may hold values from -6 to 6
- node_ids: int32 [8, 1024], P('blk', 'rep'), may hold values from 0 to 8388607
- labels: int32 [8, 1024], P('blk', 'rep'), may hold values from 0 to 171
- train_mask: int32 [8, 1024], P('blk', 'rep'), may hold values 0 or 1
- tile_values: bfloat16 [8, 4, 2, 16, 128, 128], P('blk', 'rep'), may hold values from -0.1875 to 0.1875
- tile_place: int32 [8, 4, 2, 16], P('blk', 'rep'), may hold values from 0 to 63, as said below
- tile_count: int32 [8, 4, 2], P('blk', 'rep'), may hold values from 1 to 16, as said below
- weight_in: bfloat16 [128, 256], replicated, may hold values from -0.5 to 0.5
- weight_out: bfloat16 [256, 172], replicated, may hold values from -8 to 8
- class_bias: float32 [172], replicated, may hold values from -5 to 5
Outputs:
- logits: float32 [8, 1024, 172], P('blk', 'rep')
- grad_in: float32 [128, 256], replicated
- grad_out: float32 [256, 172], replicated
The draws below stay inside these ranges and needn't reach their ends.
Inputs may be any that keep to these rules, and one draw needn't show every extreme that they name: `tile_place`: within one block pair the slots name distinct positions. `tile_count`: the live slots of a pair are its first ones; some device has 16 live slots in each of its pairs.
All inputs are finite; a program needn't handle non-finite values. No bound on the sum of `train_mask` on one device may be relied on, other than what follows from the above.
Results may differ from the reference program's by a relative error of at most 0.015.
The reference program's roundings to bfloat16 on the way count: a program that leaves them out, or rounds other values in their place, can miss the bound.
Values may be sent and summed in bfloat16 or wider, within the bound.
No kernel may reach another device: no remote copies, remote signals or barrier semaphores. Data moves between devices by JAX's collectives and lax.ppermute only.
A program may use at most 128 MiB of HBM per device.

```python
import math
import jax
import jax.numpy as jnp
from jax import lax

IN_WIDTH = 128
UNITS = 256
CLASSES = 172
TILE = 128
TMAX = 16
BLOCKS = 8
SECTIONS = 2
BROWS = 1024
TILES_SIDE = 8
NODES = 8192
N_REP = 4


def draw_tile_place(key, part):
    pair_total = BLOCKS * (BLOCKS // SECTIONS) * SECTIONS
    position_total = TILES_SIDE * TILES_SIDE
    pair_keys = jax.random.split(key, pair_total)
    orders = jax.vmap(lambda pair_key: jax.random.permutation(pair_key, position_total)[:TMAX])(pair_keys)
    ascending = jnp.arange(TMAX, dtype=jnp.int32)
    descending = position_total - 1 - ascending
    orders = orders.astype(jnp.int32).at[0].set(descending).at[pair_total - 1].set(ascending)
    return orders.reshape(BLOCKS, BLOCKS // SECTIONS, SECTIONS, TMAX).astype(jnp.int32)


def draw_tile_count(key, part):
    heavy_key, light_key = jax.random.split(key)
    rep_total = BLOCKS // SECTIONS
    heavy_device = jax.random.randint(heavy_key, (BLOCKS, rep_total, 1), 0, 4) == 0
    light_count = jax.random.randint(light_key, (BLOCKS, rep_total, SECTIONS), 1, TMAX // 2 + 1)
    counts = jnp.where(heavy_device, TMAX, light_count).astype(jnp.int32)
    counts = counts.at[0, 0, :].set(TMAX).at[BLOCKS - 1, rep_total - 1, 0].set(1)
    return counts.astype(jnp.int32)


def draw_weight_out(key, part):
    base_key = jax.random.fold_in(key, 0)
    values = jnp.clip(jax.random.normal(base_key, (UNITS, CLASSES), jnp.float32), -6.0, 6.0) * (3.5 / math.sqrt(UNITS))
    return values.astype(jnp.bfloat16)


def draw_class_bias(key, part):
    values = jax.random.uniform(key, (CLASSES,), jnp.float32, -3.0, 3.0)
    return values


def touch_ends(values, rng, smallest, high):
    longest = values.shape.index(max(values.shape))
    spots = []
    for shift in (0, 1):
        where = [jax.random.randint(jax.random.fold_in(rng, axis), (), 0, length) for axis, length in enumerate(values.shape)]
        where[longest] = (where[longest] + shift) % values.shape[longest]
        spots.append(tuple(where))
    return values.at[spots[0]].set(smallest).at[spots[1]].set(high)


def shard_levels(key, shape, shards, low, largest):
    def one(position, blocks):
        draws = jax.random.uniform(jax.random.fold_in(jax.random.fold_in(key, 6), position), (blocks,), jnp.float32, low / len(shards), largest / len(shards))
        return jnp.repeat(jnp.exp(draws), shape[position] // blocks).reshape((-1,) + (1,) * (len(shape) - position - 1))

    loudness = one(*shards[0])
    for cut in shards[1:]:
        loudness = loudness * one(*cut)
    return loudness


def gaussian(rng, shape, scale, most, cuts=(), kind=jnp.bfloat16):
    factor_of = shard_levels(rng, shape, cuts, -0.22, 0.18) if cuts else 1.0
    values = jax.random.normal(rng, shape, jnp.float32) * scale * factor_of
    return jnp.minimum(jnp.maximum(values, -most), most).astype(kind)


def setup_inputs(seed: int = 0) -> dict:
    arg_keys = jax.random.split(jax.random.key(seed), 11)
    features = gaussian(arg_keys[0], (BLOCKS, BROWS, IN_WIDTH), 1.0, 6.0, ((0, 8), (1, 4)))
    node_ids = touch_ends(jax.random.randint(arg_keys[1], (BLOCKS, BROWS), 0, 8388608), jax.random.fold_in(arg_keys[1], 1), 0, 8388607).astype(jnp.int32)
    labels = touch_ends(jax.random.randint(arg_keys[2], (BLOCKS, BROWS), 0, CLASSES), jax.random.fold_in(arg_keys[2], 1), 0, CLASSES - 1).astype(jnp.int32)
    train_mask = touch_ends((jax.random.randint(arg_keys[3], (BLOCKS, BROWS), 0, 2) < 1).astype(jnp.int32), jax.random.fold_in(arg_keys[3], 1), 0, 1)
    tile_values = gaussian(arg_keys[4], (BLOCKS, N_REP, SECTIONS, TMAX, TILE, TILE), (BLOCKS * TMAX * TILE // (2 * TILES_SIDE)) ** -0.5, 0.1875, ((0, 8), (1, 4)))
    tile_place = draw_tile_place(jax.random.fold_in(arg_keys[10], 71), 0)
    tile_count = draw_tile_count(jax.random.fold_in(arg_keys[10], 71), 0)
    weight_in = gaussian(arg_keys[7], (IN_WIDTH, UNITS), IN_WIDTH ** -0.5, 0.5)
    weight_out = draw_weight_out(jax.random.fold_in(arg_keys[10], 71), 0)
    class_bias = draw_class_bias(jax.random.fold_in(arg_keys[10], 71), 0)
    return dict(features=features, node_ids=node_ids, labels=labels, train_mask=train_mask, tile_values=tile_values, tile_place=tile_place, tile_count=tile_count, weight_in=weight_in, weight_out=weight_out, class_bias=class_bias)


def keep_factor(id_values, unit_count):
    columns = jnp.arange(unit_count, dtype=jnp.int32)
    mixed = id_values[:, None] * 73244475 + columns[None, :] * 19349663 + 12345
    mixed = mixed ^ jnp.right_shift(mixed, 15)
    mixed = mixed * 40503
    mixed = mixed ^ jnp.right_shift(mixed, 13)
    kept_mask = jnp.bitwise_and(mixed, 3) != 0
    return jnp.where(kept_mask, jnp.float32(4.0 / 3.0), jnp.float32(0.0))

def forward_section(section_tiles, section_place, section_count, source, tile_side):
    tile_edge = section_tiles.shape[-1]
    feat_width = source.shape[-1]
    pieces = source.reshape(tile_side, tile_edge, feat_width)
    gathered = jnp.take(pieces, section_place % tile_side, axis=0).astype(jnp.float32)
    products = jnp.einsum('tij,tjf->tif', section_tiles.astype(jnp.float32), gathered, precision=lax.Precision.HIGHEST)
    live_slots = jnp.arange(section_tiles.shape[0], dtype=jnp.int32) < section_count
    placing = ((section_place // tile_side)[None, :] == jnp.arange(tile_side, dtype=jnp.int32)[:, None]) & live_slots[None, :]
    summed = jnp.einsum('rt,tif->rif', placing.astype(jnp.float32), products, precision=lax.Precision.HIGHEST)
    return summed.reshape(tile_side * tile_edge, feat_width)

def backward_section(section_tiles, section_place, section_count, source, tile_side):
    tile_edge = section_tiles.shape[-1]
    feat_width = source.shape[-1]
    pieces = source.reshape(tile_side, tile_edge, feat_width)
    gathered = jnp.take(pieces, section_place // tile_side, axis=0).astype(jnp.float32)
    products = jnp.einsum('tji,tjf->tif', section_tiles.astype(jnp.float32), gathered, precision=lax.Precision.HIGHEST)
    live_slots = jnp.arange(section_tiles.shape[0], dtype=jnp.int32) < section_count
    placing = ((section_place % tile_side)[None, :] == jnp.arange(tile_side, dtype=jnp.int32)[:, None]) & live_slots[None, :]
    summed = jnp.einsum('rt,tif->rif', placing.astype(jnp.float32), products, precision=lax.Precision.HIGHEST)
    return summed.reshape(tile_side * tile_edge, feat_width)

def pair_data(tile_values, tile_place, tile_count, block_index):
    section_tiles = tile_values[block_index].reshape(BLOCKS, TMAX, TILE, TILE)
    section_place = tile_place[block_index].reshape(BLOCKS, TMAX)
    section_count = tile_count[block_index].reshape(BLOCKS)
    sources = jnp.mod(block_index - jnp.arange(BLOCKS, dtype=jnp.int32), BLOCKS).astype(jnp.int32)
    return (section_tiles, section_place, section_count, sources)

def aggregate(rows_all, tile_values, tile_place, tile_count):

    def per_block(block_index):
        section_tiles, section_place, section_count, sources = pair_data(tile_values, tile_place, tile_count, block_index)
        blocks_in = rows_all[sources]
        parts_all = jax.vmap(forward_section, in_axes=(0, 0, 0, 0, None))(section_tiles, section_place, section_count, blocks_in, TILES_SIDE)
        return lax.optimization_barrier(jnp.sum(parts_all, axis=0))
    return lax.map(per_block, jnp.arange(BLOCKS, dtype=jnp.int32))

def aggregate_back(rows_all, tile_values, tile_place, tile_count):

    def per_block(carried, block_index):
        section_tiles, section_place, section_count, sources = pair_data(tile_values, tile_place, tile_count, block_index)
        parts_all = jax.vmap(backward_section, in_axes=(0, 0, 0, None, None))(section_tiles, section_place, section_count, rows_all[block_index], TILES_SIDE)
        return (carried.at[sources].add(parts_all), None)
    start_zero = jnp.zeros((BLOCKS, BROWS, rows_all.shape[-1]), jnp.float32)
    result, unused = lax.scan(per_block, start_zero, jnp.arange(BLOCKS, dtype=jnp.int32))
    return result

def reference(features, node_ids, labels, train_mask, tile_values, tile_place, tile_count, weight_in, weight_out, class_bias):
    z_input = aggregate(features, tile_values, tile_place, tile_count).astype(jnp.bfloat16)
    pre_act = jnp.einsum('bnf,fh->bnh', z_input.astype(jnp.float32), weight_in.astype(jnp.float32), precision=lax.Precision.HIGHEST)
    kept = keep_factor(node_ids.reshape(-1), UNITS).reshape(BLOCKS, BROWS, UNITS)
    dropped = (jnp.maximum(pre_act, 0.0) * kept).astype(jnp.bfloat16)
    z_output = aggregate(dropped, tile_values, tile_place, tile_count).astype(jnp.bfloat16)
    logits = jnp.einsum('bnh,hc->bnc', z_output.astype(jnp.float32), weight_out.astype(jnp.float32), precision=lax.Precision.HIGHEST) + class_bias
    likelihood = jax.nn.softmax(logits, axis=-1)
    onehot = (labels[..., None] == jnp.arange(CLASSES, dtype=jnp.int32)).astype(jnp.float32)
    scale = 1.0 / math.sqrt(NODES)
    slope = ((likelihood - onehot) * train_mask[..., None].astype(jnp.float32) * scale).astype(jnp.bfloat16)
    grad_out = jnp.einsum('bnh,bnc->hc', z_output.astype(jnp.float32), slope.astype(jnp.float32), precision=lax.Precision.HIGHEST)
    grad_rows = jnp.einsum('bnc,hc->bnh', slope.astype(jnp.float32), weight_out.astype(jnp.float32), precision=lax.Precision.HIGHEST).astype(jnp.bfloat16)
    back_rows = aggregate_back(grad_rows, tile_values, tile_place, tile_count)
    pre_slope = (back_rows * kept * (pre_act > 0)).astype(jnp.bfloat16)
    grad_in = jnp.einsum('bnf,bnh->fh', z_input.astype(jnp.float32), pre_slope.astype(jnp.float32), precision=lax.Precision.HIGHEST)
    return (logits, grad_in, grad_out)
```

```python
import functools
import math

import jax
import jax.numpy as jnp
from jax import lax
from jax.experimental import pallas as pl
from jax.experimental.pallas import tpu as pltpu
from jax.sharding import PartitionSpec as P


def keep_mask(id_values, unit_count):
    columns = jnp.arange(unit_count, dtype=jnp.int32)
    mixed = id_values[:, None] * 73244475 + columns[None, :] * 19349663 + 12345
    mixed = mixed ^ jnp.right_shift(mixed, 15)
    mixed = mixed * 40503
    mixed = mixed ^ jnp.right_shift(mixed, 13)
    return jnp.bitwise_and(mixed, 3) != 0


def dense_kernel(per_rep, tile_side, rep_ref, count_ref, place_ref, tiles_ref, dense_ref):
    section = pl.program_id(0)
    edge = tiles_ref.shape[-1]
    dense_ref[...] = jnp.zeros_like(dense_ref)
    rep_index = rep_ref[0]

    def put(slot, carried):
        place = place_ref[section, slot]
        row = place // tile_side
        column = place % tile_side
        row = ((row // per_rep) ^ rep_index) * per_rep + row % per_rep
        column = ((column // per_rep) ^ rep_index) * per_rep + column % per_rep
        dense_ref[
            pl.ds(pl.multiple_of(row * edge, edge), edge),
            pl.ds(pl.multiple_of(column * edge, edge), edge),
        ] = tiles_ref[0, slot]
        return carried

    lax.fori_loop(0, count_ref[section], put, 0)


def build_dense(tiles, place, count, rep_index, own_rows, group_rows):
    sections, slots, edge, _ = tiles.shape
    body = functools.partial(dense_kernel, own_rows // edge, group_rows // edge)
    smem = pl.BlockSpec(memory_space=pltpu.SMEM)
    return pl.pallas_call(
        body,
        grid=(sections,),
        in_specs=[
            smem,
            smem,
            smem,
            pl.BlockSpec((1, slots, edge, edge), lambda s: (s, 0, 0, 0)),
        ],
        out_specs=pl.BlockSpec((group_rows, group_rows), lambda s: (0, s)),
        out_shape=jax.ShapeDtypeStruct((group_rows, sections * group_rows), tiles.dtype),
        compiler_params=pltpu.CompilerParams(vmem_limit_bytes=40 * 1024 * 1024),
        cost_estimate=pl.CostEstimate(
            flops=0, bytes_accessed=2 * sections * group_rows * group_rows, transcendentals=0
        ),
        name="dense_tiles",
    )(rep_index.reshape(1), count, place, tiles)


def on_device(
    features,
    node_ids,
    labels,
    train_mask,
    tile_values,
    tile_place,
    tile_count,
    weight_in,
    weight_out,
    class_bias,
):
    own_rows = features.shape[1]
    reps = lax.axis_size("rep")
    blks = lax.axis_size("blk")
    rep_index = lax.axis_index("rep")
    sections = tile_values.shape[2]
    group_rows = own_rows * reps
    hidden_width = weight_in.shape[1]
    scale = 1.0 / math.sqrt(group_rows * blks)
    f32 = jnp.float32
    bf16 = jnp.bfloat16

    def swap(value, delta):
        if delta == 0:
            return value
        return lax.ppermute(value, "rep", [(r, r ^ delta) for r in range(reps)])

    def to_columns(value):
        pieces = []
        for section in range(sections):
            for delta in range(reps):
                pairs = []
                for r in range(reps):
                    for c in range(blks):
                        target = r ^ delta
                        row_block = (c + sections * target + section) % blks
                        pairs.append((r * blks + c, target * blks + row_block))
                pieces.append(lax.ppermute(value, ("rep", "blk"), pairs))
        return jnp.concatenate(pieces, axis=0)

    def shift(value, steps):
        return lax.ppermute(value, "blk", [(c, (c + steps) % blks) for c in range(blks)])

    def scatter_rows(partial):
        chunks = partial.reshape(reps, own_rows, partial.shape[1])
        total = chunks[0]
        for delta in range(1, reps):
            total = total + swap(chunks[delta], delta)
        return total

    def sum_everywhere(value):
        rows, width = value.shape
        chunk = rows // reps
        mine = lax.dynamic_slice_in_dim(value, rep_index * chunk, chunk, 0)
        total = mine
        for delta in range(1, reps):
            other = lax.dynamic_slice_in_dim(value, (rep_index ^ delta) * chunk, chunk, 0)
            total = total + swap(other, delta)
        part = total
        for steps in range(1, blks):
            total = total + shift(part, steps)
        whole = jnp.zeros((rows, width), value.dtype)
        for delta in range(reps):
            whole = lax.dynamic_update_slice_in_dim(
                whole, swap(total, delta), (rep_index ^ delta) * chunk, 0
            )
        return whole

    dense = build_dense(
        tile_values[0, 0], tile_place[0, 0], tile_count[0, 0], rep_index, own_rows, group_rows
    )
    feature_columns = to_columns(features[0])
    id_columns = to_columns(node_ids[0])
    first = jnp.dot(dense, feature_columns, preferred_element_type=f32)
    z_input = scatter_rows(first).astype(bf16)
    kept = jnp.where(keep_mask(id_columns, hidden_width), f32(4.0 / 3.0), f32(0.0))
    z_columns = to_columns(z_input)
    pre_act = jnp.dot(z_columns, weight_in, preferred_element_type=f32)
    dropped = (jnp.maximum(pre_act, 0.0) * kept).astype(bf16)
    factor = kept * (pre_act > 0)
    second = jnp.dot(dense, dropped, preferred_element_type=f32)
    z_output = scatter_rows(second).astype(bf16)
    logits = jnp.dot(z_output, weight_out, preferred_element_type=f32) + class_bias
    likelihood = jax.nn.softmax(logits, axis=-1)
    onehot = labels[0][:, None] == jnp.arange(logits.shape[-1], dtype=jnp.int32)[None, :]
    slope = (
        (likelihood - onehot.astype(f32)) * train_mask[0][:, None].astype(f32) * scale
    ).astype(bf16)
    grad_rows = jnp.einsum(
        "nc,hc->nh", slope, weight_out, preferred_element_type=f32
    ).astype(bf16)
    grad_block = jnp.concatenate([swap(grad_rows, delta) for delta in range(reps)], axis=0)
    out_terms = jnp.einsum("nh,nc->hc", z_output, slope, preferred_element_type=f32)
    grad_out = sum_everywhere(out_terms)
    back = jnp.einsum("nc,nh->ch", dense, grad_block, preferred_element_type=f32)
    pre_slope = (back * factor).astype(bf16)
    in_terms = jnp.einsum("nf,nh->fh", z_columns, pre_slope, preferred_element_type=f32)
    grad_in = sum_everywhere(in_terms)
    return (logits[None], grad_in, grad_out)


def solution(mesh):
    placed = (
        P("blk", "rep", None),
        P("blk", "rep"),
        P("blk", "rep"),
        P("blk", "rep"),
        P("blk", "rep", None, None, None, None),
        P("blk", "rep", None, None),
        P("blk", "rep", None),
        P(),
        P(),
        P(),
    )
    return jax.shard_map(
        on_device,
        mesh=mesh,
        in_specs=placed,
        out_specs=(P("blk", "rep", None), P(), P()),
        check_vma=False,
    )
```

```python
import functools
import math

import jax
import jax.numpy as jnp
from jax import lax
from jax.experimental import pallas as pl
from jax.experimental.pallas import tpu as pltpu
from jax.sharding import PartitionSpec as P


def keep_mask(id_values, unit_count):
    columns = jnp.arange(unit_count, dtype=jnp.int32)
    mixed = id_values[:, None] * 73244475 + columns[None, :] * 19349663 + 12345
    mixed = mixed ^ jnp.right_shift(mixed, 15)
    mixed = mixed * 40503
    mixed = mixed ^ jnp.right_shift(mixed, 13)
    return jnp.bitwise_and(mixed, 3) != 0


def dense_kernel(tile_side, count_ref, place_ref, tiles_ref, dense_ref):
    section = pl.program_id(0)
    edge = tiles_ref.shape[-1]
    dense_ref[...] = jnp.zeros_like(dense_ref)

    def put(slot, carried):
        place = place_ref[section, slot]
        row = place // tile_side
        column = place % tile_side
        dense_ref[
            pl.ds(pl.multiple_of(row * edge, edge), edge),
            pl.ds(pl.multiple_of(column * edge, edge), edge),
        ] = tiles_ref[0, slot]
        return carried

    lax.fori_loop(0, count_ref[section], put, 0)


def build_dense(tiles, place, count, group_rows):
    sections, slots, edge, _ = tiles.shape
    body = functools.partial(dense_kernel, group_rows // edge)
    smem = pl.BlockSpec(memory_space=pltpu.SMEM)
    return pl.pallas_call(
        body,
        grid=(sections,),
        in_specs=[
            smem,
            smem,
            pl.BlockSpec((1, slots, edge, edge), lambda s: (s, 0, 0, 0)),
        ],
        out_specs=pl.BlockSpec((group_rows, group_rows), lambda s: (0, s)),
        out_shape=jax.ShapeDtypeStruct((group_rows, sections * group_rows), tiles.dtype),
        compiler_params=pltpu.CompilerParams(vmem_limit_bytes=40 * 1024 * 1024),
        cost_estimate=pl.CostEstimate(
            flops=0, bytes_accessed=2 * sections * group_rows * group_rows, transcendentals=0
        ),
        name="dense_tiles",
    )(count, place, tiles)


def on_device(
    features,
    node_ids,
    labels,
    train_mask,
    tile_values,
    tile_place,
    tile_count,
    weight_in,
    weight_out,
    class_bias,
):
    own_rows = features.shape[1]
    reps = lax.axis_size("rep")
    blks = lax.axis_size("blk")
    rep_index = lax.axis_index("rep")
    blk_index = lax.axis_index("blk")
    sections = tile_values.shape[2]
    group_rows = own_rows * reps
    hidden_width = weight_in.shape[1]
    scale = 1.0 / math.sqrt(group_rows * blks)
    f32 = jnp.float32
    bf16 = jnp.bfloat16

    everywhere = ("blk", "rep")

    def pick(blocks):
        return jnp.concatenate(
            [blocks[(blk_index - sections * rep_index - j) % blks] for j in range(sections)], axis=0
        )

    def swap_chunks(chunks):
        return lax.all_to_all(chunks, "rep", split_axis=0, concat_axis=0, tiled=True)

    def scatter_rows(partial):
        return jnp.sum(swap_chunks(partial.reshape(reps, own_rows, partial.shape[1])), axis=0)

    def to_columns(value):
        held = lax.all_gather(value, "blk", axis=0)
        wanted = [
            held[(blk_index - sections * r - j) % blks] for r in range(reps) for j in range(sections)
        ]
        wanted = jnp.stack(wanted).reshape(reps, sections, own_rows, value.shape[1])
        got = swap_chunks(wanted)
        return jnp.swapaxes(got, 0, 1).reshape(sections * group_rows, value.shape[1])

    def sum_everywhere(value):
        devices = reps * blks
        tall = value if value.shape[0] % devices == 0 else value.reshape(devices, -1)
        chunks = tall.reshape(devices, tall.shape[0] // devices, tall.shape[1])
        chunks = lax.all_to_all(chunks, everywhere, split_axis=0, concat_axis=0, tiled=True)
        whole = lax.all_gather(jnp.sum(chunks, axis=0), everywhere, axis=0, tiled=True)
        return whole.reshape(value.shape)

    dense = build_dense(tile_values[0, 0], tile_place[0, 0], tile_count[0, 0], group_rows)
    feature_columns = pick(
        lax.all_gather(features[0], everywhere, axis=0).reshape(blks, group_rows, features.shape[2])
    )
    id_columns = pick(lax.all_gather(node_ids[0], everywhere, axis=0).reshape(blks, group_rows))
    first = jnp.dot(dense, feature_columns, preferred_element_type=f32)
    z_input = scatter_rows(first).astype(bf16)
    kept = jnp.where(keep_mask(id_columns, hidden_width), f32(4.0 / 3.0), f32(0.0))
    z_columns = to_columns(z_input)
    pre_act = jnp.dot(z_columns, weight_in, preferred_element_type=f32)
    dropped = (jnp.maximum(pre_act, 0.0) * kept).astype(bf16)
    factor = kept * (pre_act > 0)
    second = jnp.dot(dense, dropped, preferred_element_type=f32)
    z_output = scatter_rows(second).astype(bf16)
    logits = jnp.dot(z_output, weight_out, preferred_element_type=f32) + class_bias
    likelihood = jax.nn.softmax(logits, axis=-1)
    onehot = labels[0][:, None] == jnp.arange(logits.shape[-1], dtype=jnp.int32)[None, :]
    slope = (
        (likelihood - onehot.astype(f32)) * train_mask[0][:, None].astype(f32) * scale
    ).astype(bf16)
    grad_rows = jnp.einsum(
        "nc,hc->nh", slope, weight_out, preferred_element_type=f32
    ).astype(bf16)
    grad_block = swap_chunks(jnp.broadcast_to(grad_rows[None], (reps,) + grad_rows.shape))
    grad_block = grad_block.reshape(group_rows, hidden_width)
    out_terms = jnp.einsum("nh,nc->hc", z_output, slope, preferred_element_type=f32)
    grad_out = sum_everywhere(out_terms)
    back = jnp.einsum("nc,nh->ch", dense, grad_block, preferred_element_type=f32)
    pre_slope = (back * factor).astype(bf16)
    in_terms = jnp.einsum("nf,nh->fh", z_columns, pre_slope, preferred_element_type=f32)
    grad_in = sum_everywhere(in_terms)
    return (logits[None], grad_in, grad_out)


def solution(mesh):
    placed = (
        P("blk", "rep", None),
        P("blk", "rep"),
        P("blk", "rep"),
        P("blk", "rep"),
        P("blk", "rep", None, None, None, None),
        P("blk", "rep", None, None),
        P("blk", "rep", None),
        P(),
        P(),
        P(),
    )
    return jax.shard_map(
        on_device,
        mesh=mesh,
        in_specs=placed,
        out_specs=(P("blk", "rep", None), P(), P()),
        check_vma=False,
    )
```

```python
import functools
import math

import jax
import jax.numpy as jnp
from jax import lax
from jax.experimental import pallas as pl
from jax.experimental.pallas import tpu as pltpu
from jax.sharding import PartitionSpec as P


def keep_mask(id_values, unit_count):
    columns = jnp.arange(unit_count, dtype=jnp.int32)
    mixed = id_values[:, None] * 73244475 + columns[None, :] * 19349663 + 12345
    mixed = mixed ^ jnp.right_shift(mixed, 15)
    mixed = mixed * 40503
    mixed = mixed ^ jnp.right_shift(mixed, 13)
    return jnp.bitwise_and(mixed, 3) != 0


def dense_kernel(
    per_rep, tile_side, spot_ref, order_ref, moved_ref, place_ref, own_ref, other_ref, dense_ref
):
    position = pl.program_id(0)
    rep_index = spot_ref[0]
    edge = own_ref.shape[-1]
    slots = own_ref.shape[1]
    dense_ref[...] = jnp.zeros_like(dense_ref)

    def put_all(tiles_ref):
        def put(slot, carried):
            place = place_ref[position, slot]
            row = place // tile_side
            column = place % tile_side
            row = ((row // per_rep) ^ rep_index) * per_rep + row % per_rep
            column = ((column // per_rep) ^ rep_index) * per_rep + column % per_rep

            @pl.when(place >= 0)
            def _():
                dense_ref[
                    pl.ds(pl.multiple_of(row * edge, edge), edge),
                    pl.ds(pl.multiple_of(column * edge, edge), edge),
                ] = tiles_ref[0, slot]

            return carried

        lax.fori_loop(0, slots, put, 0)

    @pl.when(moved_ref[position] == 0)
    def _():
        put_all(own_ref)

    @pl.when(moved_ref[position] != 0)
    def _():
        put_all(other_ref)


def build_dense(tiles, others, place, spot, order, moved, own_rows, group_rows):
    sections, slots, edge, _ = tiles.shape
    body = functools.partial(dense_kernel, own_rows // edge, group_rows // edge)
    tile_block = (1, slots, edge, edge)
    return pl.pallas_call(
        body,
        grid_spec=pltpu.PrefetchScalarGridSpec(
            num_scalar_prefetch=4,
            grid=(sections,),
            in_specs=[
                pl.BlockSpec(tile_block, lambda p, spot, order, *_: (order[p], 0, 0, 0)),
                pl.BlockSpec(
                    tile_block, lambda p, spot, order, *_: (jnp.maximum(order[p] - 1, 0), 0, 0, 0)
                ),
            ],
            out_specs=pl.BlockSpec((group_rows, group_rows), lambda p, *_: (0, p)),
        ),
        out_shape=jax.ShapeDtypeStruct((group_rows, sections * group_rows), tiles.dtype),
        compiler_params=pltpu.CompilerParams(vmem_limit_bytes=40 * 1024 * 1024),
        cost_estimate=pl.CostEstimate(
            flops=0, bytes_accessed=2 * sections * group_rows * group_rows, transcendentals=0
        ),
        name="dense_tiles",
    )(spot, order, moved, place, tiles, others)


def on_device(
    features,
    node_ids,
    labels,
    train_mask,
    tile_values,
    tile_place,
    tile_count,
    weight_in,
    weight_out,
    class_bias,
):
    own_rows = features.shape[1]
    reps = lax.axis_size("rep")
    blks = lax.axis_size("blk")
    rep_index = lax.axis_index("rep")
    blk_index = lax.axis_index("blk")
    sections = tile_values.shape[2]
    group_rows = own_rows * reps
    hidden_width = weight_in.shape[1]
    scale = 1.0 / math.sqrt(group_rows * blks)
    f32 = jnp.float32
    bf16 = jnp.bfloat16

    def swap(value, delta):
        if delta == 0:
            return value
        return lax.ppermute(value, "rep", [(r, r ^ delta) for r in range(reps)])

    def exchange(value, delta):
        return lax.ppermute(value, "blk", [(c, c ^ delta) for c in range(blks)])

    def to_columns(value):
        pieces = []
        for delta in range(reps):
            pairs = []
            for r in range(reps):
                for c in range(blks):
                    target = r ^ delta
                    pairs.append((r * blks + c, target * blks + (c + sections * target) % blks))
            pieces.append(lax.ppermute(value, ("rep", "blk"), pairs))
        block = jnp.concatenate(pieces, axis=0)
        return [block] + [exchange(block, delta) for delta in range(1, sections)]

    def scatter_rows(partial):
        chunks = partial.reshape(reps, own_rows, partial.shape[1])
        total = chunks[0]
        for delta in range(1, reps):
            total = total + swap(chunks[delta], delta)
        return total

    def sum_everywhere(value):
        half = value.shape[0] // 2
        side = lax.rem(blk_index, 2)
        theirs = exchange(lax.dynamic_slice_in_dim(value, (1 - side) * half, half, 0), 1)
        total = lax.dynamic_slice_in_dim(value, side * half, half, 0) + theirs
        steps = [(exchange, 1 << bit) for bit in range(1, (blks - 1).bit_length())]
        steps += [(swap, 1 << bit) for bit in range((reps - 1).bit_length())]
        for move, delta in steps:
            rounded = total.astype(bf16)
            total = rounded.astype(f32) + move(rounded, delta).astype(f32)
        other = exchange(total, 1)
        lower = jnp.where(side == 0, total, other)
        upper = jnp.where(side == 0, other, total)
        return jnp.concatenate([lower, upper], axis=0)

    def digits(ids):
        lanes = features.shape[2]
        parts = [ids & 255, (ids >> 8) & 255, ids >> 16]
        rows = jnp.concatenate([part.reshape(-1, lanes) for part in parts], axis=0)
        return jnp.pad(rows, ((0, -rows.shape[0] % 16), (0, 0))).astype(bf16)

    def undo_digits(rows):
        count = own_rows // rows.shape[1]
        parts = [rows[i * count : (i + 1) * count].astype(jnp.int32) for i in range(3)]
        return (parts[0] + (parts[1] << 8) + (parts[2] << 16)).reshape(own_rows)

    member = lax.rem(blk_index, sections)
    live = jnp.arange(tile_values.shape[3], dtype=jnp.int32)[None, :] < tile_count[0, 0][:, None]
    place = jnp.where(live, tile_place[0, 0], -1)
    other_tiles = []
    other_place = [place[0]]
    for j in range(1, sections):
        pairs = []
        for r in range(reps):
            for c in range(blks):
                if c % sections < j:
                    pairs.append((r * blks + c, (r + 1) % reps * blks + c))
        other_tiles.append(lax.ppermute(tile_values[0, 0, j], ("rep", "blk"), pairs))
        other_place.append(lax.ppermute(place[j], ("rep", "blk"), pairs))
    position = jnp.arange(sections, dtype=jnp.int32)
    column = position ^ member
    order = jnp.mod(member - column, sections)
    moved = (column > member).astype(jnp.int32)
    placed = jnp.where(moved[:, None] != 0, jnp.stack(other_place)[order], place[order])
    dense = build_dense(
        tile_values[0, 0],
        jnp.stack(other_tiles),
        placed,
        rep_index.reshape(1),
        order,
        moved,
        own_rows,
        group_rows,
    )
    bundle = jnp.concatenate([features[0], digits(node_ids[0])], axis=0)
    bundles = jnp.concatenate(to_columns(bundle), axis=0).reshape(sections * reps, -1, features.shape[2])
    feature_columns = bundles[:, :own_rows].reshape(sections * group_rows, features.shape[2])
    id_columns = jnp.concatenate(
        [undo_digits(bundles[i, own_rows:]) for i in range(sections * reps)]
    )
    first = jnp.dot(dense, feature_columns, preferred_element_type=f32)
    z_input = scatter_rows(first).astype(bf16)
    kept = jnp.where(keep_mask(id_columns, hidden_width), f32(4.0 / 3.0), f32(0.0))
    z_columns = jnp.concatenate(to_columns(z_input), axis=0)
    pre_act = jnp.dot(z_columns, weight_in, preferred_element_type=f32)
    dropped = (jnp.maximum(pre_act, 0.0) * kept).astype(bf16)
    factor = kept * (pre_act > 0)
    second = jnp.dot(dense, dropped, preferred_element_type=f32)
    z_output = scatter_rows(second).astype(bf16)
    logits = jnp.dot(z_output, weight_out, preferred_element_type=f32) + class_bias
    likelihood = jax.nn.softmax(logits, axis=-1)
    onehot = labels[0][:, None] == jnp.arange(logits.shape[-1], dtype=jnp.int32)[None, :]
    slope = (
        (likelihood - onehot.astype(f32)) * train_mask[0][:, None].astype(f32) * scale
    ).astype(bf16)
    grad_rows = jnp.einsum(
        "nc,hc->nh", slope, weight_out, preferred_element_type=f32
    ).astype(bf16)
    grad_block = jnp.concatenate([swap(grad_rows, delta) for delta in range(reps)], axis=0)
    out_terms = jnp.einsum("nh,nc->hc", z_output, slope, preferred_element_type=f32)
    grad_out = sum_everywhere(out_terms)
    back = jnp.einsum("nc,nh->ch", dense, grad_block, preferred_element_type=f32)
    pre_slope = (back * factor).astype(bf16)
    in_terms = jnp.einsum("nf,nh->fh", z_columns, pre_slope, preferred_element_type=f32)
    grad_in = sum_everywhere(in_terms)
    return (logits[None], grad_in, grad_out)


def solution(mesh):
    placed = (
        P("blk", "rep", None),
        P("blk", "rep"),
        P("blk", "rep"),
        P("blk", "rep"),
        P("blk", "rep", None, None, None, None),
        P("blk", "rep", None, None),
        P("blk", "rep", None),
        P(),
        P(),
        P(),
    )
    return jax.shard_map(
        on_device,
        mesh=mesh,
        in_specs=placed,
        out_specs=(P("blk", "rep", None), P(), P()),
        check_vma=False,
    )
```

```python
import functools
import math

import jax
import jax.numpy as jnp
from jax import lax
from jax.experimental import pallas as pl
from jax.experimental.pallas import tpu as pltpu
from jax.sharding import PartitionSpec as P


CODE_BITS = 14
HEAD_ROWS = 16


def keep_mask(id_values, unit_values):
    mixed = id_values * 73244475 + unit_values * 19349663 + 12345
    mixed = mixed ^ jnp.right_shift(mixed, 15)
    mixed = mixed * 40503
    mixed = mixed ^ jnp.right_shift(mixed, 13)
    return (jnp.bitwise_and(mixed, 3) != 0).astype(jnp.bfloat16)


def eye_of(count):
    rows = lax.broadcasted_iota(jnp.int32, (count, count), 0)
    columns = lax.broadcasted_iota(jnp.int32, (count, count), 1)
    return rows == columns


def dot(left, right):
    return jnp.dot(left, right, preferred_element_type=jnp.float32)


def dot_wide(left, right):
    return lax.dot_general(
        left, right, (((1,), (1,)), ((), ())), preferred_element_type=jnp.float32
    )


def encode(values):
    rows, width = values.shape
    largest = jnp.max(jnp.abs(values), axis=1, keepdims=True)
    power = jnp.ceil(jnp.log2(jnp.maximum(largest, 1e-30)))
    coded = jnp.round(values * jnp.exp2(CODE_BITS - power))
    square = eye_of(width)
    index = lax.broadcasted_iota(jnp.int32, (HEAD_ROWS, width), 0)
    head = jnp.zeros((HEAD_ROWS, width), jnp.float32)
    for part in range(rows // width):
        column = power[part * width : (part + 1) * width]
        line = jnp.sum(jnp.where(square, column, 0.0), axis=0, keepdims=True)
        head = jnp.where(index == part, line, head)
    whole = jnp.concatenate([coded, head], axis=0)
    return whole.astype(jnp.int32).astype(jnp.int16)


def decode(coded):
    whole = coded.astype(jnp.int32).astype(jnp.float32)
    rows, width = whole.shape[0] - HEAD_ROWS, whole.shape[1]
    square = eye_of(width)
    columns = []
    for part in range(rows // width):
        line = whole[rows + part : rows + part + 1]
        columns.append(jnp.sum(jnp.where(square, line, 0.0), axis=1, keepdims=True))
    power = jnp.concatenate(columns, axis=0)
    return whole[:rows] * jnp.exp2(power - CODE_BITS)


def share_out(values, own_ref, coded_refs):
    step = pl.program_id(0)

    @pl.when(step == 0)
    def _():
        own_ref[...] = values

    @pl.when(step != 0)
    def _():
        coded = encode(values)
        for delta, coded_ref in enumerate(coded_refs, 1):

            @pl.when(step == delta)
            def _():
                coded_ref[...] = coded


def first_kernel(sections, reps, dense_ref, *refs):
    block_refs, own_ref, coded_refs = refs[:sections], refs[sections], refs[sections + 1 :]
    own_rows = own_ref.shape[0]
    total = jnp.zeros(own_ref.shape, jnp.float32)
    stride = block_refs[0].shape[0] // reps
    for p in range(sections):
        for d in range(reps):
            start = (p * reps + d) * own_rows
            total += dot(
                dense_ref[:, start : start + own_rows],
                block_refs[p][d * stride : d * stride + own_rows, :],
            )
    share_out(total, own_ref, coded_refs)


def second_kernel(sections, dense_ref, weight_ref, kept_ref, *refs):
    block_refs, own_ref = refs[:sections], refs[sections]
    coded_refs, dropped_ref = refs[sections + 1 : -1], refs[-1]
    size = block_refs[0].shape[0]

    @pl.when(pl.program_id(0) == 0)
    def _():
        for p in range(sections):
            rows = pl.ds(p * size, size)
            pre_act = dot(block_refs[p][...], weight_ref[...])
            kept = kept_ref[rows, :].astype(jnp.float32) * jnp.float32(4.0 / 3.0)
            dropped_ref[rows, :] = (jnp.maximum(pre_act, 0.0) * kept).astype(jnp.bfloat16)

    share_out(dot(dense_ref[...], dropped_ref[...]), own_ref, coded_refs)


def partial_product(body, dense, fixed, blocks, reps, width, scratch, name):
    own_rows, columns = dense.shape[0] // reps, dense.shape[1]
    whole = [pl.BlockSpec(value.shape, lambda i: (0, 0)) for value in fixed + blocks]
    kept_here = jax.ShapeDtypeStruct((own_rows, width), jnp.float32)
    sent = jax.ShapeDtypeStruct((own_rows + HEAD_ROWS, width), jnp.int16)
    shapes = [kept_here] + [sent] * (reps - 1)
    return pl.pallas_call(
        body,
        grid=(reps,),
        in_specs=[pl.BlockSpec((own_rows, columns), lambda i: (i, 0))] + whole,
        out_specs=[pl.BlockSpec(shape.shape, lambda i: (0, 0)) for shape in shapes],
        out_shape=shapes,
        scratch_shapes=scratch,
        compiler_params=pltpu.CompilerParams(vmem_limit_bytes=48 * 1024 * 1024),
        name=name,
    )(dense, *fixed, *blocks)


def sum_kernel(own_ref, *refs):
    coded_refs, out_ref = refs[:-1], refs[-1]
    total = own_ref[...]
    for coded_ref in coded_refs:
        total += decode(coded_ref[...])
    out_ref[...] = total.astype(out_ref.dtype)


def head_kernel(scale, weight_ref, bias_ref, label_ref, mask_ref, own_ref, *refs):
    coded_refs, (logits_ref, grad_rows_ref, out_terms_ref) = refs[:-3], refs[-3:]
    total = own_ref[...]
    for coded_ref in coded_refs:
        total += decode(coded_ref[...])
    z_output = total.astype(jnp.bfloat16)
    logits = dot(z_output, weight_ref[...]) + bias_ref[...]
    logits_ref[...] = logits
    shifted = jnp.exp(logits - jnp.max(logits, axis=1, keepdims=True))
    likelihood = shifted / jnp.sum(shifted, axis=1, keepdims=True)
    onehot = label_ref[...] == lax.broadcasted_iota(jnp.int32, logits.shape, 1)
    slope = (likelihood - onehot.astype(jnp.float32)) * mask_ref[...].astype(jnp.float32) * scale
    slope = slope.astype(jnp.bfloat16)
    grad_rows_ref[...] = dot_wide(weight_ref[...], slope).astype(jnp.bfloat16)
    classes = logits.shape[1]
    terms = lax.dot_general(
        slope, z_output, (((0,), (0,)), ((), ())), preferred_element_type=jnp.float32
    )
    out_terms_ref[:classes, :] = terms
    pad = out_terms_ref.shape[0] - classes
    if pad:
        out_terms_ref[classes:, :] = jnp.zeros((pad, terms.shape[1]), jnp.float32)


def back_kernel(reps, dense_ref, block_ref, kept_ref, weight_ref, *refs):
    grad_refs, out_ref, total_ref = refs[:reps], refs[reps], refs[reps + 1]
    own_rows = grad_refs[0].shape[1]
    back = jnp.zeros(kept_ref.shape, jnp.float32)
    for d in range(reps):
        back += dot(grad_refs[d][...], dense_ref[d * own_rows : (d + 1) * own_rows, :])
    pre_act = dot_wide(weight_ref[...], block_ref[...])
    factor = jnp.where(pre_act > 0, kept_ref[...].astype(jnp.float32), 0.0)
    pre_slope = (back * (factor * jnp.float32(4.0 / 3.0))).astype(jnp.bfloat16)
    terms = dot(pre_slope, block_ref[...])

    @pl.when(pl.program_id(0) == 0)
    def _():
        total_ref[...] = terms

    @pl.when(pl.program_id(0) != 0)
    def _():
        total_ref[...] += terms

    @pl.when(pl.program_id(0) == pl.num_programs(0) - 1)
    def _():
        out_ref[...] = total_ref[...].T


def backward(dense, z_columns, kept_wide, weight_wide, grad_parts, reps):
    step = dense.shape[0] // 2
    hidden, inputs = weight_wide.shape
    whole = [pl.BlockSpec(value.shape, lambda i: (0, 0)) for value in [weight_wide] + grad_parts]
    return pl.pallas_call(
        functools.partial(back_kernel, reps),
        grid=(dense.shape[1] // step,),
        in_specs=[
            pl.BlockSpec((dense.shape[0], step), lambda i: (0, i)),
            pl.BlockSpec((step, inputs), lambda i: (i, 0)),
            pl.BlockSpec((hidden, step), lambda i: (0, i)),
        ]
        + whole,
        out_specs=pl.BlockSpec((inputs, hidden), lambda i: (0, 0)),
        out_shape=jax.ShapeDtypeStruct((inputs, hidden), jnp.float32),
        scratch_shapes=[pltpu.VMEM((hidden, inputs), jnp.float32)],
        compiler_params=pltpu.CompilerParams(vmem_limit_bytes=48 * 1024 * 1024),
        name="backward",
    )(dense, z_columns, kept_wide, weight_wide, *grad_parts)


def simple_call(body, shapes, name, *values):
    return pl.pallas_call(
        body,
        out_shape=shapes,
        compiler_params=pltpu.CompilerParams(vmem_limit_bytes=32 * 1024 * 1024),
        name=name,
    )(*values)


def dense_kernel(
    per_rep, tile_side, spot_ref, order_ref, moved_ref, place_ref, own_ref, other_ref, dense_ref
):
    position = pl.program_id(0)
    rep_index = spot_ref[0]
    edge = own_ref.shape[-1]
    slots = place_ref.shape[1]
    dense_ref[...] = jnp.zeros_like(dense_ref)

    def put_all(tiles_ref):
        def put(slot, carried):
            place = place_ref[position, slot]
            row = place // tile_side
            column = place % tile_side
            row = ((row // per_rep) ^ rep_index) * per_rep + row % per_rep
            column = ((column // per_rep) ^ rep_index) * per_rep + column % per_rep

            @pl.when(place >= 0)
            def _():
                dense_ref[
                    pl.ds(pl.multiple_of(row * edge, edge), edge),
                    pl.ds(pl.multiple_of(column * edge, edge), edge),
                ] = tiles_ref[0, slot]

            return carried

        lax.fori_loop(0, slots, put, 0)

    @pl.when(moved_ref[position] == 0)
    def _():
        put_all(own_ref)

    @pl.when(moved_ref[position] != 0)
    def _():
        put_all(other_ref)


def build_dense(tiles, others, place, spot, order, moved, own_rows, group_rows):
    sections, slots, edge, _ = tiles.shape
    body = functools.partial(dense_kernel, own_rows // edge, group_rows // edge)
    tile_block = (1, slots, edge, edge)
    other_block = (1, slots + 1, edge, edge)
    return pl.pallas_call(
        body,
        grid_spec=pltpu.PrefetchScalarGridSpec(
            num_scalar_prefetch=4,
            grid=(sections,),
            in_specs=[
                pl.BlockSpec(tile_block, lambda p, spot, order, *_: (order[p], 0, 0, 0)),
                pl.BlockSpec(
                    other_block, lambda p, spot, order, *_: (jnp.maximum(order[p] - 1, 0), 0, 0, 0)
                ),
            ],
            out_specs=pl.BlockSpec((group_rows, group_rows), lambda p, *_: (0, p)),
        ),
        out_shape=jax.ShapeDtypeStruct((group_rows, sections * group_rows), tiles.dtype),
        compiler_params=pltpu.CompilerParams(vmem_limit_bytes=40 * 1024 * 1024),
        cost_estimate=pl.CostEstimate(
            flops=0, bytes_accessed=2 * sections * group_rows * group_rows, transcendentals=0
        ),
        name="dense_tiles",
    )(spot, order, moved, place, tiles, others)


def on_device(
    features,
    node_ids,
    labels,
    train_mask,
    tile_values,
    tile_place,
    tile_count,
    weight_in,
    weight_out,
    class_bias,
):
    own_rows = features.shape[1]
    reps = lax.axis_size("rep")
    blks = lax.axis_size("blk")
    rep_index = lax.axis_index("rep")
    blk_index = lax.axis_index("blk")
    sections = tile_values.shape[2]
    group_rows = own_rows * reps
    hidden_width = weight_in.shape[1]
    scale = 1.0 / math.sqrt(group_rows * blks)
    f32 = jnp.float32
    bf16 = jnp.bfloat16

    def swap(value, delta):
        if delta == 0:
            return value
        return lax.ppermute(value, "rep", [(r, r ^ delta) for r in range(reps)])

    def exchange(value, delta):
        return lax.ppermute(value, "blk", [(c, c ^ delta) for c in range(blks)])

    def to_columns(value):
        pieces = []
        for delta in range(reps):
            pairs = []
            for r in range(reps):
                for c in range(blks):
                    target = r ^ delta
                    pairs.append((r * blks + c, target * blks + (c + sections * target) % blks))
            pieces.append(lax.ppermute(value, ("rep", "blk"), pairs))
        block = jnp.concatenate(pieces, axis=0)
        return [block] + [exchange(block, delta) for delta in range(1, sections)]

    def halve(value):
        half = value.shape[0] // 2
        side = lax.rem(blk_index, 2)
        theirs = exchange(lax.dynamic_slice_in_dim(value, (1 - side) * half, half, 0), 1)
        total = lax.dynamic_slice_in_dim(value, side * half, half, 0) + theirs
        for bit in range(1, (blks - 1).bit_length()):
            total = add_other(total, exchange, 1 << bit)
        return total

    def add_other(total, move, delta):
        rounded = total.astype(bf16)
        return rounded.astype(f32) + move(rounded, delta).astype(f32)

    def finish(total):
        for bit in range((reps - 1).bit_length()):
            total = add_other(total, swap, 1 << bit)
        other = exchange(total, 1)
        side = lax.rem(blk_index, 2)
        return jnp.where(side == 0, total, other), jnp.where(side == 0, other, total)

    def digits(ids):
        lanes = features.shape[2]
        parts = [ids & 255, (ids >> 8) & 255, ids >> 16]
        rows = jnp.concatenate([part.reshape(-1, lanes) for part in parts], axis=0)
        return jnp.pad(rows, ((0, -rows.shape[0] % 16), (0, 0))).astype(bf16)

    def undo_digits(rows):
        count = own_rows // rows.shape[1]
        parts = [rows[i * count : (i + 1) * count].astype(jnp.int32) for i in range(3)]
        return (parts[0] + (parts[1] << 8) + (parts[2] << 16)).reshape(own_rows)

    member = lax.rem(blk_index, sections)
    live = jnp.arange(tile_values.shape[3], dtype=jnp.int32)[None, :] < tile_count[0, 0][:, None]
    place = jnp.where(live, tile_place[0, 0], -1)
    edge = tile_values.shape[-1]
    slots = tile_values.shape[3]
    other_tiles = []
    other_place = [place[0]]
    for j in range(1, sections):
        pairs = []
        for r in range(reps):
            for c in range(blks):
                if c % sections < j:
                    pairs.append((r * blks + c, (r + 1) % reps * blks + c))
        extra = jnp.pad(place[j][None] + 1, ((0, edge - 1), (0, edge - slots)))
        parcel = jnp.concatenate([tile_values[0, 0, j], extra[None].astype(bf16)], axis=0)
        parcel = lax.ppermute(parcel, ("rep", "blk"), pairs)
        other_tiles.append(parcel)
        other_place.append(parcel[slots, 0, :slots].astype(jnp.int32) - 1)
    position = jnp.arange(sections, dtype=jnp.int32)
    column = position ^ member
    order = jnp.mod(member - column, sections)
    moved = (column > member).astype(jnp.int32)
    placed = jnp.where(moved[:, None] != 0, jnp.stack(other_place)[order], place[order])
    dense = build_dense(
        tile_values[0, 0],
        jnp.stack(other_tiles),
        placed,
        rep_index.reshape(1),
        order,
        moved,
        own_rows,
        group_rows,
    )
    width = features.shape[2]
    bundle = jnp.concatenate([features[0], digits(node_ids[0])], axis=0)
    bundles = to_columns(bundle)
    stride = bundle.shape[0]
    id_columns = jnp.concatenate(
        [
            undo_digits(block[d * stride + own_rows : (d + 1) * stride])
            for block in bundles
            for d in range(reps)
        ]
    )
    units = jnp.arange(hidden_width, dtype=jnp.int32)
    kept = keep_mask(id_columns[:, None], units[None, :])
    kept_wide = keep_mask(id_columns[None, :], units[:, None])
    first = partial_product(
        functools.partial(first_kernel, sections, reps),
        dense, [], bundles, reps, width, [], "first_product",
    )
    arrived = [swap(first[d], d) for d in range(1, reps)]
    z_input = simple_call(
        sum_kernel, jax.ShapeDtypeStruct((own_rows, width), bf16), "first_sum", first[0], *arrived
    )
    z_blocks = to_columns(z_input)
    kept, z_blocks = lax.optimization_barrier((kept, z_blocks))
    second = partial_product(
        functools.partial(second_kernel, sections),
        dense, [weight_in, kept], z_blocks, reps, hidden_width,
        [pltpu.VMEM((sections * group_rows, hidden_width), bf16)], "second_product",
    )
    arrived = [swap(second[d], d) for d in range(1, reps)]
    classes = weight_out.shape[1]
    logits, grad_rows, out_terms = simple_call(
        functools.partial(head_kernel, scale),
        (
            jax.ShapeDtypeStruct((own_rows, classes), f32),
            jax.ShapeDtypeStruct((hidden_width, own_rows), bf16),
            jax.ShapeDtypeStruct((classes + -classes % 16, hidden_width), f32),
        ),
        "head",
        weight_out, class_bias[None], labels[0][:, None], train_mask[0][:, None],
        second[0], *arrived,
    )
    grad_parts = [swap(grad_rows, d) for d in range(reps)]
    out_total = halve(out_terms)
    z_columns = jnp.concatenate(z_blocks, axis=0)
    grad_parts, out_total = lax.optimization_barrier((grad_parts, out_total))
    in_terms = backward(dense, z_columns, kept_wide, weight_in.T, grad_parts, reps)
    both = jnp.concatenate([halve(in_terms), out_total], axis=0)
    lower, upper = finish(both)
    cut = in_terms.shape[0] // 2
    grad_in = jnp.concatenate([lower[:cut], upper[:cut]], axis=0)
    grad_out = jnp.concatenate([lower[cut:], upper[cut:]], axis=0)[:classes].T
    return (logits[None], grad_in, grad_out)


def solution(mesh):
    placed = (
        P("blk", "rep", None),
        P("blk", "rep"),
        P("blk", "rep"),
        P("blk", "rep"),
        P("blk", "rep", None, None, None, None),
        P("blk", "rep", None, None),
        P("blk", "rep", None),
        P(),
        P(),
        P(),
    )
    return jax.shard_map(
        on_device,
        mesh=mesh,
        in_specs=placed,
        out_specs=(P("blk", "rep", None), P(), P()),
        check_vma=False,
    )
```

```python
import functools
import math

import jax
import jax.numpy as jnp
from jax import lax
from jax.experimental import pallas as pl
from jax.experimental.pallas import tpu as pltpu
from jax.sharding import PartitionSpec as P


LEVELS = 32767.0
MANTISSA_BITS = 14
HEAD_ROWS = 16


def keep_mask(id_values, unit_values):
    mixed = id_values * 73244475 + unit_values * 19349663 + 12345
    mixed = mixed ^ jnp.right_shift(mixed, 15)
    mixed = mixed * 40503
    mixed = mixed ^ jnp.right_shift(mixed, 13)
    return (jnp.bitwise_and(mixed, 3) != 0).astype(jnp.bfloat16)


def eye_of(count):
    rows = lax.broadcasted_iota(jnp.int32, (count, count), 0)
    columns = lax.broadcasted_iota(jnp.int32, (count, count), 1)
    return rows == columns


def dot(left, right):
    return jnp.dot(left, right, preferred_element_type=jnp.float32)


def dot_wide(left, right):
    return lax.dot_general(
        left, right, (((1,), (1,)), ((), ())), preferred_element_type=jnp.float32
    )


def encode(values):
    rows, width = values.shape
    largest = jnp.maximum(jnp.max(jnp.abs(values), axis=1, keepdims=True), 1e-30)
    power = jnp.ceil(jnp.log2(largest))
    mantissa = jnp.ceil(largest * jnp.exp2(MANTISSA_BITS - power))
    scale = mantissa * jnp.exp2(power - MANTISSA_BITS)
    coded = jnp.clip(jnp.round(values * (LEVELS / scale)), -LEVELS, LEVELS)
    square = eye_of(width)
    index = lax.broadcasted_iota(jnp.int32, (HEAD_ROWS, width), 0)
    head = jnp.zeros((HEAD_ROWS, width), jnp.float32)
    for part in range(rows // width):
        for offset, column in enumerate((power, mantissa)):
            column = column[part * width : (part + 1) * width]
            line = jnp.sum(jnp.where(square, column, 0.0), axis=0, keepdims=True)
            head = jnp.where(index == 2 * part + offset, line, head)
    whole = jnp.concatenate([coded, head], axis=0)
    return whole.astype(jnp.int32).astype(jnp.int16)


def decode(coded):
    whole = coded.astype(jnp.int32).astype(jnp.float32)
    rows, width = whole.shape[0] - HEAD_ROWS, whole.shape[1]
    square = eye_of(width)
    columns = [[], []]
    for part in range(rows // width):
        for offset in range(2):
            start = rows + 2 * part + offset
            line = whole[start : start + 1]
            columns[offset].append(jnp.sum(jnp.where(square, line, 0.0), axis=1, keepdims=True))
    power, mantissa = (jnp.concatenate(parts, axis=0) for parts in columns)
    return whole[:rows] * (mantissa * jnp.exp2(power - MANTISSA_BITS) * (1.0 / LEVELS))


def encode_kernel(partial_ref, *coded_refs):
    own_rows = partial_ref.shape[0] // (len(coded_refs) + 1)
    for delta, coded_ref in enumerate(coded_refs, 1):
        coded_ref[...] = encode(partial_ref[delta * own_rows : (delta + 1) * own_rows, :])


def pack_kernel(count_ref, feature_ref, id_ref, place_ref, tiles_ref, bundle_ref, *parcel_refs):
    own_rows, lanes = feature_ref.shape
    bundle_ref[:own_rows, :] = feature_ref[...]
    ids = id_ref[...]
    rows = ids.shape[0]
    parts = [ids & 255, jnp.right_shift(ids, 8) & 255, jnp.right_shift(ids, 16)]
    pad = bundle_ref.shape[0] - own_rows - 3 * rows
    parts += [jnp.zeros((pad, lanes), jnp.int32)] if pad else []
    bundle_ref[own_rows:, :] = jnp.concatenate(parts, axis=0).astype(jnp.float32).astype(jnp.bfloat16)
    slots, edge = tiles_ref.shape[1], tiles_ref.shape[2]
    slot = lax.broadcasted_iota(jnp.int32, (1, slots), 1)
    for section, parcel_ref in enumerate(parcel_refs, 1):
        parcel_ref[:slots] = tiles_ref[section]
        place = place_ref[section : section + 1, :]
        line = jnp.where(slot < count_ref[section], place + 1, 0)
        line = jnp.concatenate([line, jnp.zeros((1, edge - slots), jnp.int32)], axis=1)
        first = lax.broadcasted_iota(jnp.int32, (edge, edge), 0) == 0
        parcel_ref[slots] = jnp.where(first, line, 0).astype(jnp.float32).astype(jnp.bfloat16)


def last_kernel(classes, side_ref, total_ref, other_ref, grad_in_ref, grad_out_ref):
    half = grad_in_ref.shape[0] // 2
    mine, theirs = total_ref[...], other_ref[...]
    lower = jnp.where(side_ref[0] == 0, mine, theirs)
    upper = jnp.where(side_ref[0] == 0, theirs, mine)
    grad_in_ref[...] = jnp.concatenate([lower[:half], upper[:half]], axis=0)
    grad_out = jnp.concatenate([lower[half:], upper[half:]], axis=0)
    grad_out_ref[...] = grad_out.T[:, :classes]


def head_kernel(scale, weight_ref, bias_ref, label_ref, mask_ref, own_ref, *refs):
    coded_refs, (logits_ref, grad_rows_ref, out_terms_ref) = refs[:-3], refs[-3:]
    total = own_ref[: logits_ref.shape[0], :]
    for coded_ref in coded_refs:
        total += decode(coded_ref[...])
    z_output = total.astype(jnp.bfloat16)
    logits = dot(z_output, weight_ref[...]) + bias_ref[...]
    logits_ref[...] = logits
    shifted = jnp.exp(logits - jnp.max(logits, axis=1, keepdims=True))
    likelihood = shifted / jnp.sum(shifted, axis=1, keepdims=True)
    onehot = label_ref[...] == lax.broadcasted_iota(jnp.int32, logits.shape, 1)
    slope = (likelihood - onehot.astype(jnp.float32)) * mask_ref[...].astype(jnp.float32) * scale
    slope = slope.astype(jnp.bfloat16)
    grad_rows_ref[...] = dot_wide(weight_ref[...], slope).astype(jnp.bfloat16)
    classes = logits.shape[1]
    terms = lax.dot_general(
        slope, z_output, (((0,), (0,)), ((), ())), preferred_element_type=jnp.float32
    )
    out_terms_ref[:classes, :] = terms
    pad = out_terms_ref.shape[0] - classes
    if pad:
        out_terms_ref[classes:, :] = jnp.zeros((pad, terms.shape[1]), jnp.float32)


def simple_call(body, shapes, name, *values):
    return pl.pallas_call(
        body,
        out_shape=shapes,
        compiler_params=pltpu.CompilerParams(vmem_limit_bytes=32 * 1024 * 1024),
        name=name,
    )(*values)


def dense_kernel(
    per_rep, tile_side, spot_ref, order_ref, moved_ref, place_ref, own_ref, other_ref, dense_ref
):
    position = pl.program_id(0)
    rep_index = spot_ref[0]
    edge = own_ref.shape[-1]
    slots = place_ref.shape[1]
    dense_ref[...] = jnp.zeros_like(dense_ref)

    def put_all(tiles_ref):
        def put(slot, carried):
            place = place_ref[position, slot]
            row = place // tile_side
            column = place % tile_side
            row = ((row // per_rep) ^ rep_index) * per_rep + row % per_rep
            column = ((column // per_rep) ^ rep_index) * per_rep + column % per_rep

            @pl.when(place >= 0)
            def _():
                dense_ref[
                    pl.ds(pl.multiple_of(row * edge, edge), edge),
                    pl.ds(pl.multiple_of(column * edge, edge), edge),
                ] = tiles_ref[0, slot]

            return carried

        lax.fori_loop(0, slots, put, 0)

    @pl.when(moved_ref[position] == 0)
    def _():
        put_all(own_ref)

    @pl.when(moved_ref[position] != 0)
    def _():
        put_all(other_ref)


def build_dense(tiles, others, place, spot, order, moved, own_rows, group_rows):
    sections, slots, edge, _ = tiles.shape
    body = functools.partial(dense_kernel, own_rows // edge, group_rows // edge)
    tile_block = (1, slots, edge, edge)
    other_block = (1, slots + 1, edge, edge)
    return pl.pallas_call(
        body,
        grid_spec=pltpu.PrefetchScalarGridSpec(
            num_scalar_prefetch=4,
            grid=(sections,),
            in_specs=[
                pl.BlockSpec(tile_block, lambda p, spot, order, *_: (order[p], 0, 0, 0)),
                pl.BlockSpec(
                    other_block, lambda p, spot, order, *_: (jnp.maximum(order[p] - 1, 0), 0, 0, 0)
                ),
            ],
            out_specs=pl.BlockSpec((group_rows, group_rows), lambda p, *_: (0, p)),
        ),
        out_shape=jax.ShapeDtypeStruct((group_rows, sections * group_rows), tiles.dtype),
        compiler_params=pltpu.CompilerParams(vmem_limit_bytes=40 * 1024 * 1024),
        cost_estimate=pl.CostEstimate(
            flops=0, bytes_accessed=2 * sections * group_rows * group_rows, transcendentals=0
        ),
        name="dense_tiles",
    )(spot, order, moved, place, tiles, others)


def on_device(
    features,
    node_ids,
    labels,
    train_mask,
    tile_values,
    tile_place,
    tile_count,
    weight_in,
    weight_out,
    class_bias,
):
    own_rows = features.shape[1]
    reps = lax.axis_size("rep")
    blks = lax.axis_size("blk")
    rep_index = lax.axis_index("rep")
    blk_index = lax.axis_index("blk")
    sections = tile_values.shape[2]
    group_rows = own_rows * reps
    hidden_width = weight_in.shape[1]
    scale = 1.0 / math.sqrt(group_rows * blks)
    f32 = jnp.float32
    bf16 = jnp.bfloat16

    def swap(value, delta):
        if delta == 0:
            return value
        return lax.ppermute(value, "rep", [(r, r ^ delta) for r in range(reps)])

    def exchange(value, delta):
        return lax.ppermute(value, "blk", [(c, c ^ delta) for c in range(blks)])

    def to_block(value):
        pieces = []
        for delta in range(reps):
            pairs = []
            for r in range(reps):
                for c in range(blks):
                    target = r ^ delta
                    pairs.append((r * blks + c, target * blks + (c + sections * target) % blks))
            pieces.append(lax.ppermute(value, ("rep", "blk"), pairs))
        return jnp.concatenate(pieces, axis=0)

    def to_both(block):
        return [block] + [exchange(block, delta) for delta in range(1, sections)]

    side = lax.rem(blk_index, 2)

    def halve(value):
        half = value.shape[0] // 2
        theirs = exchange(lax.dynamic_slice_in_dim(value, (1 - side) * half, half, 0), 1)
        return lax.dynamic_slice_in_dim(value, side * half, half, 0) + theirs

    def sum_over(value, move, first, size):
        rounded = value.astype(bf16)
        parts = [rounded if d == 0 else move(rounded, d) for d in range(0, size, first)]
        parts = [part.astype(f32) for part in parts]
        while len(parts) > 1:
            parts = [parts[i] + parts[i + 1] for i in range(0, len(parts), 2)]
        return parts[0]

    def undo_digits(rows):
        count = own_rows // rows.shape[1]
        parts = [rows[i * count : (i + 1) * count].astype(jnp.int32) for i in range(3)]
        return (parts[0] + (parts[1] << 8) + (parts[2] << 16)).reshape(own_rows)

    member = lax.rem(blk_index, sections)
    live = jnp.arange(tile_values.shape[3], dtype=jnp.int32)[None, :] < tile_count[0, 0][:, None]
    place = jnp.where(live, tile_place[0, 0], -1)
    slots, edge = tile_values.shape[3], tile_values.shape[4]
    width = features.shape[2]
    digit_rows = 3 * own_rows // width
    stride = own_rows + digit_rows + -digit_rows % 16
    vmem = pl.BlockSpec(memory_space=pltpu.VMEM)
    smem = pl.BlockSpec(memory_space=pltpu.SMEM)
    bundle, *parcels = pl.pallas_call(
        pack_kernel,
        in_specs=[smem, vmem, vmem, vmem, vmem],
        out_shape=[jax.ShapeDtypeStruct((stride, width), bf16)]
        + [jax.ShapeDtypeStruct((slots + 1, edge, edge), bf16)] * (sections - 1),
        compiler_params=pltpu.CompilerParams(vmem_limit_bytes=32 * 1024 * 1024),
        name="pack",
    )(
        tile_count[0, 0], features[0], node_ids.reshape(-1, width), tile_place[0, 0],
        tile_values[0, 0],
    )
    for j in range(1, sections):
        pairs = []
        for r in range(reps):
            for c in range(blks):
                if c % sections < j:
                    pairs.append((r * blks + c, (r + 1) % reps * blks + c))
        parcels[j - 1] = lax.ppermute(parcels[j - 1], ("rep", "blk"), pairs)
    block = to_block(bundle)
    block, parcels = lax.optimization_barrier((block, parcels))
    other_place = [place[0]]
    other_place += [parcel[slots, 0, :slots].astype(jnp.int32) - 1 for parcel in parcels]
    position = jnp.arange(sections, dtype=jnp.int32)
    column = position ^ member
    order = jnp.mod(member - column, sections)
    moved = (column > member).astype(jnp.int32)
    placed = jnp.where(moved[:, None] != 0, jnp.stack(other_place)[order], place[order])
    dense = build_dense(
        tile_values[0, 0],
        jnp.stack(parcels),
        placed,
        rep_index.reshape(1),
        order,
        moved,
        own_rows,
        group_rows,
    )
    pieces = [
        whole[d * stride : (d + 1) * stride] for whole in to_both(block) for d in range(reps)
    ]
    id_columns = jnp.concatenate([undo_digits(piece[own_rows:]) for piece in pieces])
    feature_columns = jnp.concatenate([piece[:own_rows] for piece in pieces], axis=0)
    units = jnp.arange(hidden_width, dtype=jnp.int32)
    kept = keep_mask(id_columns[:, None], units[None, :])
    kept_wide = keep_mask(id_columns[None, :], units[:, None])
    chunks = dot(dense, feature_columns).reshape(reps, own_rows, width)
    total = chunks[0]
    for delta in range(1, reps):
        total = total + swap(chunks[delta], delta)
    z_input = total.astype(bf16)
    z_columns = jnp.concatenate(to_both(to_block(z_input)), axis=0)
    kept, kept_wide, z_columns = lax.optimization_barrier((kept, kept_wide, z_columns))
    third = f32(4.0 / 3.0)
    pre_act = dot(z_columns, weight_in)
    dropped = (jnp.maximum(pre_act, 0.0) * (kept.astype(f32) * third)).astype(bf16)
    second = dot(dense, dropped)
    sent = simple_call(
        encode_kernel,
        [jax.ShapeDtypeStruct((own_rows + HEAD_ROWS, hidden_width), jnp.int16)] * (reps - 1),
        "encode", second,
    )
    arrived = [swap(sent[d - 1], d) for d in range(1, reps)]
    classes = weight_out.shape[1]
    logits, grad_rows, out_terms = simple_call(
        functools.partial(head_kernel, scale),
        (
            jax.ShapeDtypeStruct((own_rows, classes), f32),
            jax.ShapeDtypeStruct((hidden_width, own_rows), bf16),
            jax.ShapeDtypeStruct((classes + -classes % 16, hidden_width), f32),
        ),
        "head",
        weight_out, class_bias[None], labels[0][:, None], train_mask[0][:, None],
        second, *arrived,
    )
    grad_parts = [swap(grad_rows, d) for d in range(reps)]
    grad_parts, out_half = lax.optimization_barrier((grad_parts, halve(out_terms)))
    out_total = sum_over(out_half, exchange, 2, blks)
    pre_wide = lax.dot_general(
        weight_in, z_columns, (((0,), (1,)), ((), ())), preferred_element_type=f32
    )
    factor = jnp.where(pre_wide > 0, kept_wide.astype(f32) * third, 0.0)
    back = dot(jnp.concatenate(grad_parts, axis=1), dense)
    pre_slope = (back * factor).astype(bf16)
    in_terms = lax.dot_general(
        z_columns, pre_slope, (((0,), (1,)), ((), ())), preferred_element_type=f32
    )
    in_total = sum_over(halve(in_terms), exchange, 2, blks)
    both = sum_over(jnp.concatenate([in_total, out_total], axis=0), swap, 1, reps)
    grad_in, grad_out = pl.pallas_call(
        functools.partial(last_kernel, classes),
        in_specs=[smem, vmem, vmem],
        out_shape=[
            jax.ShapeDtypeStruct((width, hidden_width), f32),
            jax.ShapeDtypeStruct((hidden_width, classes), f32),
        ],
        name="last",
    )(side.reshape(1), both, exchange(both, 1))
    return (logits[None], grad_in, grad_out)


def solution(mesh):
    placed = (
        P("blk", "rep", None),
        P("blk", "rep"),
        P("blk", "rep"),
        P("blk", "rep"),
        P("blk", "rep", None, None, None, None),
        P("blk", "rep", None, None),
        P("blk", "rep", None),
        P(),
        P(),
        P(),
    )
    return jax.shard_map(
        on_device,
        mesh=mesh,
        in_specs=placed,
        out_specs=(P("blk", "rep", None), P(), P()),
        check_vma=False,
    )
```

```python
import functools
import math

import jax
import jax.numpy as jnp
from jax import lax
from jax.experimental import pallas as pl
from jax.experimental.pallas import tpu as pltpu
from jax.sharding import PartitionSpec as P


LEVELS = 32767.0
MANTISSA_BITS = 14
HEAD_ROWS = 16


def keep_mask(id_values, unit_values):
    mixed = id_values * 73244475 + unit_values * 19349663 + 12345
    mixed = mixed ^ jnp.right_shift(mixed, 15)
    mixed = mixed * 40503
    mixed = mixed ^ jnp.right_shift(mixed, 13)
    return (jnp.bitwise_and(mixed, 3) != 0).astype(jnp.bfloat16)


def eye_of(count):
    rows = lax.broadcasted_iota(jnp.int32, (count, count), 0)
    columns = lax.broadcasted_iota(jnp.int32, (count, count), 1)
    return rows == columns


def dot(left, right):
    return jnp.dot(left, right, preferred_element_type=jnp.float32)


def dot_wide(left, right):
    return lax.dot_general(
        left, right, (((1,), (1,)), ((), ())), preferred_element_type=jnp.float32
    )


def encode(values):
    rows, width = values.shape
    largest = jnp.maximum(jnp.max(jnp.abs(values), axis=1, keepdims=True), 1e-30)
    power = jnp.ceil(jnp.log2(largest))
    mantissa = jnp.ceil(largest * jnp.exp2(MANTISSA_BITS - power))
    scale = mantissa * jnp.exp2(power - MANTISSA_BITS)
    coded = jnp.clip(jnp.round(values * (LEVELS / scale)), -LEVELS, LEVELS)
    square = eye_of(width)
    index = lax.broadcasted_iota(jnp.int32, (HEAD_ROWS, width), 0)
    head = jnp.zeros((HEAD_ROWS, width), jnp.float32)
    for part in range(rows // width):
        for offset, column in enumerate((power, mantissa)):
            column = column[part * width : (part + 1) * width]
            line = jnp.sum(jnp.where(square, column, 0.0), axis=0, keepdims=True)
            head = jnp.where(index == 2 * part + offset, line, head)
    whole = jnp.concatenate([coded, head], axis=0)
    return whole.astype(jnp.int32).astype(jnp.int16)


def decode(coded):
    whole = coded.astype(jnp.int32).astype(jnp.float32)
    rows, width = whole.shape[0] - HEAD_ROWS, whole.shape[1]
    square = eye_of(width)
    columns = [[], []]
    for part in range(rows // width):
        for offset in range(2):
            start = rows + 2 * part + offset
            line = whole[start : start + 1]
            columns[offset].append(jnp.sum(jnp.where(square, line, 0.0), axis=1, keepdims=True))
    power, mantissa = (jnp.concatenate(parts, axis=0) for parts in columns)
    return whole[:rows] * (mantissa * jnp.exp2(power - MANTISSA_BITS) * (1.0 / LEVELS))


def encode_kernel(partial_ref, *coded_refs):
    own_rows = partial_ref.shape[0] // (len(coded_refs) + 1)
    for delta, coded_ref in enumerate(coded_refs, 1):
        coded_ref[...] = encode(partial_ref[delta * own_rows : (delta + 1) * own_rows, :])


def pack_kernel(sections, count_hbm, feature_hbm, id_hbm, place_hbm, tiles_hbm, bundle_ref, *refs):
    parcel_refs = refs[: sections - 1]
    count_ref, id_ref, place_ref, sems = refs[sections - 1 :]
    own_rows, lanes = feature_hbm.shape
    slots, edge = tiles_hbm.shape[1], tiles_hbm.shape[2]
    small = [
        pltpu.make_async_copy(id_hbm, id_ref, sems.at[0]),
        pltpu.make_async_copy(count_hbm, count_ref, sems.at[1]),
        pltpu.make_async_copy(place_hbm, place_ref, sems.at[2]),
    ]
    large = [pltpu.make_async_copy(feature_hbm, bundle_ref.at[pl.ds(0, own_rows)], sems.at[3])]
    for section, parcel_ref in enumerate(parcel_refs, 1):
        large.append(
            pltpu.make_async_copy(
                tiles_hbm.at[section], parcel_ref.at[pl.ds(0, slots)], sems.at[3 + section]
            )
        )
    for copy in small + large:
        copy.start()
    for copy in small:
        copy.wait()
    ids = id_ref[...]
    rows = ids.shape[0]
    parts = [ids & 255, jnp.right_shift(ids, 8) & 255, jnp.right_shift(ids, 16)]
    pad = bundle_ref.shape[0] - own_rows - 3 * rows
    parts += [jnp.zeros((pad, lanes), jnp.int32)] if pad else []
    digit_rows = jnp.concatenate(parts, axis=0).astype(jnp.float32).astype(jnp.bfloat16)
    bundle_ref[own_rows:, :] = digit_rows
    slot = lax.broadcasted_iota(jnp.int32, (1, slots), 1)
    first = lax.broadcasted_iota(jnp.int32, (edge, edge), 0) == 0
    for section, parcel_ref in enumerate(parcel_refs, 1):
        place = place_ref[section : section + 1, :]
        line = jnp.where(slot < count_ref[section], place + 1, 0)
        line = jnp.concatenate([line, jnp.zeros((1, edge - slots), jnp.int32)], axis=1)
        parcel_ref[slots] = jnp.where(first, line, 0).astype(jnp.float32).astype(jnp.bfloat16)
    for copy in large:
        copy.wait()


def last_kernel(chunk, spot_ref, total_ref, other_ref, grad_in_ref, grad_out_ref):
    side, rep_index = spot_ref[0], spot_ref[1]
    half = grad_in_ref.shape[0] // 2
    piece = chunk // 2
    classes = grad_out_ref.shape[0]
    reps = (total_ref.shape[0] - half) // piece
    for part in range(2):

        def take(start, size):
            rows = pl.ds(start, size)
            return jnp.where(side == part, total_ref[rows, :], other_ref[rows, :])

        grad_in_ref[part * half : (part + 1) * half, :] = take(0, half)
        for r in range(reps):
            start = r * chunk + part * piece
            size = min(piece, classes - start)
            if size > 0:
                spot = pl.multiple_of(half + (r ^ rep_index) * piece, 8)
                grad_out_ref[start : start + size, :] = take(spot, piece)[:size]


def head_kernel(
    scale, reps, spot_ref, weight_ref, bias_ref, label_ref, mask_ref, own_ref, *refs
):
    coded_refs, refs = refs[: reps - 1], refs[reps - 1 :]
    logits_ref, own_terms_ref, sent_refs, terms_ref = refs[0], refs[1], refs[2:-1], refs[-1]
    own_rows, classes = logits_ref.shape
    total = own_ref[:own_rows, :]
    for coded_ref in coded_refs:
        total += decode(coded_ref[...])
    z_output = total.astype(jnp.bfloat16)
    logits = dot(z_output, weight_ref[...]) + bias_ref[...]
    logits_ref[...] = logits
    shifted = jnp.exp(logits - jnp.max(logits, axis=1, keepdims=True))
    likelihood = shifted / jnp.sum(shifted, axis=1, keepdims=True)
    onehot = label_ref[...] == lax.broadcasted_iota(jnp.int32, logits.shape, 1)
    slope = (likelihood - onehot.astype(jnp.float32)) * mask_ref[...].astype(jnp.float32) * scale
    slope = slope.astype(jnp.bfloat16)
    grad_rows = dot_wide(slope, weight_ref[...]).astype(jnp.bfloat16)
    terms = lax.dot_general(
        slope, z_output, (((0,), (0,)), ((), ())), preferred_element_type=jnp.float32
    )
    terms_ref[:classes, :] = terms
    pad = terms_ref.shape[0] - classes
    if pad:
        terms_ref[classes:, :] = jnp.zeros((pad, terms.shape[1]), jnp.float32)
    chunk = own_terms_ref.shape[0]
    for delta, sent_ref in enumerate(sent_refs):
        start = pl.multiple_of((spot_ref[1] ^ delta) * chunk, 8)
        piece = terms_ref[pl.ds(start, chunk), :]
        sent_ref[:own_rows, :] = grad_rows
        sent_ref[own_rows:, :] = piece.astype(jnp.bfloat16)
        if delta == 0:
            own_terms_ref[...] = piece


def simple_call(body, shapes, name, *values, spot=(), scratch=()):
    smem = pl.BlockSpec(memory_space=pltpu.SMEM)
    vmem = pl.BlockSpec(memory_space=pltpu.VMEM)
    return pl.pallas_call(
        body,
        in_specs=[smem] * len(spot) + [vmem] * len(values),
        out_shape=shapes,
        scratch_shapes=scratch,
        compiler_params=pltpu.CompilerParams(vmem_limit_bytes=32 * 1024 * 1024),
        name=name,
    )(*spot, *values)


def dense_kernel(per_rep, tile_side, spot_ref, order_ref, moved_ref, place_ref, own_ref, *refs):
    other_ref, dense_ref, turned_ref = refs if len(refs) == 3 else (None, refs[0], None)
    position = pl.program_id(0)
    rep_index = spot_ref[0]
    edge = own_ref.shape[-1]
    slots = place_ref.shape[1]
    dense_ref[...] = jnp.zeros_like(dense_ref)
    if turned_ref is not None:
        turned_ref[...] = jnp.zeros_like(turned_ref)

    def put_all(tiles_ref):
        def put(slot, carried):
            place = place_ref[position, slot]
            row = place // tile_side
            column = place % tile_side
            row = ((row // per_rep) ^ rep_index) * per_rep + row % per_rep
            column = ((column // per_rep) ^ rep_index) * per_rep + column % per_rep

            @pl.when(place >= 0)
            def _():
                rows = pl.ds(pl.multiple_of(row * edge, edge), edge)
                columns = pl.ds(pl.multiple_of(column * edge, edge), edge)
                tile = tiles_ref[0, slot]
                dense_ref[rows, columns] = tile
                if turned_ref is not None:
                    turned_ref[columns, rows] = tile.T

            return carried

        lax.fori_loop(0, slots, put, 0)

    if other_ref is None:
        put_all(own_ref)
        return

    @pl.when(moved_ref[position] == 0)
    def _():
        put_all(own_ref)

    @pl.when(moved_ref[position] != 0)
    def _():
        put_all(other_ref)


def build_dense(tiles, others, place, spot, order, moved, own_rows, group_rows):
    sections, slots, edge, _ = tiles.shape
    body = functools.partial(dense_kernel, own_rows // edge, group_rows // edge)
    own_block = pl.BlockSpec((1, slots, edge, edge), lambda p, spot, order, *_: (order[p], 0, 0, 0))
    other_block = pl.BlockSpec(
        (1, slots + 1, edge, edge),
        lambda p, spot, order, *_: (jnp.maximum(order[p] - 1, 0), 0, 0, 0),
    )
    both = others is not None
    block = (group_rows, group_rows)
    flat = jax.ShapeDtypeStruct((group_rows, sections * group_rows), tiles.dtype)
    tall = jax.ShapeDtypeStruct((sections * group_rows, group_rows), tiles.dtype)
    flat_spec = pl.BlockSpec(block, lambda p, *_: (0, p))
    tall_spec = pl.BlockSpec(block, lambda p, *_: (p, 0))
    return pl.pallas_call(
        body,
        grid_spec=pltpu.PrefetchScalarGridSpec(
            num_scalar_prefetch=4,
            grid=(sections,),
            in_specs=[own_block, other_block] if both else [own_block],
            out_specs=[flat_spec, tall_spec] if both else flat_spec,
        ),
        out_shape=[flat, tall] if both else flat,
        compiler_params=pltpu.CompilerParams(vmem_limit_bytes=40 * 1024 * 1024),
        cost_estimate=pl.CostEstimate(
            flops=0, bytes_accessed=4 * sections * group_rows * group_rows, transcendentals=0
        ),
        name="dense_both" if both else "dense_first",
    )(spot, order, moved, place, *([tiles, others] if both else [tiles]))


def on_device(
    features,
    node_ids,
    labels,
    train_mask,
    tile_values,
    tile_place,
    tile_count,
    weight_in,
    weight_out,
    class_bias,
):
    own_rows = features.shape[1]
    reps = lax.axis_size("rep")
    blks = lax.axis_size("blk")
    rep_index = lax.axis_index("rep")
    blk_index = lax.axis_index("blk")
    sections = tile_values.shape[2]
    group_rows = own_rows * reps
    hidden_width = weight_in.shape[1]
    scale = 1.0 / math.sqrt(group_rows * blks)
    f32 = jnp.float32
    bf16 = jnp.bfloat16

    def swap(value, delta):
        if delta == 0:
            return value
        return lax.ppermute(value, "rep", [(r, r ^ delta) for r in range(reps)])

    def shift(value, steps):
        return lax.ppermute(value, "blk", [(c, (c + steps) % blks) for c in range(blks)])

    def exchange(value, delta):
        return lax.ppermute(value, "blk", [(c, c ^ delta) for c in range(blks)])

    def to_pieces(value):
        pieces = []
        for delta in range(reps):
            pairs = []
            for r in range(reps):
                for c in range(blks):
                    target = r ^ delta
                    pairs.append((r * blks + c, target * blks + (c + sections * target) % blks))
            pieces.append(lax.ppermute(value, ("rep", "blk"), pairs))
        return pieces

    def to_both(block):
        return [block] + [exchange(block, delta) for delta in range(1, sections)]

    side = lax.rem(blk_index, 2)

    def halve(value):
        half = value.shape[0] // 2
        theirs = exchange(lax.dynamic_slice_in_dim(value, (1 - side) * half, half, 0), 1)
        return lax.dynamic_slice_in_dim(value, side * half, half, 0) + theirs

    def sum_over(value, move, first, size):
        rounded = value.astype(bf16)
        parts = [rounded if d == 0 else move(rounded, d) for d in range(0, size, first)]
        parts = [part.astype(f32) for part in parts]
        while len(parts) > 1:
            parts = [parts[i] + parts[i + 1] for i in range(0, len(parts), 2)]
        return parts[0]

    def undo_digits(rows):
        count = own_rows // rows.shape[1]
        parts = [rows[i * count : (i + 1) * count].astype(jnp.int32) for i in range(3)]
        return (parts[0] + (parts[1] << 8) + (parts[2] << 16)).reshape(own_rows)

    member = lax.rem(blk_index, sections)
    live = jnp.arange(tile_values.shape[3], dtype=jnp.int32)[None, :] < tile_count[0, 0][:, None]
    place = jnp.where(live, tile_place[0, 0], -1)
    slots, edge = tile_values.shape[3], tile_values.shape[4]
    width = features.shape[2]
    digit_rows = 3 * own_rows // width
    stride = own_rows + digit_rows + -digit_rows % 16
    anywhere = pl.BlockSpec(memory_space=pl.ANY)
    bundle, *parcels = pl.pallas_call(
        functools.partial(pack_kernel, sections),
        in_specs=[anywhere] * 5,
        out_shape=[jax.ShapeDtypeStruct((stride, width), bf16)]
        + [jax.ShapeDtypeStruct((slots + 1, edge, edge), bf16)] * (sections - 1),
        scratch_shapes=[
            pltpu.SMEM((sections,), jnp.int32),
            pltpu.VMEM((own_rows // width, width), jnp.int32),
            pltpu.VMEM((sections, slots), jnp.int32),
            pltpu.SemaphoreType.DMA((sections + 3,)),
        ],
        compiler_params=pltpu.CompilerParams(vmem_limit_bytes=60 * 1024 * 1024),
        name="pack",
    )(
        tile_count[0, 0], features[0], node_ids.reshape(-1, width), tile_place[0, 0],
        tile_values[0, 0],
    )
    arrived = to_pieces(bundle)
    for j in range(1, sections):
        pairs = []
        for r in range(reps):
            for c in range(blks):
                if c % sections < j:
                    pairs.append((r * blks + c, (r + 1) % reps * blks + c))
        parcels[j - 1] = lax.ppermute(parcels[j - 1], ("rep", "blk"), pairs)
    other_place = [place[0]]
    other_place += [parcel[slots, 0, :slots].astype(jnp.int32) - 1 for parcel in parcels]
    position = jnp.arange(sections, dtype=jnp.int32)
    column = position ^ member
    order = jnp.mod(member - column, sections)
    moved = (column > member).astype(jnp.int32)
    placed = jnp.where(moved[:, None] != 0, jnp.stack(other_place)[order], place[order])
    tiles = tile_values[0, 0]
    where = rep_index.reshape(1)
    dense = build_dense(tiles, None, place, where, position, position, own_rows, group_rows)
    block = jnp.concatenate(arrived, axis=0)
    blocks = [block] + [shift(block, j) for j in range(1, sections)]
    pieces = [whole[d * stride : (d + 1) * stride] for whole in blocks for d in range(reps)]
    digit_sets = to_both(jnp.stack([part[own_rows:] for part in pieces[:reps]]))
    id_columns = jnp.concatenate([undo_digits(rows[d]) for rows in digit_sets for d in range(reps)])
    feature_columns = jnp.concatenate([piece[:own_rows] for piece in pieces], axis=0)
    units = jnp.arange(hidden_width, dtype=jnp.int32)
    kept = keep_mask(id_columns[:, None], units[None, :])
    chunks = dot(dense, feature_columns).reshape(reps, own_rows, width)
    dense, turned = build_dense(
        tiles, jnp.stack(parcels), placed, where, order, moved, own_rows, group_rows
    )
    total = chunks[0]
    for delta in range(1, reps):
        total = total + swap(chunks[delta], delta)
    z_input = total.astype(bf16)
    arrived = to_pieces(z_input)
    dense, turned, arrived = lax.optimization_barrier((dense, turned, arrived))
    z_columns = jnp.concatenate(to_both(jnp.concatenate(arrived, axis=0)), axis=0)
    kept, z_columns = lax.optimization_barrier((kept, z_columns))
    third = f32(4.0 / 3.0)
    pre_act = dot(z_columns, weight_in)
    factor = kept.astype(f32) * third
    dropped = (jnp.maximum(pre_act, 0.0) * factor).astype(bf16)
    second = dot(dense, dropped)
    sent = simple_call(
        encode_kernel,
        [jax.ShapeDtypeStruct((own_rows + HEAD_ROWS, hidden_width), jnp.int16)] * (reps - 1),
        "encode", second,
    )
    arrived = [swap(sent[d - 1], d) for d in range(1, reps)]
    classes = weight_out.shape[1]
    chunk = -(-classes // (16 * reps)) * 16
    spot = jnp.stack([side, rep_index])
    logits, out_total, *sent = simple_call(
        functools.partial(head_kernel, scale, reps),
        [
            jax.ShapeDtypeStruct((own_rows, classes), f32),
            jax.ShapeDtypeStruct((chunk, hidden_width), f32),
        ]
        + [jax.ShapeDtypeStruct((own_rows + chunk, hidden_width), bf16)] * reps,
        "head",
        weight_out, class_bias[None], labels[0][:, None], train_mask[0][:, None],
        second, *arrived,
        spot=(spot,),
        scratch=[pltpu.VMEM((chunk * reps, hidden_width), f32)],
    )
    arrived = [swap(sent[d], d) for d in range(reps)]
    grad_block = jnp.concatenate([part[:own_rows] for part in arrived], axis=0)
    for part in arrived[1:]:
        out_total = out_total + part[own_rows:].astype(f32)
    back = dot(turned, grad_block)
    pre_slope = (back * jnp.where(pre_act > 0, factor, 0.0)).astype(bf16)
    pre_slope, out_total = lax.optimization_barrier((pre_slope, out_total))
    in_terms = lax.dot_general(
        z_columns, pre_slope, (((0,), (0,)), ((), ())), preferred_element_type=f32
    )
    half, piece = width // 2, chunk // 2

    def halves(which):
        rows = [
            lax.dynamic_slice_in_dim(in_terms, which * half, half, 0),
            lax.dynamic_slice_in_dim(out_total, which * piece, piece, 0),
        ]
        return jnp.concatenate(rows, axis=0)

    total = halves(side) + exchange(halves(1 - side), 1)
    total = sum_over(total, exchange, 2, blks).astype(bf16)
    arrived = [swap(total, d) for d in range(reps)]
    parts = [part[:half].astype(f32) for part in arrived]
    while len(parts) > 1:
        parts = [parts[i] + parts[i + 1] for i in range(0, len(parts), 2)]
    total = jnp.concatenate(parts + [part[half:].astype(f32) for part in arrived], axis=0)
    grad_in, grad_wide = simple_call(
        functools.partial(last_kernel, chunk),
        [
            jax.ShapeDtypeStruct((width, hidden_width), f32),
            jax.ShapeDtypeStruct((classes, hidden_width), f32),
        ],
        "last", total, exchange(total, 1), spot=(spot,),
    )
    grad_out = grad_wide.T
    return (logits[None], grad_in, grad_out)


def solution(mesh):
    placed = (
        P("blk", "rep", None),
        P("blk", "rep"),
        P("blk", "rep"),
        P("blk", "rep"),
        P("blk", "rep", None, None, None, None),
        P("blk", "rep", None, None),
        P("blk", "rep", None),
        P(),
        P(),
        P(),
    )
    return jax.shard_map(
        on_device,
        mesh=mesh,
        in_specs=placed,
        out_specs=(P("blk", "rep", None), P(), P()),
        check_vma=False,
    )
```

```python
import functools
import math

import jax
import jax.numpy as jnp
from jax import lax
from jax.experimental import pallas as pl
from jax.experimental.pallas import tpu as pltpu
from jax.sharding import PartitionSpec as P


LEVELS = 32767.0
MANTISSA_BITS = 14
HEAD_ROWS = 16


def keep_mask(id_values, unit_values):
    mixed = id_values * 73244475 + unit_values * 19349663 + 12345
    mixed = mixed ^ jnp.right_shift(mixed, 15)
    mixed = mixed * 40503
    mixed = mixed ^ jnp.right_shift(mixed, 13)
    return (jnp.bitwise_and(mixed, 3) != 0).astype(jnp.bfloat16)


def eye_of(count):
    rows = lax.broadcasted_iota(jnp.int32, (count, count), 0)
    columns = lax.broadcasted_iota(jnp.int32, (count, count), 1)
    return rows == columns


def dot(left, right):
    return jnp.dot(left, right, preferred_element_type=jnp.float32)


def dot_wide(left, right):
    return lax.dot_general(
        left, right, (((1,), (1,)), ((), ())), preferred_element_type=jnp.float32
    )


def encode(values):
    rows, width = values.shape
    largest = jnp.maximum(jnp.max(jnp.abs(values), axis=1, keepdims=True), 1e-30)
    power = jnp.ceil(jnp.log2(largest))
    mantissa = jnp.ceil(largest * jnp.exp2(MANTISSA_BITS - power))
    scale = mantissa * jnp.exp2(power - MANTISSA_BITS)
    coded = jnp.clip(jnp.round(values * (LEVELS / scale)), -LEVELS, LEVELS)
    square = eye_of(width)
    index = lax.broadcasted_iota(jnp.int32, (HEAD_ROWS, width), 0)
    head = jnp.zeros((HEAD_ROWS, width), jnp.float32)
    for part in range(rows // width):
        for offset, column in enumerate((power, mantissa)):
            column = column[part * width : (part + 1) * width]
            line = jnp.sum(jnp.where(square, column, 0.0), axis=0, keepdims=True)
            head = jnp.where(index == 2 * part + offset, line, head)
    whole = jnp.concatenate([coded, head], axis=0)
    return whole.astype(jnp.int32).astype(jnp.int16)


def decode(coded):
    whole = coded.astype(jnp.int32).astype(jnp.float32)
    rows, width = whole.shape[0] - HEAD_ROWS, whole.shape[1]
    square = eye_of(width)
    columns = [[], []]
    for part in range(rows // width):
        for offset in range(2):
            start = rows + 2 * part + offset
            line = whole[start : start + 1]
            columns[offset].append(jnp.sum(jnp.where(square, line, 0.0), axis=1, keepdims=True))
    power, mantissa = (jnp.concatenate(parts, axis=0) for parts in columns)
    return whole[:rows] * (mantissa * jnp.exp2(power - MANTISSA_BITS) * (1.0 / LEVELS))


def encode_kernel(partial_ref, *coded_refs):
    own_rows = partial_ref.shape[0] // (len(coded_refs) + 1)
    for delta, coded_ref in enumerate(coded_refs, 1):
        coded_ref[...] = encode(partial_ref[delta * own_rows : (delta + 1) * own_rows, :])


def pack_kernel(sections, count_hbm, feature_hbm, id_hbm, place_hbm, tiles_hbm, bundle_ref, *refs):
    parcel_refs = refs[: sections - 1]
    count_ref, id_ref, place_ref, sems = refs[sections - 1 :]
    own_rows, lanes = feature_hbm.shape
    slots, edge = tiles_hbm.shape[1], tiles_hbm.shape[2]
    small = [
        pltpu.make_async_copy(id_hbm, id_ref, sems.at[0]),
        pltpu.make_async_copy(count_hbm, count_ref, sems.at[1]),
        pltpu.make_async_copy(place_hbm, place_ref, sems.at[2]),
    ]
    large = [pltpu.make_async_copy(feature_hbm, bundle_ref.at[pl.ds(0, own_rows)], sems.at[3])]
    for section, parcel_ref in enumerate(parcel_refs, 1):
        large.append(
            pltpu.make_async_copy(
                tiles_hbm.at[section], parcel_ref.at[pl.ds(0, slots)], sems.at[3 + section]
            )
        )
    for copy in small + large:
        copy.start()
    for copy in small:
        copy.wait()
    ids = id_ref[...]
    rows = ids.shape[0]
    parts = [ids & 255, jnp.right_shift(ids, 8) & 255, jnp.right_shift(ids, 16)]
    pad = bundle_ref.shape[0] - own_rows - 3 * rows
    parts += [jnp.zeros((pad, lanes), jnp.int32)] if pad else []
    digit_rows = jnp.concatenate(parts, axis=0).astype(jnp.float32).astype(jnp.bfloat16)
    bundle_ref[own_rows:, :] = digit_rows
    slot = lax.broadcasted_iota(jnp.int32, (1, slots), 1)
    first = lax.broadcasted_iota(jnp.int32, (edge, edge), 0) == 0
    for section, parcel_ref in enumerate(parcel_refs, 1):
        place = place_ref[section : section + 1, :]
        line = jnp.where(slot < count_ref[section], place + 1, 0)
        line = jnp.concatenate([line, jnp.zeros((1, edge - slots), jnp.int32)], axis=1)
        parcel_ref[slots] = jnp.where(first, line, 0).astype(jnp.float32).astype(jnp.bfloat16)
    for copy in large:
        copy.wait()


def last_kernel(chunk, spot_ref, total_ref, other_ref, grad_in_ref, grad_out_ref):
    side, rep_index = spot_ref[0], spot_ref[1]
    half = grad_in_ref.shape[0] // 2
    piece = chunk // 2
    classes = grad_out_ref.shape[0]
    reps = (total_ref.shape[0] - half) // piece
    for part in range(2):

        def take(start, size):
            rows = pl.ds(start, size)
            return jnp.where(side == part, total_ref[rows, :], other_ref[rows, :])

        grad_in_ref[part * half : (part + 1) * half, :] = take(0, half)
        for r in range(reps):
            start = r * chunk + part * piece
            size = min(piece, classes - start)
            if size > 0:
                spot = pl.multiple_of(half + (r ^ rep_index) * piece, 8)
                grad_out_ref[start : start + size, :] = take(spot, piece)[:size]


def head_kernel(
    scale, reps, spot_ref, weight_ref, bias_ref, label_ref, mask_ref, own_ref, *refs
):
    coded_refs, refs = refs[: reps - 1], refs[reps - 1 :]
    logits_ref, own_terms_ref, sent_refs, terms_ref = refs[0], refs[1], refs[2:-1], refs[-1]
    own_rows, classes = logits_ref.shape
    total = own_ref[:own_rows, :]
    for coded_ref in coded_refs:
        total += decode(coded_ref[...])
    z_output = total.astype(jnp.bfloat16)
    logits = dot(z_output, weight_ref[...]) + bias_ref[...]
    logits_ref[...] = logits
    shifted = jnp.exp(logits - jnp.max(logits, axis=1, keepdims=True))
    likelihood = shifted / jnp.sum(shifted, axis=1, keepdims=True)
    onehot = label_ref[...] == lax.broadcasted_iota(jnp.int32, logits.shape, 1)
    slope = (likelihood - onehot.astype(jnp.float32)) * mask_ref[...].astype(jnp.float32) * scale
    slope = slope.astype(jnp.bfloat16)
    grad_rows = dot_wide(slope, weight_ref[...]).astype(jnp.bfloat16)
    terms = lax.dot_general(
        slope, z_output, (((0,), (0,)), ((), ())), preferred_element_type=jnp.float32
    )
    terms_ref[:classes, :] = terms
    pad = terms_ref.shape[0] - classes
    if pad:
        terms_ref[classes:, :] = jnp.zeros((pad, terms.shape[1]), jnp.float32)
    chunk = own_terms_ref.shape[0]
    for delta, sent_ref in enumerate(sent_refs):
        start = pl.multiple_of((spot_ref[1] ^ delta) * chunk, 8)
        piece = terms_ref[pl.ds(start, chunk), :]
        sent_ref[:own_rows, :] = grad_rows
        sent_ref[own_rows:, :] = piece.astype(jnp.bfloat16)
        if delta == 0:
            own_terms_ref[...] = piece


def simple_call(body, shapes, name, *values, spot=(), scratch=()):
    smem = pl.BlockSpec(memory_space=pltpu.SMEM)
    vmem = pl.BlockSpec(memory_space=pltpu.VMEM)
    return pl.pallas_call(
        body,
        in_specs=[smem] * len(spot) + [vmem] * len(values),
        out_shape=shapes,
        scratch_shapes=scratch,
        compiler_params=pltpu.CompilerParams(vmem_limit_bytes=32 * 1024 * 1024),
        name=name,
    )(*spot, *values)


def dense_kernel(
    per_rep, tile_side, turn, spot_ref, order_ref, moved_ref, place_ref, own_ref, *refs
):
    other_ref, dense_ref = refs if len(refs) == 2 else (None, refs[0])
    position = pl.program_id(0)
    rep_index, source_rep = spot_ref[0], spot_ref[1 + position]
    edge = own_ref.shape[-1]
    slots = place_ref.shape[1]
    dense_ref[...] = jnp.zeros_like(dense_ref)

    def put_all(tiles_ref):
        def put(slot, carried):
            place = place_ref[position, slot]
            row = place // tile_side
            column = place % tile_side
            row = ((row // per_rep) ^ rep_index) * per_rep + row % per_rep
            column = ((column // per_rep) ^ source_rep) * per_rep + column % per_rep

            @pl.when(place >= 0)
            def _():
                rows = pl.ds(pl.multiple_of(row * edge, edge), edge)
                columns = pl.ds(pl.multiple_of(column * edge, edge), edge)
                tile = tiles_ref[0, slot]
                if turn:
                    dense_ref[columns, rows] = tile.T
                else:
                    dense_ref[rows, columns] = tile

            return carried

        lax.fori_loop(0, slots, put, 0)

    if other_ref is None:
        put_all(own_ref)
        return

    @pl.when(moved_ref[position] == 0)
    def _():
        put_all(own_ref)

    @pl.when(moved_ref[position] != 0)
    def _():
        put_all(other_ref)


def build_dense(tiles, others, place, spot, order, moved, own_rows, group_rows, turn=False):
    sections, slots, edge, _ = tiles.shape
    body = functools.partial(dense_kernel, own_rows // edge, group_rows // edge, turn)
    own_block = pl.BlockSpec((1, slots, edge, edge), lambda p, spot, order, *_: (order[p], 0, 0, 0))
    other_block = pl.BlockSpec(
        (1, slots + 1, edge, edge),
        lambda p, spot, order, *_: (jnp.maximum(order[p] - 1, 0), 0, 0, 0),
    )
    both = others is not None
    block = (group_rows, group_rows)
    shape = (sections * group_rows, group_rows) if turn else (group_rows, sections * group_rows)
    return pl.pallas_call(
        body,
        grid_spec=pltpu.PrefetchScalarGridSpec(
            num_scalar_prefetch=4,
            grid=(sections,),
            in_specs=[own_block, other_block] if both else [own_block],
            out_specs=pl.BlockSpec(block, lambda p, *_: (p, 0) if turn else (0, p)),
        ),
        out_shape=jax.ShapeDtypeStruct(shape, tiles.dtype),
        compiler_params=pltpu.CompilerParams(vmem_limit_bytes=40 * 1024 * 1024),
        cost_estimate=pl.CostEstimate(
            flops=0, bytes_accessed=4 * sections * group_rows * group_rows, transcendentals=0
        ),
        name="dense_turned" if turn else "dense",
    )(spot, order, moved, place, *([tiles, others] if both else [tiles]))


def on_device(
    features,
    node_ids,
    labels,
    train_mask,
    tile_values,
    tile_place,
    tile_count,
    weight_in,
    weight_out,
    class_bias,
):
    own_rows = features.shape[1]
    reps = lax.axis_size("rep")
    blks = lax.axis_size("blk")
    rep_index = lax.axis_index("rep")
    blk_index = lax.axis_index("blk")
    sections = tile_values.shape[2]
    group_rows = own_rows * reps
    hidden_width = weight_in.shape[1]
    scale = 1.0 / math.sqrt(group_rows * blks)
    f32 = jnp.float32
    bf16 = jnp.bfloat16

    def swap(value, delta):
        if delta == 0:
            return value
        return lax.ppermute(value, "rep", [(r, r ^ delta) for r in range(reps)])

    def to_section(block, j):
        pairs = []
        for r in range(reps):
            for c in range(blks):
                member = c % sections + j
                if member < sections:
                    pairs.append((r * blks + c, r * blks + c + j))
                else:
                    pairs.append((r * blks + c, (r - 1) % reps * blks + c + j - sections))
        return lax.ppermute(block, ("rep", "blk"), pairs)

    def exchange(value, delta):
        return lax.ppermute(value, "blk", [(c, c ^ delta) for c in range(blks)])

    def to_pieces(value):
        pieces = []
        for delta in range(reps):
            pairs = []
            for r in range(reps):
                for c in range(blks):
                    target = r ^ delta
                    pairs.append((r * blks + c, target * blks + (c + sections * target) % blks))
            pieces.append(lax.ppermute(value, ("rep", "blk"), pairs))
        return pieces

    def to_both(block):
        return [block] + [exchange(block, delta) for delta in range(1, sections)]

    side = lax.rem(blk_index, 2)

    def halve(value):
        half = value.shape[0] // 2
        theirs = exchange(lax.dynamic_slice_in_dim(value, (1 - side) * half, half, 0), 1)
        return lax.dynamic_slice_in_dim(value, side * half, half, 0) + theirs

    def sum_over(value, move, first, size):
        rounded = value.astype(bf16)
        parts = [rounded if d == 0 else move(rounded, d) for d in range(0, size, first)]
        parts = [part.astype(f32) for part in parts]
        while len(parts) > 1:
            parts = [parts[i] + parts[i + 1] for i in range(0, len(parts), 2)]
        return parts[0]

    def undo_digits(rows):
        count = own_rows // rows.shape[1]
        parts = [rows[i * count : (i + 1) * count].astype(jnp.int32) for i in range(3)]
        return (parts[0] + (parts[1] << 8) + (parts[2] << 16)).reshape(own_rows)

    member = lax.rem(blk_index, sections)
    live = jnp.arange(tile_values.shape[3], dtype=jnp.int32)[None, :] < tile_count[0, 0][:, None]
    place = jnp.where(live, tile_place[0, 0], -1)
    slots, edge = tile_values.shape[3], tile_values.shape[4]
    width = features.shape[2]
    digit_rows = 3 * own_rows // width
    stride = own_rows + digit_rows + -digit_rows % 16
    anywhere = pl.BlockSpec(memory_space=pl.ANY)
    bundle, *parcels = pl.pallas_call(
        functools.partial(pack_kernel, sections),
        in_specs=[anywhere] * 5,
        out_shape=[jax.ShapeDtypeStruct((stride, width), bf16)]
        + [jax.ShapeDtypeStruct((slots + 1, edge, edge), bf16)] * (sections - 1),
        scratch_shapes=[
            pltpu.SMEM((sections,), jnp.int32),
            pltpu.VMEM((own_rows // width, width), jnp.int32),
            pltpu.VMEM((sections, slots), jnp.int32),
            pltpu.SemaphoreType.DMA((sections + 3,)),
        ],
        compiler_params=pltpu.CompilerParams(vmem_limit_bytes=60 * 1024 * 1024),
        name="pack",
    )(
        tile_count[0, 0], features[0], node_ids.reshape(-1, width), tile_place[0, 0],
        tile_values[0, 0],
    )
    arrived = to_pieces(bundle)
    for j in range(1, sections):
        pairs = []
        for r in range(reps):
            for c in range(blks):
                if c % sections < j:
                    pairs.append((r * blks + c, (r + 1) % reps * blks + c))
        parcels[j - 1] = lax.ppermute(parcels[j - 1], ("rep", "blk"), pairs)
    other_place = [place[0]]
    other_place += [parcel[slots, 0, :slots].astype(jnp.int32) - 1 for parcel in parcels]
    position = jnp.arange(sections, dtype=jnp.int32)
    column = position ^ member
    order = jnp.mod(member - column, sections)
    moved = (column > member).astype(jnp.int32)
    placed = jnp.where(moved[:, None] != 0, jnp.stack(other_place)[order], place[order])
    tiles = tile_values[0, 0]
    where = jnp.broadcast_to(rep_index, (sections + 1,))
    next_rep = lax.rem(rep_index + 1, reps)
    first_where = jnp.where(member < jnp.arange(sections + 1) - 1, next_rep, rep_index)
    block = jnp.concatenate(arrived, axis=0)
    place, block = lax.optimization_barrier((place, block))
    dense = build_dense(
        tiles, None, place, first_where, position, position, own_rows, group_rows
    )
    blocks = [block] + [to_section(block, j) for j in range(1, sections)]
    pieces = [whole[d * stride : (d + 1) * stride] for whole in blocks for d in range(reps)]
    digit_sets = to_both(jnp.stack([part[own_rows:] for part in pieces[:reps]]))
    id_columns = jnp.concatenate([undo_digits(rows[d]) for rows in digit_sets for d in range(reps)])
    feature_columns = jnp.concatenate([piece[:own_rows] for piece in pieces], axis=0)
    units = jnp.arange(hidden_width, dtype=jnp.int32)
    kept = keep_mask(id_columns[:, None], units[None, :])
    chunks = dot(dense, feature_columns).reshape(reps, own_rows, width)
    layout = (tiles, jnp.stack(parcels), placed, where, order, moved, own_rows, group_rows)
    arrived = [swap(chunks[delta], delta) for delta in range(1, reps)]
    dense, arrived = lax.optimization_barrier((build_dense(*layout), arrived))
    total = chunks[0]
    for part in arrived:
        total = total + part
    z_input = total.astype(bf16)
    arrived = to_pieces(z_input)
    z_columns = jnp.concatenate(to_both(jnp.concatenate(arrived, axis=0)), axis=0)
    kept, z_columns = lax.optimization_barrier((kept, z_columns))
    third = f32(4.0 / 3.0)
    pre_act = dot(z_columns, weight_in)
    dropped = (jnp.maximum(pre_act, 0.0) * (kept.astype(f32) * third)).astype(bf16)
    mask = jnp.where(pre_act > 0, kept, jnp.zeros_like(kept))
    second = dot(dense, dropped)
    sent = simple_call(
        encode_kernel,
        [jax.ShapeDtypeStruct((own_rows + HEAD_ROWS, hidden_width), jnp.int16)] * (reps - 1),
        "encode", second,
    )
    arrived = [swap(sent[d - 1], d) for d in range(1, reps)]
    turned, mask, second = lax.optimization_barrier(
        (build_dense(*layout, turn=True), mask, second)
    )
    classes = weight_out.shape[1]
    chunk = -(-classes // (16 * reps)) * 16
    spot = jnp.stack([side, rep_index])
    logits, out_total, *sent = simple_call(
        functools.partial(head_kernel, scale, reps),
        [
            jax.ShapeDtypeStruct((own_rows, classes), f32),
            jax.ShapeDtypeStruct((chunk, hidden_width), f32),
        ]
        + [jax.ShapeDtypeStruct((own_rows + chunk, hidden_width), bf16)] * reps,
        "head",
        weight_out, class_bias[None], labels[0][:, None], train_mask[0][:, None],
        second, *arrived,
        spot=(spot,),
        scratch=[pltpu.VMEM((chunk * reps, hidden_width), f32)],
    )
    arrived = [swap(sent[d], d) for d in range(reps)]
    grad_block = jnp.concatenate([part[:own_rows] for part in arrived], axis=0)
    for part in arrived[1:]:
        out_total = out_total + part[own_rows:].astype(f32)
    grad_block, out_total = lax.optimization_barrier((grad_block, out_total))
    back = dot(turned, grad_block)
    pre_slope = (back * (mask.astype(f32) * third)).astype(bf16)
    pre_slope, out_total = lax.optimization_barrier((pre_slope, out_total))
    in_terms = lax.dot_general(
        z_columns, pre_slope, (((0,), (0,)), ((), ())), preferred_element_type=f32
    )
    half, piece = width // 2, chunk // 2

    def halves(which):
        rows = [
            lax.dynamic_slice_in_dim(in_terms, which * half, half, 0),
            lax.dynamic_slice_in_dim(out_total, which * piece, piece, 0),
        ]
        return jnp.concatenate(rows, axis=0)

    total = halves(side) + exchange(halves(1 - side), 1)
    total = sum_over(total, exchange, 2, blks).astype(bf16)
    arrived = [swap(total, d) for d in range(reps)]
    parts = [part[:half].astype(f32) for part in arrived]
    while len(parts) > 1:
        parts = [parts[i] + parts[i + 1] for i in range(0, len(parts), 2)]
    total = jnp.concatenate(parts + [part[half:].astype(f32) for part in arrived], axis=0)
    grad_in, grad_wide = simple_call(
        functools.partial(last_kernel, chunk),
        [
            jax.ShapeDtypeStruct((width, hidden_width), f32),
            jax.ShapeDtypeStruct((classes, hidden_width), f32),
        ],
        "last", total, exchange(total, 1), spot=(spot,),
    )
    grad_out = grad_wide.T
    return (logits[None], grad_in, grad_out)


def solution(mesh):
    placed = (
        P("blk", "rep", None),
        P("blk", "rep"),
        P("blk", "rep"),
        P("blk", "rep"),
        P("blk", "rep", None, None, None, None),
        P("blk", "rep", None, None),
        P("blk", "rep", None),
        P(),
        P(),
        P(),
    )
    return jax.shard_map(
        on_device,
        mesh=mesh,
        in_specs=placed,
        out_specs=(P("blk", "rep", None), P(), P()),
        check_vma=False,
    )
```

```python
import functools
import math

import jax
import jax.numpy as jnp
from jax import lax
from jax.experimental import pallas as pl
from jax.experimental.pallas import tpu as pltpu
from jax.sharding import PartitionSpec as P


LEVELS = 32767.0
MANTISSA_BITS = 14
HEAD_ROWS = 16


def keep_mask(id_values, unit_values):
    mixed = id_values * 73244475 + unit_values * 19349663 + 12345
    mixed = mixed ^ jnp.right_shift(mixed, 15)
    mixed = mixed * 40503
    mixed = mixed ^ jnp.right_shift(mixed, 13)
    return (jnp.bitwise_and(mixed, 3) != 0).astype(jnp.bfloat16)


def eye_of(count):
    rows = lax.broadcasted_iota(jnp.int32, (count, count), 0)
    columns = lax.broadcasted_iota(jnp.int32, (count, count), 1)
    return rows == columns


def dot(left, right):
    return jnp.dot(left, right, preferred_element_type=jnp.float32)


def dot_wide(left, right):
    return lax.dot_general(
        left, right, (((1,), (1,)), ((), ())), preferred_element_type=jnp.float32
    )


def encode(values):
    rows, width = values.shape
    largest = jnp.maximum(jnp.max(jnp.abs(values), axis=1, keepdims=True), 1e-30)
    power = jnp.ceil(jnp.log2(largest))
    mantissa = jnp.ceil(largest * jnp.exp2(MANTISSA_BITS - power))
    scale = mantissa * jnp.exp2(power - MANTISSA_BITS)
    coded = jnp.clip(jnp.round(values * (LEVELS / scale)), -LEVELS, LEVELS)
    square = eye_of(width)
    index = lax.broadcasted_iota(jnp.int32, (HEAD_ROWS, width), 0)
    head = jnp.zeros((HEAD_ROWS, width), jnp.float32)
    for part in range(rows // width):
        for offset, column in enumerate((power, mantissa)):
            column = column[part * width : (part + 1) * width]
            line = jnp.sum(jnp.where(square, column, 0.0), axis=0, keepdims=True)
            head = jnp.where(index == 2 * part + offset, line, head)
    whole = jnp.concatenate([coded, head], axis=0)
    return whole.astype(jnp.int32).astype(jnp.int16)


def decode(coded):
    whole = coded.astype(jnp.int32).astype(jnp.float32)
    rows, width = whole.shape[0] - HEAD_ROWS, whole.shape[1]
    square = eye_of(width)
    columns = [[], []]
    for part in range(rows // width):
        for offset in range(2):
            start = rows + 2 * part + offset
            line = whole[start : start + 1]
            columns[offset].append(jnp.sum(jnp.where(square, line, 0.0), axis=1, keepdims=True))
    power, mantissa = (jnp.concatenate(parts, axis=0) for parts in columns)
    return whole[:rows] * (mantissa * jnp.exp2(power - MANTISSA_BITS) * (1.0 / LEVELS))


def encode_kernel(partial_ref, *coded_refs):
    own_rows = partial_ref.shape[0] // (len(coded_refs) + 1)
    for delta, coded_ref in enumerate(coded_refs, 1):
        coded_ref[...] = encode(partial_ref[delta * own_rows : (delta + 1) * own_rows, :])


def pack_kernel(sections, count_hbm, feature_hbm, id_hbm, place_hbm, tiles_hbm, bundle_ref, *refs):
    parcel_refs = refs[: sections - 1]
    count_ref, id_ref, place_ref, sems = refs[sections - 1 :]
    own_rows, lanes = feature_hbm.shape
    slots, edge = tiles_hbm.shape[1], tiles_hbm.shape[2]
    small = [
        pltpu.make_async_copy(id_hbm, id_ref, sems.at[0]),
        pltpu.make_async_copy(count_hbm, count_ref, sems.at[1]),
        pltpu.make_async_copy(place_hbm, place_ref, sems.at[2]),
    ]
    large = [pltpu.make_async_copy(feature_hbm, bundle_ref.at[pl.ds(0, own_rows)], sems.at[3])]
    for section, parcel_ref in enumerate(parcel_refs, 1):
        large.append(
            pltpu.make_async_copy(
                tiles_hbm.at[section], parcel_ref.at[pl.ds(0, slots)], sems.at[3 + section]
            )
        )
    for copy in small + large:
        copy.start()
    for copy in small:
        copy.wait()
    ids = id_ref[...]
    rows = ids.shape[0]
    parts = [ids & 255, jnp.right_shift(ids, 8) & 255, jnp.right_shift(ids, 16)]
    pad = bundle_ref.shape[0] - own_rows - 3 * rows
    parts += [jnp.zeros((pad, lanes), jnp.int32)] if pad else []
    digit_rows = jnp.concatenate(parts, axis=0).astype(jnp.float32).astype(jnp.bfloat16)
    bundle_ref[own_rows:, :] = digit_rows
    first = lax.broadcasted_iota(jnp.int32, (edge, edge), 0) == 0
    for section, parcel_ref in enumerate(parcel_refs, 1):
        place = place_ref[section : section + 1, :]
        line = jnp.concatenate(
            [place, jnp.full((1, edge - slots), count_ref[section], jnp.int32)], axis=1
        )
        parcel_ref[slots] = jnp.where(first, line, 0).astype(jnp.float32).astype(jnp.bfloat16)
    for copy in large:
        copy.wait()


def last_kernel(chunk, spot_ref, total_ref, other_ref, grad_in_ref, grad_out_ref):
    side, rep_index = spot_ref[0], spot_ref[1]
    half = grad_in_ref.shape[0] // 2
    piece = chunk // 2
    classes = grad_out_ref.shape[0]
    reps = (total_ref.shape[0] - half) // piece
    for part in range(2):

        def take(start, size):
            rows = pl.ds(start, size)
            return jnp.where(side == part, total_ref[rows, :], other_ref[rows, :])

        grad_in_ref[part * half : (part + 1) * half, :] = take(0, half)
        for r in range(reps):
            start = r * chunk + part * piece
            size = min(piece, classes - start)
            if size > 0:
                spot = pl.multiple_of(half + (r ^ rep_index) * piece, 8)
                grad_out_ref[start : start + size, :] = take(spot, piece)[:size]


def head_kernel(
    scale, reps, spot_ref, weight_ref, bias_ref, label_ref, mask_ref, own_ref, *refs
):
    coded_refs, refs = refs[: reps - 1], refs[reps - 1 :]
    logits_ref, own_terms_ref, sent_refs, terms_ref = refs[0], refs[1], refs[2:-1], refs[-1]
    own_rows, classes = logits_ref.shape
    total = own_ref[:own_rows, :]
    for coded_ref in coded_refs:
        total += decode(coded_ref[...])
    z_output = total.astype(jnp.bfloat16)
    logits = dot(z_output, weight_ref[...]) + bias_ref[...]
    logits_ref[...] = logits
    shifted = jnp.exp(logits - jnp.max(logits, axis=1, keepdims=True))
    likelihood = shifted / jnp.sum(shifted, axis=1, keepdims=True)
    onehot = label_ref[...] == lax.broadcasted_iota(jnp.int32, logits.shape, 1)
    slope = (likelihood - onehot.astype(jnp.float32)) * mask_ref[...].astype(jnp.float32) * scale
    slope = slope.astype(jnp.bfloat16)
    grad_rows = dot_wide(slope, weight_ref[...]).astype(jnp.bfloat16)
    terms = lax.dot_general(
        slope, z_output, (((0,), (0,)), ((), ())), preferred_element_type=jnp.float32
    )
    terms_ref[:classes, :] = terms
    pad = terms_ref.shape[0] - classes
    if pad:
        terms_ref[classes:, :] = jnp.zeros((pad, terms.shape[1]), jnp.float32)
    chunk = own_terms_ref.shape[0]
    for delta, sent_ref in enumerate(sent_refs):
        start = pl.multiple_of((spot_ref[1] ^ delta) * chunk, 8)
        piece = terms_ref[pl.ds(start, chunk), :]
        sent_ref[:own_rows, :] = grad_rows
        sent_ref[own_rows:, :] = piece.astype(jnp.bfloat16)
        if delta == 0:
            own_terms_ref[...] = piece


def simple_call(body, shapes, name, *values, spot=(), scratch=()):
    smem = pl.BlockSpec(memory_space=pltpu.SMEM)
    vmem = pl.BlockSpec(memory_space=pltpu.VMEM)
    return pl.pallas_call(
        body,
        in_specs=[smem] * len(spot) + [vmem] * len(values),
        out_shape=shapes,
        scratch_shapes=scratch,
        compiler_params=pltpu.CompilerParams(vmem_limit_bytes=8 * 1024 * 1024),
        name=name,
    )(*spot, *values)


def dense_kernel(
    per_rep, tile_side, turn, spot_ref, order_ref, moved_ref, place_ref, count_ref, own_ref, *refs
):
    other_ref, dense_ref = refs if len(refs) == 2 else (None, refs[0])
    position = pl.program_id(0)
    rep_index, source_rep = spot_ref[0], spot_ref[1 + position]
    edge = own_ref.shape[-1]
    dense_ref[...] = jnp.zeros_like(dense_ref)

    section = order_ref[position]

    def put_all(tiles_ref, row_of, count):
        def put(slot, carried):
            place = place_ref[row_of, slot]
            row = place // tile_side
            column = place % tile_side
            row = ((row // per_rep) ^ rep_index) * per_rep + row % per_rep
            column = ((column // per_rep) ^ source_rep) * per_rep + column % per_rep

            rows = pl.ds(pl.multiple_of(row * edge, edge), edge)
            columns = pl.ds(pl.multiple_of(column * edge, edge), edge)
            tile = tiles_ref[0, slot]
            if turn:
                dense_ref[columns, rows] = tile.T
            else:
                dense_ref[rows, columns] = tile
            return carried

        lax.fori_loop(0, count, put, 0)

    if other_ref is None:
        put_all(own_ref, section, count_ref[section])
        return

    @pl.when(moved_ref[position] == 0)
    def _():
        put_all(own_ref, section, count_ref[section])

    @pl.when(moved_ref[position] != 0)
    def _():
        put_all(other_ref, moved_ref[position], count_ref[moved_ref[position]])


def build_dense(
    tiles, others, place, count, spot, order, moved, own_rows, group_rows, turn=False
):
    sections, slots, edge, _ = tiles.shape
    body = functools.partial(dense_kernel, own_rows // edge, group_rows // edge, turn)
    own_block = pl.BlockSpec((1, slots, edge, edge), lambda p, spot, order, *_: (order[p], 0, 0, 0))
    other_block = pl.BlockSpec(
        (1, slots + 1, edge, edge),
        lambda p, spot, order, *_: (jnp.maximum(order[p] - 1, 0), 0, 0, 0),
    )
    both = others is not None
    block = (group_rows, group_rows)
    shape = (sections * group_rows, group_rows) if turn else (group_rows, sections * group_rows)
    return pl.pallas_call(
        body,
        grid_spec=pltpu.PrefetchScalarGridSpec(
            num_scalar_prefetch=5,
            grid=(sections,),
            in_specs=[own_block, other_block] if both else [own_block],
            out_specs=pl.BlockSpec(block, lambda p, *_: (p, 0) if turn else (0, p)),
        ),
        out_shape=jax.ShapeDtypeStruct(shape, tiles.dtype),
        compiler_params=pltpu.CompilerParams(
            vmem_limit_bytes=4 * group_rows**2 + 8 * (slots + 1) * edge**2 + (2 << 20)
        ),
        cost_estimate=pl.CostEstimate(
            flops=0, bytes_accessed=4 * sections * group_rows * group_rows, transcendentals=0
        ),
        name="dense_turned" if turn else "dense",
    )(spot, order, moved, place, count, *([tiles, others] if both else [tiles]))


def on_device(
    features,
    node_ids,
    labels,
    train_mask,
    tile_values,
    tile_place,
    tile_count,
    weight_in,
    weight_out,
    class_bias,
):
    own_rows = features.shape[1]
    reps = lax.axis_size("rep")
    blks = lax.axis_size("blk")
    rep_index = lax.axis_index("rep")
    blk_index = lax.axis_index("blk")
    sections = tile_values.shape[2]
    group_rows = own_rows * reps
    hidden_width = weight_in.shape[1]
    scale = 1.0 / math.sqrt(group_rows * blks)
    f32 = jnp.float32
    bf16 = jnp.bfloat16

    def swap(value, delta):
        if delta == 0:
            return value
        return lax.ppermute(value, "rep", [(r, r ^ delta) for r in range(reps)])

    def to_section(block, j):
        pairs = []
        for r in range(reps):
            for c in range(blks):
                member = c % sections + j
                if member < sections:
                    pairs.append((r * blks + c, r * blks + c + j))
                else:
                    pairs.append((r * blks + c, (r - 1) % reps * blks + c + j - sections))
        return lax.ppermute(block, ("rep", "blk"), pairs)

    def exchange(value, delta):
        return lax.ppermute(value, "blk", [(c, c ^ delta) for c in range(blks)])

    def to_pieces(value):
        pieces = []
        for delta in range(reps):
            pairs = []
            for r in range(reps):
                for c in range(blks):
                    target = r ^ delta
                    pairs.append((r * blks + c, target * blks + (c + sections * target) % blks))
            pieces.append(lax.ppermute(value, ("rep", "blk"), pairs))
        return pieces

    def to_both(block):
        return [block] + [exchange(block, delta) for delta in range(1, sections)]

    side = lax.rem(blk_index, 2)

    def halve(value):
        half = value.shape[0] // 2
        theirs = exchange(lax.dynamic_slice_in_dim(value, (1 - side) * half, half, 0), 1)
        return lax.dynamic_slice_in_dim(value, side * half, half, 0) + theirs

    def sum_over(value, move, first, size):
        rounded = value.astype(bf16)
        parts = [rounded if d == 0 else move(rounded, d) for d in range(0, size, first)]
        parts = [part.astype(f32) for part in parts]
        while len(parts) > 1:
            parts = [parts[i] + parts[i + 1] for i in range(0, len(parts), 2)]
        return parts[0]

    def undo_digits(rows):
        count = own_rows // rows.shape[1]
        parts = [rows[i * count : (i + 1) * count].astype(jnp.int32) for i in range(3)]
        return (parts[0] + (parts[1] << 8) + (parts[2] << 16)).reshape(own_rows)

    member = lax.rem(blk_index, sections)
    place, count = tile_place[0, 0], tile_count[0, 0]
    slots, edge = tile_values.shape[3], tile_values.shape[4]
    width = features.shape[2]
    digit_rows = 3 * own_rows // width
    stride = own_rows + digit_rows + -digit_rows % 16
    anywhere = pl.BlockSpec(memory_space=pl.ANY)
    bundle, *parcels = pl.pallas_call(
        functools.partial(pack_kernel, sections),
        in_specs=[anywhere] * 5,
        out_shape=[jax.ShapeDtypeStruct((stride, width), bf16)]
        + [jax.ShapeDtypeStruct((slots + 1, edge, edge), bf16)] * (sections - 1),
        scratch_shapes=[
            pltpu.SMEM((sections,), jnp.int32),
            pltpu.VMEM((own_rows // width, width), jnp.int32),
            pltpu.VMEM((sections, slots), jnp.int32),
            pltpu.SemaphoreType.DMA((sections + 3,)),
        ],
        compiler_params=pltpu.CompilerParams(vmem_limit_bytes=60 * 1024 * 1024),
        name="pack",
    )(
        tile_count[0, 0], features[0], node_ids.reshape(-1, width), tile_place[0, 0],
        tile_values[0, 0],
    )
    arrived = to_pieces(bundle)
    for j in range(1, sections):
        pairs = []
        for r in range(reps):
            for c in range(blks):
                if c % sections < j:
                    pairs.append((r * blks + c, (r + 1) % reps * blks + c))
        parcels[j - 1] = lax.ppermute(parcels[j - 1], ("rep", "blk"), pairs)
    other_place = [parcel[slots, 0, : slots + 1].astype(jnp.int32) for parcel in parcels]
    position = jnp.arange(sections, dtype=jnp.int32)
    column = position ^ member
    order = jnp.mod(member - column, sections)
    moved = jnp.where(column > member, sections - 1 + order, 0)
    both_place = jnp.concatenate([place] + [part[None, :slots] for part in other_place], axis=0)
    both_count = jnp.concatenate([count] + [part[slots:] for part in other_place])
    tiles = tile_values[0, 0]
    where = jnp.broadcast_to(rep_index, (sections + 1,))
    next_rep = lax.rem(rep_index + 1, reps)
    first_where = jnp.where(member < jnp.arange(sections + 1) - 1, next_rep, rep_index)
    block = jnp.concatenate(arrived, axis=0)
    count, block = lax.optimization_barrier((count, block))
    dense = build_dense(
        tiles, None, place, count, first_where, position, position, own_rows, group_rows
    )
    blocks = [block] + [to_section(block, j) for j in range(1, sections)]
    pieces = [whole[d * stride : (d + 1) * stride] for whole in blocks for d in range(reps)]
    digit_sets = to_both(jnp.stack([part[own_rows:] for part in pieces[:reps]]))
    id_columns = jnp.concatenate([undo_digits(rows[d]) for rows in digit_sets for d in range(reps)])
    feature_columns = jnp.concatenate([piece[:own_rows] for piece in pieces], axis=0)
    units = jnp.arange(hidden_width, dtype=jnp.int32)
    kept = keep_mask(id_columns[:, None], units[None, :])
    chunks = dot(dense, feature_columns).reshape(reps, own_rows, width)
    layout = (
        tiles, jnp.stack(parcels), both_place, both_count, where, order, moved, own_rows, group_rows
    )
    arrived = [swap(chunks[delta], delta) for delta in range(1, reps)]
    dense, arrived = lax.optimization_barrier((build_dense(*layout), arrived))
    total = chunks[0]
    for part in arrived:
        total = total + part
    z_input = total.astype(bf16)
    arrived = to_pieces(z_input)
    z_columns = jnp.concatenate(to_both(jnp.concatenate(arrived, axis=0)), axis=0)
    kept, z_columns = lax.optimization_barrier((kept, z_columns))
    third = f32(4.0 / 3.0)
    pre_act = dot(z_columns, weight_in)
    dropped = (jnp.maximum(pre_act, 0.0) * (kept.astype(f32) * third)).astype(bf16)
    mask = jnp.where(pre_act > 0, kept, jnp.zeros_like(kept))
    second = dot(dense, dropped)
    sent = simple_call(
        encode_kernel,
        [jax.ShapeDtypeStruct((own_rows + HEAD_ROWS, hidden_width), jnp.int16)] * (reps - 1),
        "encode", second,
    )
    arrived = [swap(sent[d - 1], d) for d in range(1, reps)]
    turned, mask, second = lax.optimization_barrier(
        (build_dense(*layout, turn=True), mask, second)
    )
    classes = weight_out.shape[1]
    chunk = -(-classes // (16 * reps)) * 16
    spot = jnp.stack([side, rep_index])
    logits, out_total, *sent = simple_call(
        functools.partial(head_kernel, scale, reps),
        [
            jax.ShapeDtypeStruct((own_rows, classes), f32),
            jax.ShapeDtypeStruct((chunk, hidden_width), f32),
        ]
        + [jax.ShapeDtypeStruct((own_rows + chunk, hidden_width), bf16)] * reps,
        "head",
        weight_out, class_bias[None], labels[0][:, None], train_mask[0][:, None],
        second, *arrived,
        spot=(spot,),
        scratch=[pltpu.VMEM((chunk * reps, hidden_width), f32)],
    )
    arrived = [swap(sent[d], d) for d in range(reps)]
    grad_block = jnp.concatenate([part[:own_rows] for part in arrived], axis=0)
    for part in arrived[1:]:
        out_total = out_total + part[own_rows:].astype(f32)
    grad_block, out_total = lax.optimization_barrier((grad_block, out_total))
    back = dot(turned, grad_block)
    pre_slope = (back * (mask.astype(f32) * third)).astype(bf16)
    pre_slope, out_total = lax.optimization_barrier((pre_slope, out_total))
    in_terms = lax.dot_general(
        z_columns, pre_slope, (((0,), (0,)), ((), ())), preferred_element_type=f32
    )
    half, piece = width // 2, chunk // 2

    def halves(which):
        rows = [
            lax.dynamic_slice_in_dim(in_terms, which * half, half, 0),
            lax.dynamic_slice_in_dim(out_total, which * piece, piece, 0),
        ]
        return jnp.concatenate(rows, axis=0)

    total = halves(side) + exchange(halves(1 - side), 1)
    total = sum_over(total, exchange, 2, blks).astype(bf16)
    arrived = [swap(total, d) for d in range(reps)]
    parts = [part[:half].astype(f32) for part in arrived]
    while len(parts) > 1:
        parts = [parts[i] + parts[i + 1] for i in range(0, len(parts), 2)]
    total = jnp.concatenate(parts + [part[half:].astype(f32) for part in arrived], axis=0)
    grad_in, grad_wide = simple_call(
        functools.partial(last_kernel, chunk),
        [
            jax.ShapeDtypeStruct((width, hidden_width), f32),
            jax.ShapeDtypeStruct((classes, hidden_width), f32),
        ],
        "last", total, exchange(total, 1), spot=(spot,),
    )
    grad_out = grad_wide.T
    return (logits[None], grad_in, grad_out)


def solution(mesh):
    placed = (
        P("blk", "rep", None),
        P("blk", "rep"),
        P("blk", "rep"),
        P("blk", "rep"),
        P("blk", "rep", None, None, None, None),
        P("blk", "rep", None, None),
        P("blk", "rep", None),
        P(),
        P(),
        P(),
    )
    return jax.shard_map(
        on_device,
        mesh=mesh,
        in_specs=placed,
        out_specs=(P("blk", "rep", None), P(), P()),
        check_vma=False,
    )
```

```python
import functools
import math

import jax
import jax.numpy as jnp
from jax import lax
from jax.experimental import pallas as pl
from jax.experimental.pallas import tpu as pltpu
from jax.sharding import PartitionSpec as P


LEVELS = 32767.0
MANTISSA_BITS = 14
HEAD_ROWS = 16


def keep_mask(id_values, unit_values):
    mixed = id_values * 73244475 + unit_values * 19349663 + 12345
    mixed = mixed ^ jnp.right_shift(mixed, 15)
    mixed = mixed * 40503
    mixed = mixed ^ jnp.right_shift(mixed, 13)
    return (jnp.bitwise_and(mixed, 3) != 0).astype(jnp.bfloat16)


def eye_of(count):
    rows = lax.broadcasted_iota(jnp.int32, (count, count), 0)
    columns = lax.broadcasted_iota(jnp.int32, (count, count), 1)
    return rows == columns


def dot(left, right):
    return jnp.dot(left, right, preferred_element_type=jnp.float32)


def dot_wide(left, right):
    return lax.dot_general(
        left, right, (((1,), (1,)), ((), ())), preferred_element_type=jnp.float32
    )


def encode(values):
    rows, width = values.shape
    largest = jnp.maximum(jnp.max(jnp.abs(values), axis=1, keepdims=True), 1e-30)
    power = jnp.ceil(jnp.log2(largest))
    mantissa = jnp.ceil(largest * jnp.exp2(MANTISSA_BITS - power))
    scale = mantissa * jnp.exp2(power - MANTISSA_BITS)
    coded = jnp.clip(jnp.round(values * (LEVELS / scale)), -LEVELS, LEVELS)
    square = eye_of(width)
    index = lax.broadcasted_iota(jnp.int32, (HEAD_ROWS, width), 0)
    head = jnp.zeros((HEAD_ROWS, width), jnp.float32)
    for part in range(rows // width):
        for offset, column in enumerate((power, mantissa)):
            column = column[part * width : (part + 1) * width]
            line = jnp.sum(jnp.where(square, column, 0.0), axis=0, keepdims=True)
            head = jnp.where(index == 2 * part + offset, line, head)
    whole = jnp.concatenate([coded, head], axis=0)
    return whole.astype(jnp.int32).astype(jnp.int16)


def decode(coded):
    whole = coded.astype(jnp.int32).astype(jnp.float32)
    rows, width = whole.shape[0] - HEAD_ROWS, whole.shape[1]
    square = eye_of(width)
    columns = [[], []]
    for part in range(rows // width):
        for offset in range(2):
            start = rows + 2 * part + offset
            line = whole[start : start + 1]
            columns[offset].append(jnp.sum(jnp.where(square, line, 0.0), axis=1, keepdims=True))
    power, mantissa = (jnp.concatenate(parts, axis=0) for parts in columns)
    return whole[:rows] * (mantissa * jnp.exp2(power - MANTISSA_BITS) * (1.0 / LEVELS))


def encode_kernel(partial_ref, *coded_refs):
    own_rows = partial_ref.shape[0] // (len(coded_refs) + 1)
    for delta, coded_ref in enumerate(coded_refs, 1):
        coded_ref[...] = encode(partial_ref[delta * own_rows : (delta + 1) * own_rows, :])


def pack_kernel(feature_hbm, id_hbm, bundle_ref, id_ref, sems):
    own_rows, lanes = feature_hbm.shape
    small = pltpu.make_async_copy(id_hbm, id_ref, sems.at[0])
    large = pltpu.make_async_copy(feature_hbm, bundle_ref.at[pl.ds(0, own_rows)], sems.at[1])
    small.start()
    large.start()
    small.wait()
    ids = id_ref[...]
    rows = ids.shape[0]
    parts = [ids & 255, jnp.right_shift(ids, 8) & 255, jnp.right_shift(ids, 16)]
    pad = bundle_ref.shape[0] - own_rows - 3 * rows
    parts += [jnp.zeros((pad, lanes), jnp.int32)] if pad else []
    digit_rows = jnp.concatenate(parts, axis=0).astype(jnp.float32).astype(jnp.bfloat16)
    bundle_ref[own_rows:, :] = digit_rows
    large.wait()


def last_kernel(chunk, spot_ref, total_ref, other_ref, grad_in_ref, grad_out_ref):
    side, rep_index = spot_ref[0], spot_ref[1]
    half = grad_in_ref.shape[0] // 2
    piece = chunk // 2
    classes = grad_out_ref.shape[0]
    reps = (total_ref.shape[0] - half) // piece
    for part in range(2):

        def take(start, size):
            rows = pl.ds(start, size)
            return jnp.where(side == part, total_ref[rows, :], other_ref[rows, :])

        grad_in_ref[part * half : (part + 1) * half, :] = take(0, half)
        for r in range(reps):
            start = r * chunk + part * piece
            size = min(piece, classes - start)
            if size > 0:
                spot = pl.multiple_of(half + (r ^ rep_index) * piece, 8)
                grad_out_ref[start : start + size, :] = take(spot, piece)[:size]


def head_kernel(
    scale, reps, spot_ref, weight_ref, bias_ref, label_ref, mask_ref, own_ref, *refs
):
    coded_refs, refs = refs[: reps - 1], refs[reps - 1 :]
    logits_ref, own_terms_ref, sent_refs, terms_ref = refs[0], refs[1], refs[2:-1], refs[-1]
    own_rows, classes = logits_ref.shape
    total = own_ref[:own_rows, :]
    for coded_ref in coded_refs:
        total += decode(coded_ref[...])
    z_output = total.astype(jnp.bfloat16)
    logits = dot(z_output, weight_ref[...]) + bias_ref[...]
    logits_ref[...] = logits
    shifted = jnp.exp(logits - jnp.max(logits, axis=1, keepdims=True))
    likelihood = shifted / jnp.sum(shifted, axis=1, keepdims=True)
    onehot = label_ref[...] == lax.broadcasted_iota(jnp.int32, logits.shape, 1)
    slope = (likelihood - onehot.astype(jnp.float32)) * mask_ref[...].astype(jnp.float32) * scale
    slope = slope.astype(jnp.bfloat16)
    grad_rows = dot_wide(slope, weight_ref[...]).astype(jnp.bfloat16)
    terms = lax.dot_general(
        slope, z_output, (((0,), (0,)), ((), ())), preferred_element_type=jnp.float32
    )
    terms_ref[:classes, :] = terms
    pad = terms_ref.shape[0] - classes
    if pad:
        terms_ref[classes:, :] = jnp.zeros((pad, terms.shape[1]), jnp.float32)
    chunk = own_terms_ref.shape[0]
    for delta, sent_ref in enumerate(sent_refs):
        start = pl.multiple_of((spot_ref[1] ^ delta) * chunk, 8)
        piece = terms_ref[pl.ds(start, chunk), :]
        sent_ref[:own_rows, :] = grad_rows
        sent_ref[own_rows:, :] = piece.astype(jnp.bfloat16)
        if delta == 0:
            own_terms_ref[...] = piece


def simple_call(body, shapes, name, *values, spot=(), scratch=()):
    smem = pl.BlockSpec(memory_space=pltpu.SMEM)
    vmem = pl.BlockSpec(memory_space=pltpu.VMEM)
    return pl.pallas_call(
        body,
        in_specs=[smem] * len(spot) + [vmem] * len(values),
        out_shape=shapes,
        scratch_shapes=scratch,
        compiler_params=pltpu.CompilerParams(vmem_limit_bytes=8 * 1024 * 1024),
        name=name,
    )(*spot, *values)


def dense_kernel(
    per_rep, tile_side, turn, spot_ref, place_ref, count_ref, tiles_ref, dense_ref
):
    section = pl.program_id(0)
    rep_index, source_rep = spot_ref[0], spot_ref[1 + section]
    edge = tiles_ref.shape[-1]
    dense_ref[...] = jnp.zeros_like(dense_ref)

    def put(slot, carried):
        place = place_ref[section, slot]
        row = place // tile_side
        column = place % tile_side
        row = ((row // per_rep) ^ rep_index) * per_rep + row % per_rep
        column = ((column // per_rep) ^ source_rep) * per_rep + column % per_rep
        rows = pl.ds(pl.multiple_of(row * edge, edge), edge)
        columns = pl.ds(pl.multiple_of(column * edge, edge), edge)
        tile = tiles_ref[0, slot]
        if turn:
            dense_ref[columns, rows] = tile.T
        else:
            dense_ref[rows, columns] = tile
        return carried

    lax.fori_loop(0, count_ref[section], put, 0)


def build_dense(tiles, place, count, spot, own_rows, group_rows, turn):
    sections, slots, edge, _ = tiles.shape
    body = functools.partial(dense_kernel, own_rows // edge, group_rows // edge, turn)
    block = (group_rows, group_rows)
    shape = (sections * group_rows, group_rows) if turn else (group_rows, sections * group_rows)
    return pl.pallas_call(
        body,
        grid_spec=pltpu.PrefetchScalarGridSpec(
            num_scalar_prefetch=3,
            grid=(sections,),
            in_specs=[pl.BlockSpec((1, slots, edge, edge), lambda p, *_: (p, 0, 0, 0))],
            out_specs=pl.BlockSpec(block, lambda p, *_: (p, 0) if turn else (0, p)),
        ),
        out_shape=jax.ShapeDtypeStruct(shape, tiles.dtype),
        compiler_params=pltpu.CompilerParams(
            vmem_limit_bytes=4 * group_rows**2 + 8 * slots * edge**2 + (2 << 20)
        ),
        cost_estimate=pl.CostEstimate(
            flops=0, bytes_accessed=4 * sections * group_rows * group_rows, transcendentals=0
        ),
        name="dense_turned" if turn else "dense",
    )(spot, place, count, tiles)


def on_device(
    features,
    node_ids,
    labels,
    train_mask,
    tile_values,
    tile_place,
    tile_count,
    weight_in,
    weight_out,
    class_bias,
):
    own_rows = features.shape[1]
    reps = lax.axis_size("rep")
    blks = lax.axis_size("blk")
    rep_index = lax.axis_index("rep")
    blk_index = lax.axis_index("blk")
    sections = tile_values.shape[2]
    group_rows = own_rows * reps
    hidden_width = weight_in.shape[1]
    scale = 1.0 / math.sqrt(group_rows * blks)
    f32 = jnp.float32
    bf16 = jnp.bfloat16

    def swap(value, delta):
        if delta == 0:
            return value
        return lax.ppermute(value, "rep", [(r, r ^ delta) for r in range(reps)])

    def to_section(block, j):
        pairs = []
        for r in range(reps):
            for c in range(blks):
                member = c % sections + j
                if member < sections:
                    pairs.append((r * blks + c, r * blks + c + j))
                else:
                    pairs.append((r * blks + c, (r - 1) % reps * blks + c + j - sections))
        return lax.ppermute(block, ("rep", "blk"), pairs)

    def exchange(value, delta):
        return lax.ppermute(value, "blk", [(c, c ^ delta) for c in range(blks)])

    def to_pieces(value):
        pieces = []
        for delta in range(reps):
            pairs = []
            for r in range(reps):
                for c in range(blks):
                    target = r ^ delta
                    pairs.append((r * blks + c, target * blks + (c + sections * target) % blks))
            pieces.append(lax.ppermute(value, ("rep", "blk"), pairs))
        return pieces

    def to_all(pieces):
        cut = reps // 2
        halves = [jnp.concatenate(pieces[:cut], axis=0), jnp.concatenate(pieces[cut:], axis=0)]
        blocks = list(halves)
        for j in range(1, sections):
            blocks += [to_section(half, j) for half in halves]
        return blocks

    side = lax.rem(blk_index, 2)

    def halve(value):
        half = value.shape[0] // 2
        theirs = exchange(lax.dynamic_slice_in_dim(value, (1 - side) * half, half, 0), 1)
        return lax.dynamic_slice_in_dim(value, side * half, half, 0) + theirs

    def sum_over(value, move, first, size):
        rounded = value.astype(bf16)
        parts = [rounded if d == 0 else move(rounded, d) for d in range(0, size, first)]
        parts = [part.astype(f32) for part in parts]
        while len(parts) > 1:
            parts = [parts[i] + parts[i + 1] for i in range(0, len(parts), 2)]
        return parts[0]

    def undo_digits(rows):
        count = own_rows // rows.shape[1]
        parts = [rows[i * count : (i + 1) * count].astype(jnp.int32) for i in range(3)]
        return (parts[0] + (parts[1] << 8) + (parts[2] << 16)).reshape(own_rows)

    member = lax.rem(blk_index, sections)
    place, count = tile_place[0, 0], tile_count[0, 0]
    width = features.shape[2]
    digit_rows = 3 * own_rows // width
    stride = own_rows + digit_rows + -digit_rows % 16
    anywhere = pl.BlockSpec(memory_space=pl.ANY)
    bundle = pl.pallas_call(
        pack_kernel,
        in_specs=[anywhere] * 2,
        out_shape=jax.ShapeDtypeStruct((stride, width), bf16),
        scratch_shapes=[
            pltpu.VMEM((own_rows // width, width), jnp.int32),
            pltpu.SemaphoreType.DMA((2,)),
        ],
        compiler_params=pltpu.CompilerParams(vmem_limit_bytes=60 * 1024 * 1024),
        name="pack",
    )(features[0], node_ids.reshape(-1, width))
    arrived = to_pieces(bundle)
    next_rep = lax.rem(rep_index + 1, reps)
    where = jnp.where(member < jnp.arange(sections + 1) - 1, next_rep, rep_index)
    layout = (where, own_rows, group_rows)
    count, arrived[0] = lax.optimization_barrier((count, arrived[0]))
    dense = build_dense(tile_values[0, 0], place, count, *layout, False)
    pieces = [
        half[d * stride : (d + 1) * stride] for half in to_all(arrived) for d in range(reps // 2)
    ]
    id_columns = jnp.concatenate([undo_digits(piece[own_rows:]) for piece in pieces])
    feature_columns = jnp.concatenate([piece[:own_rows] for piece in pieces], axis=0)
    units = jnp.arange(hidden_width, dtype=jnp.int32)
    kept = keep_mask(id_columns[:, None], units[None, :])
    chunks = dot(dense, feature_columns).reshape(reps, own_rows, width)
    arrived = [swap(chunks[delta], delta) for delta in range(1, reps)]
    total = chunks[0]
    for part in arrived:
        total = total + part
    z_input = total.astype(bf16)
    z_columns = jnp.concatenate(to_all(to_pieces(z_input)), axis=0)
    kept, z_columns = lax.optimization_barrier((kept, z_columns))
    third = f32(4.0 / 3.0)
    pre_act = dot(z_columns, weight_in)
    dropped = (jnp.maximum(pre_act, 0.0) * (kept.astype(f32) * third)).astype(bf16)
    second = dot(dense, dropped)
    sent = simple_call(
        encode_kernel,
        [jax.ShapeDtypeStruct((own_rows + HEAD_ROWS, hidden_width), jnp.int16)] * (reps - 1),
        "encode", second,
    )
    arrived = [swap(sent[d - 1], d) for d in range(1, reps)]
    classes = weight_out.shape[1]
    chunk = -(-classes // (16 * reps)) * 16
    spot = jnp.stack([side, rep_index])
    logits, out_total, *sent = simple_call(
        functools.partial(head_kernel, scale, reps),
        [
            jax.ShapeDtypeStruct((own_rows, classes), f32),
            jax.ShapeDtypeStruct((chunk, hidden_width), f32),
        ]
        + [jax.ShapeDtypeStruct((own_rows + chunk, hidden_width), bf16)] * reps,
        "head",
        weight_out, class_bias[None], labels[0][:, None], train_mask[0][:, None],
        second, *arrived,
        spot=(spot,),
        scratch=[pltpu.VMEM((chunk * reps, hidden_width), f32)],
    )
    arrived = [swap(sent[d], d) for d in range(reps)]
    count, z_again, kept, out_total = lax.optimization_barrier((count, z_columns, kept, out_total))
    turned = build_dense(tile_values[0, 0], place, count, *layout, True)
    mask = jnp.where(dot(z_again, weight_in) > 0, kept, jnp.zeros_like(kept))
    grad_block = jnp.concatenate([part[:own_rows] for part in arrived], axis=0)
    for part in arrived[1:]:
        out_total = out_total + part[own_rows:].astype(f32)
    grad_block, mask, out_total = lax.optimization_barrier((grad_block, mask, out_total))
    back = dot(turned, grad_block)
    pre_slope = (back * (mask.astype(f32) * third)).astype(bf16)
    pre_slope, out_total = lax.optimization_barrier((pre_slope, out_total))
    in_terms = lax.dot_general(
        z_columns, pre_slope, (((0,), (0,)), ((), ())), preferred_element_type=f32
    )
    half, piece = width // 2, chunk // 2

    def halves(which):
        rows = [
            lax.dynamic_slice_in_dim(in_terms, which * half, half, 0),
            lax.dynamic_slice_in_dim(out_total, which * piece, piece, 0),
        ]
        return jnp.concatenate(rows, axis=0)

    total = halves(side) + exchange(halves(1 - side), 1)
    total = sum_over(total, exchange, 2, blks).astype(bf16)
    arrived = [swap(total, d) for d in range(reps)]
    parts = [part[:half].astype(f32) for part in arrived]
    while len(parts) > 1:
        parts = [parts[i] + parts[i + 1] for i in range(0, len(parts), 2)]
    total = jnp.concatenate(parts + [part[half:].astype(f32) for part in arrived], axis=0)
    grad_in, grad_wide = simple_call(
        functools.partial(last_kernel, chunk),
        [
            jax.ShapeDtypeStruct((width, hidden_width), f32),
            jax.ShapeDtypeStruct((classes, hidden_width), f32),
        ],
        "last", total, exchange(total, 1), spot=(spot,),
    )
    grad_out = grad_wide.T
    return (logits[None], grad_in, grad_out)


def solution(mesh):
    placed = (
        P("blk", "rep", None),
        P("blk", "rep"),
        P("blk", "rep"),
        P("blk", "rep"),
        P("blk", "rep", None, None, None, None),
        P("blk", "rep", None, None),
        P("blk", "rep", None),
        P(),
        P(),
        P(),
    )
    return jax.shard_map(
        on_device,
        mesh=mesh,
        in_specs=placed,
        out_specs=(P("blk", "rep", None), P(), P()),
        check_vma=False,
    )
```

```python
import functools
import math

import jax
import jax.numpy as jnp
from jax import lax
from jax.experimental import pallas as pl
from jax.experimental.pallas import tpu as pltpu
from jax.sharding import PartitionSpec as P


LEVELS = 32767.0
MANTISSA_BITS = 14
HEAD_ROWS = 16


def keep_mask(id_values, unit_values):
    mixed = id_values * 73244475 + unit_values * 19349663 + 12345
    mixed = mixed ^ jnp.right_shift(mixed, 15)
    mixed = mixed * 40503
    mixed = mixed ^ jnp.right_shift(mixed, 13)
    return (jnp.bitwise_and(mixed, 3) != 0).astype(jnp.bfloat16)


def eye_of(count):
    rows = lax.broadcasted_iota(jnp.int32, (count, count), 0)
    columns = lax.broadcasted_iota(jnp.int32, (count, count), 1)
    return rows == columns


def dot(left, right):
    return jnp.dot(left, right, preferred_element_type=jnp.float32)


def dot_wide(left, right):
    return lax.dot_general(
        left, right, (((1,), (1,)), ((), ())), preferred_element_type=jnp.float32
    )


def encode(values):
    rows, width = values.shape
    largest = jnp.maximum(jnp.max(jnp.abs(values), axis=1, keepdims=True), 1e-30)
    power = jnp.ceil(jnp.log2(largest))
    mantissa = jnp.ceil(largest * jnp.exp2(MANTISSA_BITS - power))
    scale = mantissa * jnp.exp2(power - MANTISSA_BITS)
    coded = jnp.clip(jnp.round(values * (LEVELS / scale)), -LEVELS, LEVELS)
    square = eye_of(width)
    index = lax.broadcasted_iota(jnp.int32, (HEAD_ROWS, width), 0)
    head = jnp.zeros((HEAD_ROWS, width), jnp.float32)
    for part in range(rows // width):
        for offset, column in enumerate((power, mantissa)):
            column = column[part * width : (part + 1) * width]
            line = jnp.sum(jnp.where(square, column, 0.0), axis=0, keepdims=True)
            head = jnp.where(index == 2 * part + offset, line, head)
    whole = jnp.concatenate([coded, head], axis=0)
    return whole.astype(jnp.int32).astype(jnp.int16)


def decode(coded):
    whole = coded.astype(jnp.int32).astype(jnp.float32)
    rows, width = whole.shape[0] - HEAD_ROWS, whole.shape[1]
    square = eye_of(width)
    columns = [[], []]
    for part in range(rows // width):
        for offset in range(2):
            start = rows + 2 * part + offset
            line = whole[start : start + 1]
            columns[offset].append(jnp.sum(jnp.where(square, line, 0.0), axis=1, keepdims=True))
    power, mantissa = (jnp.concatenate(parts, axis=0) for parts in columns)
    return whole[:rows] * (mantissa * jnp.exp2(power - MANTISSA_BITS) * (1.0 / LEVELS))


def encode_kernel(partial_ref, *coded_refs):
    own_rows = partial_ref.shape[0] // (len(coded_refs) + 1)
    for delta, coded_ref in enumerate(coded_refs, 1):
        coded_ref[...] = encode(partial_ref[delta * own_rows : (delta + 1) * own_rows, :])


def last_kernel(chunk, spot_ref, total_ref, other_ref, grad_in_ref, grad_out_ref):
    side, rep_index = spot_ref[0], spot_ref[1]
    half = grad_in_ref.shape[0] // 2
    piece = chunk // 2
    classes = grad_out_ref.shape[0]
    reps = (total_ref.shape[0] - half) // piece
    for part in range(2):

        def take(start, size):
            rows = pl.ds(start, size)
            return jnp.where(side == part, total_ref[rows, :], other_ref[rows, :])

        grad_in_ref[part * half : (part + 1) * half, :] = take(0, half)
        for r in range(reps):
            start = r * chunk + part * piece
            size = min(piece, classes - start)
            if size > 0:
                spot = pl.multiple_of(half + (r ^ rep_index) * piece, 8)
                grad_out_ref[start : start + size, :] = take(spot, piece)[:size]


def head_kernel(
    scale, reps, spot_ref, weight_ref, bias_ref, label_ref, mask_ref, own_ref, *refs
):
    coded_refs, refs = refs[: reps - 1], refs[reps - 1 :]
    logits_ref, own_terms_ref, sent_refs, terms_ref = refs[0], refs[1], refs[2:-1], refs[-1]
    own_rows, classes = logits_ref.shape
    total = own_ref[:own_rows, :]
    for coded_ref in coded_refs:
        total += decode(coded_ref[...])
    z_output = total.astype(jnp.bfloat16)
    logits = dot(z_output, weight_ref[...]) + bias_ref[...]
    logits_ref[...] = logits
    shifted = jnp.exp(logits - jnp.max(logits, axis=1, keepdims=True))
    likelihood = shifted / jnp.sum(shifted, axis=1, keepdims=True)
    onehot = label_ref[...] == lax.broadcasted_iota(jnp.int32, logits.shape, 1)
    slope = (likelihood - onehot.astype(jnp.float32)) * mask_ref[...].astype(jnp.float32) * scale
    slope = slope.astype(jnp.bfloat16)
    grad_rows = dot_wide(slope, weight_ref[...]).astype(jnp.bfloat16)
    terms = lax.dot_general(
        slope, z_output, (((0,), (0,)), ((), ())), preferred_element_type=jnp.float32
    )
    terms_ref[:classes, :] = terms
    pad = terms_ref.shape[0] - classes
    if pad:
        terms_ref[classes:, :] = jnp.zeros((pad, terms.shape[1]), jnp.float32)
    chunk = own_terms_ref.shape[0]
    for delta, sent_ref in enumerate(sent_refs):
        start = pl.multiple_of((spot_ref[1] ^ delta) * chunk, 8)
        piece = terms_ref[pl.ds(start, chunk), :]
        sent_ref[:own_rows, :] = grad_rows
        sent_ref[own_rows:, :] = piece.astype(jnp.bfloat16)
        if delta == 0:
            own_terms_ref[...] = piece


def simple_call(body, shapes, name, *values, spot=(), scratch=()):
    smem = pl.BlockSpec(memory_space=pltpu.SMEM)
    vmem = pl.BlockSpec(memory_space=pltpu.VMEM)
    return pl.pallas_call(
        body,
        in_specs=[smem] * len(spot) + [vmem] * len(values),
        out_shape=shapes,
        scratch_shapes=scratch,
        compiler_params=pltpu.CompilerParams(vmem_limit_bytes=8 * 1024 * 1024),
        name=name,
    )(*spot, *values)


def put_tiles(own_rows, turn, section, spot_ref, place_ref, count_ref, tiles_ref, dense_ref):
    edge = tiles_ref.shape[-1]
    per_rep = own_rows // edge
    tile_side = dense_ref.shape[0] // edge
    rep_index, source_rep = spot_ref[0], spot_ref[1 + section]

    def put(slot, carried):
        place = place_ref[section, slot]
        row = place // tile_side
        column = place % tile_side
        row = ((row // per_rep) ^ rep_index) * per_rep + row % per_rep
        column = ((column // per_rep) ^ source_rep) * per_rep + column % per_rep
        rows = pl.ds(pl.multiple_of(row * edge, edge), edge)
        columns = pl.ds(pl.multiple_of(column * edge, edge), edge)
        if turn:
            dense_ref[columns, rows] = tiles_ref[slot].T
        else:
            dense_ref[rows, columns] = tiles_ref[slot]
        return carried

    lax.fori_loop(0, count_ref[section], put, 0)


def turned_kernel(own_rows, spot_ref, place_ref, count_ref, tiles_ref, dense_ref):
    dense_ref[...] = jnp.zeros_like(dense_ref)
    put_tiles(
        own_rows, True, pl.program_id(0), spot_ref, place_ref, count_ref, tiles_ref.at[0], dense_ref
    )


def build_turned(tiles, place, count, spot, own_rows, group_rows):
    sections, slots, edge, _ = tiles.shape
    return pl.pallas_call(
        functools.partial(turned_kernel, own_rows),
        grid_spec=pltpu.PrefetchScalarGridSpec(
            num_scalar_prefetch=3,
            grid=(sections,),
            in_specs=[pl.BlockSpec((1, slots, edge, edge), lambda p, *_: (p, 0, 0, 0))],
            out_specs=pl.BlockSpec((group_rows, group_rows), lambda p, *_: (p, 0)),
        ),
        out_shape=jax.ShapeDtypeStruct((sections * group_rows, group_rows), tiles.dtype),
        compiler_params=pltpu.CompilerParams(
            vmem_limit_bytes=4 * group_rows**2 + 8 * slots * edge**2 + (2 << 20)
        ),
        name="dense_turned",
    )(spot, place, count, tiles)


def pack_kernel(
    spot_ref, feature_hbm, id_hbm, place_hbm, count_hbm, tiles_hbm, bundle_ref, dense_hbm,
    id_ref, place_ref, count_ref, tiles_ref, dense_ref, sems,
):
    own_rows, lanes = feature_hbm.shape
    sections = tiles_hbm.shape[0]
    group_rows = dense_hbm.shape[0]
    ids_in = pltpu.make_async_copy(id_hbm, id_ref, sems.at[0])
    features_in = pltpu.make_async_copy(
        feature_hbm, bundle_ref.at[pl.ds(0, own_rows)], sems.at[1]
    )
    place_in = pltpu.make_async_copy(place_hbm, place_ref, sems.at[2])
    count_in = pltpu.make_async_copy(count_hbm, count_ref, sems.at[3])
    tiles_in = [
        pltpu.make_async_copy(tiles_hbm.at[j], tiles_ref.at[j], sems.at[4 + j])
        for j in range(sections)
    ]
    for copy in [ids_in, features_in, place_in, count_in] + tiles_in:
        copy.start()
    dense_ref[...] = jnp.zeros_like(dense_ref)
    ids_in.wait()
    ids = id_ref[...]
    rows = ids.shape[0]
    parts = [ids & 255, jnp.right_shift(ids, 8) & 255, jnp.right_shift(ids, 16)]
    pad = bundle_ref.shape[0] - own_rows - 3 * rows
    parts += [jnp.zeros((pad, lanes), jnp.int32)] if pad else []
    digit_rows = jnp.concatenate(parts, axis=0).astype(jnp.float32).astype(jnp.bfloat16)
    bundle_ref[own_rows:, :] = digit_rows
    place_in.wait()
    count_in.wait()
    out = []
    for j in range(sections):
        tiles_in[j].wait()
        part = dense_ref.at[:, pl.ds(j * group_rows, group_rows)]
        put_tiles(own_rows, False, j, spot_ref, place_ref, count_ref, tiles_ref.at[j], part)
        copy = pltpu.make_async_copy(
            part, dense_hbm.at[:, pl.ds(j * group_rows, group_rows)], sems.at[4 + sections + j]
        )
        copy.start()
        out.append(copy)
    features_in.wait()
    for copy in out:
        copy.wait()


def on_device(
    features,
    node_ids,
    labels,
    train_mask,
    tile_values,
    tile_place,
    tile_count,
    weight_in,
    weight_out,
    class_bias,
):
    own_rows = features.shape[1]
    reps = lax.axis_size("rep")
    blks = lax.axis_size("blk")
    rep_index = lax.axis_index("rep")
    blk_index = lax.axis_index("blk")
    sections = tile_values.shape[2]
    group_rows = own_rows * reps
    hidden_width = weight_in.shape[1]
    scale = 1.0 / math.sqrt(group_rows * blks)
    f32 = jnp.float32
    bf16 = jnp.bfloat16

    def swap(value, delta):
        if delta == 0:
            return value
        return lax.ppermute(value, "rep", [(r, r ^ delta) for r in range(reps)])

    def to_section(block, j):
        pairs = []
        for r in range(reps):
            for c in range(blks):
                member = c % sections + j
                if member < sections:
                    pairs.append((r * blks + c, r * blks + c + j))
                else:
                    pairs.append((r * blks + c, (r - 1) % reps * blks + c + j - sections))
        return lax.ppermute(block, ("rep", "blk"), pairs)

    def exchange(value, delta):
        return lax.ppermute(value, "blk", [(c, c ^ delta) for c in range(blks)])

    def to_pieces(value):
        pieces = []
        for delta in range(reps):
            pairs = []
            for r in range(reps):
                for c in range(blks):
                    target = r ^ delta
                    pairs.append((r * blks + c, target * blks + (c + sections * target) % blks))
            pieces.append(lax.ppermute(value, ("rep", "blk"), pairs))
        return pieces

    def to_all(pieces):
        cut = reps // 2
        halves = [jnp.concatenate(pieces[:cut], axis=0), jnp.concatenate(pieces[cut:], axis=0)]
        blocks = list(halves)
        for j in range(1, sections):
            blocks += [to_section(half, j) for half in halves]
        return blocks

    side = lax.rem(blk_index, 2)

    def halve(value):
        half = value.shape[0] // 2
        theirs = exchange(lax.dynamic_slice_in_dim(value, (1 - side) * half, half, 0), 1)
        return lax.dynamic_slice_in_dim(value, side * half, half, 0) + theirs

    def sum_over(value, move, first, size):
        rounded = value.astype(bf16)
        parts = [rounded if d == 0 else move(rounded, d) for d in range(0, size, first)]
        parts = [part.astype(f32) for part in parts]
        while len(parts) > 1:
            parts = [parts[i] + parts[i + 1] for i in range(0, len(parts), 2)]
        return parts[0]

    def undo_digits(rows):
        count = own_rows // rows.shape[1]
        parts = [rows[i * count : (i + 1) * count].astype(jnp.int32) for i in range(3)]
        return (parts[0] + (parts[1] << 8) + (parts[2] << 16)).reshape(own_rows)

    member = lax.rem(blk_index, sections)
    place, count = tile_place[0, 0], tile_count[0, 0]
    width = features.shape[2]
    digit_rows = 3 * own_rows // width
    stride = own_rows + digit_rows + -digit_rows % 16
    tiles = tile_values[0, 0]
    next_rep = lax.rem(rep_index + 1, reps)
    where = jnp.where(member < jnp.arange(sections + 1) - 1, next_rep, rep_index)
    anywhere = pl.BlockSpec(memory_space=pl.ANY)
    bundle, dense = pl.pallas_call(
        pack_kernel,
        in_specs=[pl.BlockSpec(memory_space=pltpu.SMEM)] + [anywhere] * 5,
        out_specs=[pl.BlockSpec(memory_space=pltpu.VMEM), anywhere],
        out_shape=[
            jax.ShapeDtypeStruct((stride, width), bf16),
            jax.ShapeDtypeStruct((group_rows, sections * group_rows), bf16),
        ],
        scratch_shapes=[
            pltpu.VMEM((own_rows // width, width), jnp.int32),
            pltpu.SMEM(place.shape, jnp.int32),
            pltpu.SMEM(count.shape, jnp.int32),
            pltpu.VMEM(tiles.shape, bf16),
            pltpu.VMEM((group_rows, sections * group_rows), bf16),
            pltpu.SemaphoreType.DMA((4 + 2 * sections,)),
        ],
        compiler_params=pltpu.CompilerParams(vmem_limit_bytes=60 * 1024 * 1024),
        name="pack",
    )(where, features[0], node_ids.reshape(-1, width), place, count, tiles)
    arrived = to_pieces(bundle)
    pieces = [
        half[d * stride : (d + 1) * stride] for half in to_all(arrived) for d in range(reps // 2)
    ]
    id_columns = jnp.concatenate([undo_digits(piece[own_rows:]) for piece in pieces])
    feature_columns = jnp.concatenate([piece[:own_rows] for piece in pieces], axis=0)
    units = jnp.arange(hidden_width, dtype=jnp.int32)
    kept = keep_mask(id_columns[:, None], units[None, :])
    chunks = dot(dense, feature_columns).reshape(reps, own_rows, width)
    arrived = [swap(chunks[delta], delta) for delta in range(1, reps)]
    total = chunks[0]
    for part in arrived:
        total = total + part
    z_input = total.astype(bf16)
    z_columns = jnp.concatenate(to_all(to_pieces(z_input)), axis=0)
    kept, z_columns = lax.optimization_barrier((kept, z_columns))
    third = f32(4.0 / 3.0)
    pre_act = dot(z_columns, weight_in)
    dropped = (jnp.maximum(pre_act, 0.0) * (kept.astype(f32) * third)).astype(bf16)
    dropped, z_again = lax.optimization_barrier((dropped, z_columns))
    second = dot(dense, dropped)
    mask = jnp.where(dot(z_again, weight_in) > 0, kept, jnp.zeros_like(kept))
    mask, ready = lax.optimization_barrier((mask, second))
    sent = simple_call(
        encode_kernel,
        [jax.ShapeDtypeStruct((own_rows + HEAD_ROWS, hidden_width), jnp.int16)] * (reps - 1),
        "encode", second,
    )
    arrived = [swap(sent[d - 1], d) for d in range(1, reps)]
    classes = weight_out.shape[1]
    chunk = -(-classes // (16 * reps)) * 16
    spot = jnp.stack([side, rep_index])
    logits, out_total, *sent = simple_call(
        functools.partial(head_kernel, scale, reps),
        [
            jax.ShapeDtypeStruct((own_rows, classes), f32),
            jax.ShapeDtypeStruct((chunk, hidden_width), f32),
        ]
        + [jax.ShapeDtypeStruct((own_rows + chunk, hidden_width), bf16)] * reps,
        "head",
        weight_out, class_bias[None], labels[0][:, None], train_mask[0][:, None],
        ready, *arrived,
        spot=(spot,),
        scratch=[pltpu.VMEM((chunk * reps, hidden_width), f32)],
    )
    arrived = [swap(sent[d], d) for d in range(reps)]
    count, out_total = lax.optimization_barrier((count, out_total))
    turned = build_turned(tiles, place, count, where, own_rows, group_rows)
    grad_block = jnp.concatenate([part[:own_rows] for part in arrived], axis=0)
    for part in arrived[1:]:
        out_total = out_total + part[own_rows:].astype(f32)
    grad_block, mask, out_total = lax.optimization_barrier((grad_block, mask, out_total))
    back = dot(turned, grad_block)
    pre_slope = (back * (mask.astype(f32) * third)).astype(bf16)
    pre_slope, out_total = lax.optimization_barrier((pre_slope, out_total))
    in_terms = lax.dot_general(
        z_columns, pre_slope, (((0,), (0,)), ((), ())), preferred_element_type=f32
    )
    half, piece = width // 2, chunk // 2

    def halves(which):
        rows = [
            lax.dynamic_slice_in_dim(in_terms, which * half, half, 0),
            lax.dynamic_slice_in_dim(out_total, which * piece, piece, 0),
        ]
        return jnp.concatenate(rows, axis=0)

    total = halves(side) + exchange(halves(1 - side), 1)
    total = sum_over(total, exchange, 2, blks).astype(bf16)
    arrived = [swap(total, d) for d in range(reps)]
    parts = [part[:half].astype(f32) for part in arrived]
    while len(parts) > 1:
        parts = [parts[i] + parts[i + 1] for i in range(0, len(parts), 2)]
    total = jnp.concatenate(parts + [part[half:].astype(f32) for part in arrived], axis=0)
    grad_in, grad_wide = simple_call(
        functools.partial(last_kernel, chunk),
        [
            jax.ShapeDtypeStruct((width, hidden_width), f32),
            jax.ShapeDtypeStruct((classes, hidden_width), f32),
        ],
        "last", total, exchange(total, 1), spot=(spot,),
    )
    grad_out = grad_wide.T
    return (logits[None], grad_in, grad_out)


def solution(mesh):
    placed = (
        P("blk", "rep", None),
        P("blk", "rep"),
        P("blk", "rep"),
        P("blk", "rep"),
        P("blk", "rep", None, None, None, None),
        P("blk", "rep", None, None),
        P("blk", "rep", None),
        P(),
        P(),
        P(),
    )
    return jax.shard_map(
        on_device,
        mesh=mesh,
        in_specs=placed,
        out_specs=(P("blk", "rep", None), P(), P()),
        check_vma=False,
    )
```

```python
import functools
import math

import jax
import jax.numpy as jnp
from jax import lax
from jax.experimental import pallas as pl
from jax.experimental.pallas import tpu as pltpu
from jax.sharding import PartitionSpec as P


LEVELS = 32767.0
MANTISSA_BITS = 14
HEAD_ROWS = 16


def keep_mask(id_values, unit_values):
    mixed = id_values * 73244475 + unit_values * 19349663 + 12345
    mixed = mixed ^ jnp.right_shift(mixed, 15)
    mixed = mixed * 40503
    mixed = mixed ^ jnp.right_shift(mixed, 13)
    return (jnp.bitwise_and(mixed, 3) != 0).astype(jnp.bfloat16)


def eye_of(count):
    rows = lax.broadcasted_iota(jnp.int32, (count, count), 0)
    columns = lax.broadcasted_iota(jnp.int32, (count, count), 1)
    return rows == columns


def dot(left, right):
    return jnp.dot(left, right, preferred_element_type=jnp.float32)


def dot_wide(left, right):
    return lax.dot_general(
        left, right, (((1,), (1,)), ((), ())), preferred_element_type=jnp.float32
    )


def encode(values):
    rows, width = values.shape
    largest = jnp.maximum(jnp.max(jnp.abs(values), axis=1, keepdims=True), 1e-30)
    power = jnp.ceil(jnp.log2(largest))
    mantissa = jnp.ceil(largest * jnp.exp2(MANTISSA_BITS - power))
    scale = mantissa * jnp.exp2(power - MANTISSA_BITS)
    coded = jnp.clip(jnp.round(values * (LEVELS / scale)), -LEVELS, LEVELS)
    square = eye_of(width)
    index = lax.broadcasted_iota(jnp.int32, (HEAD_ROWS, width), 0)
    head = jnp.zeros((HEAD_ROWS, width), jnp.float32)
    for part in range(rows // width):
        for offset, column in enumerate((power, mantissa)):
            column = column[part * width : (part + 1) * width]
            line = jnp.sum(jnp.where(square, column, 0.0), axis=0, keepdims=True)
            head = jnp.where(index == 2 * part + offset, line, head)
    whole = jnp.concatenate([coded, head], axis=0)
    return whole.astype(jnp.int32).astype(jnp.int16)


def decode(coded):
    whole = coded.astype(jnp.int32).astype(jnp.float32)
    rows, width = whole.shape[0] - HEAD_ROWS, whole.shape[1]
    square = eye_of(width)
    columns = [[], []]
    for part in range(rows // width):
        for offset in range(2):
            start = rows + 2 * part + offset
            line = whole[start : start + 1]
            columns[offset].append(jnp.sum(jnp.where(square, line, 0.0), axis=1, keepdims=True))
    power, mantissa = (jnp.concatenate(parts, axis=0) for parts in columns)
    return whole[:rows] * (mantissa * jnp.exp2(power - MANTISSA_BITS) * (1.0 / LEVELS))


def encode_kernel(partial_ref, *coded_refs):
    own_rows = partial_ref.shape[0] // (len(coded_refs) + 1)
    for delta, coded_ref in enumerate(coded_refs, 1):
        coded_ref[...] = encode(partial_ref[delta * own_rows : (delta + 1) * own_rows, :])


def last_kernel(chunk, spot_ref, total_ref, other_ref, grad_in_ref, grad_out_ref):
    side, rep_index = spot_ref[0], spot_ref[1]
    half = grad_in_ref.shape[0] // 2
    piece = chunk // 2
    classes = grad_out_ref.shape[0]
    reps = (total_ref.shape[0] - half) // piece
    for part in range(2):

        def take(start, size):
            rows = pl.ds(start, size)
            return jnp.where(side == part, total_ref[rows, :], other_ref[rows, :])

        grad_in_ref[part * half : (part + 1) * half, :] = take(0, half)
        for r in range(reps):
            start = r * chunk + part * piece
            size = min(piece, classes - start)
            if size > 0:
                spot = pl.multiple_of(half + (r ^ rep_index) * piece, 8)
                grad_out_ref[start : start + size, :] = take(spot, piece)[:size]


def head_kernel(
    scale, reps, spot_ref, weight_ref, bias_ref, label_ref, mask_ref, own_ref, *refs
):
    coded_refs, refs = refs[: reps - 1], refs[reps - 1 :]
    logits_ref, own_terms_ref, sent_refs, terms_ref = refs[0], refs[1], refs[2:-1], refs[-1]
    own_rows, classes = logits_ref.shape
    total = own_ref[:own_rows, :]
    for coded_ref in coded_refs:
        total += decode(coded_ref[...])
    z_output = total.astype(jnp.bfloat16)
    square = eye_of(own_rows)
    label, mask = (
        jnp.sum(jnp.where(square, ref[...].astype(jnp.float32), 0.0), axis=1, keepdims=True)
        for ref in (label_ref, mask_ref)
    )
    logits = dot_wide(z_output, weight_ref[...]) + bias_ref[...]
    logits_ref[...] = logits
    shifted = jnp.exp(logits - jnp.max(logits, axis=1, keepdims=True))
    likelihood = shifted / jnp.sum(shifted, axis=1, keepdims=True)
    onehot = label.astype(jnp.int32) == lax.broadcasted_iota(jnp.int32, logits.shape, 1)
    slope = (likelihood - onehot.astype(jnp.float32)) * mask * scale
    slope = slope.astype(jnp.bfloat16)
    grad_rows = dot(slope, weight_ref[...]).astype(jnp.bfloat16)
    terms = lax.dot_general(
        slope, z_output, (((0,), (0,)), ((), ())), preferred_element_type=jnp.float32
    )
    terms_ref[:classes, :] = terms
    pad = terms_ref.shape[0] - classes
    if pad:
        terms_ref[classes:, :] = jnp.zeros((pad, terms.shape[1]), jnp.float32)
    chunk = own_terms_ref.shape[0]
    for delta, sent_ref in enumerate(sent_refs):
        start = pl.multiple_of((spot_ref[1] ^ delta) * chunk, 8)
        piece = terms_ref[pl.ds(start, chunk), :]
        sent_ref[:own_rows, :] = grad_rows
        sent_ref[own_rows:, :] = piece.astype(jnp.bfloat16)
        if delta == 0:
            own_terms_ref[...] = piece


def simple_call(body, shapes, name, *values, spot=(), scratch=()):
    smem = pl.BlockSpec(memory_space=pltpu.SMEM)
    vmem = pl.BlockSpec(memory_space=pltpu.VMEM)
    return pl.pallas_call(
        body,
        in_specs=[smem] * len(spot) + [vmem] * len(values),
        out_shape=shapes,
        scratch_shapes=scratch,
        compiler_params=pltpu.CompilerParams(vmem_limit_bytes=8 * 1024 * 1024),
        name=name,
    )(*spot, *values)


def dense_kernel(per_rep, tile_side, turn, meta_ref, tiles_ref, dense_ref):
    section = pl.program_id(0)
    sections = pl.num_programs(0)
    rep_index, source_rep = meta_ref[0], meta_ref[1 + section]
    slots, edge = tiles_ref.shape[1], tiles_ref.shape[-1]
    dense_ref[...] = jnp.zeros_like(dense_ref)

    def put(slot, carried):
        place = meta_ref[1 + 2 * sections + section * slots + slot]
        row = place // tile_side
        column = place % tile_side
        row = ((row // per_rep) ^ rep_index) * per_rep + row % per_rep
        column = ((column // per_rep) ^ source_rep) * per_rep + column % per_rep
        rows = pl.ds(pl.multiple_of(row * edge, edge), edge)
        columns = pl.ds(pl.multiple_of(column * edge, edge), edge)
        tile = tiles_ref[0, slot]
        if turn:
            dense_ref[columns, rows] = tile.T
        else:
            dense_ref[rows, columns] = tile
        return carried

    lax.fori_loop(0, meta_ref[1 + sections + section], put, 0)


def build_dense(tiles, meta, own_rows, group_rows, turn):
    sections, slots, edge, _ = tiles.shape
    body = functools.partial(dense_kernel, own_rows // edge, group_rows // edge, turn)
    block = (group_rows, group_rows)
    shape = (sections * group_rows, group_rows) if turn else (group_rows, sections * group_rows)
    return pl.pallas_call(
        body,
        grid_spec=pltpu.PrefetchScalarGridSpec(
            num_scalar_prefetch=1,
            grid=(sections,),
            in_specs=[pl.BlockSpec((1, slots, edge, edge), lambda p, *_: (p, 0, 0, 0))],
            out_specs=pl.BlockSpec(block, lambda p, *_: (p, 0) if turn else (0, p)),
        ),
        out_shape=jax.ShapeDtypeStruct(shape, tiles.dtype),
        compiler_params=pltpu.CompilerParams(
            vmem_limit_bytes=4 * group_rows**2 + 8 * slots * edge**2 + (2 << 20)
        ),
        cost_estimate=pl.CostEstimate(
            flops=0, bytes_accessed=4 * sections * group_rows * group_rows, transcendentals=0
        ),
        name="dense_turned" if turn else "dense",
    )(meta, tiles)


def on_device(
    features,
    node_ids,
    labels,
    train_mask,
    tile_values,
    tile_place,
    tile_count,
    weight_in,
    weight_out,
    class_bias,
):
    own_rows = features.shape[1]
    reps = lax.axis_size("rep")
    blks = lax.axis_size("blk")
    rep_index = lax.axis_index("rep")
    blk_index = lax.axis_index("blk")
    sections = tile_values.shape[2]
    group_rows = own_rows * reps
    hidden_width = weight_in.shape[1]
    scale = 1.0 / math.sqrt(group_rows * blks)
    f32 = jnp.float32
    bf16 = jnp.bfloat16

    def swap(value, delta):
        if delta == 0:
            return value
        return lax.ppermute(value, "rep", [(r, r ^ delta) for r in range(reps)])

    def to_section(block, j):
        pairs = []
        for r in range(reps):
            for c in range(blks):
                member = c % sections + j
                if member < sections:
                    pairs.append((r * blks + c, r * blks + c + j))
                else:
                    pairs.append((r * blks + c, (r - 1) % reps * blks + c + j - sections))
        return lax.ppermute(block, ("rep", "blk"), pairs)

    def exchange(value, delta):
        return lax.ppermute(value, "blk", [(c, c ^ delta) for c in range(blks)])

    def to_pieces(value):
        pieces = []
        for delta in range(reps):
            pairs = []
            for r in range(reps):
                for c in range(blks):
                    target = r ^ delta
                    pairs.append((r * blks + c, target * blks + (c + sections * target) % blks))
            pieces.append(lax.ppermute(value, ("rep", "blk"), pairs))
        return pieces

    def to_all(pieces):
        cut = reps // 2
        halves = [jnp.concatenate(pieces[:cut], axis=0), jnp.concatenate(pieces[cut:], axis=0)]
        blocks = list(halves)
        for j in range(1, sections):
            blocks += [to_section(half, j) for half in halves]
        return blocks

    side = lax.rem(blk_index, 2)

    def halve(value):
        half = value.shape[0] // 2
        theirs = exchange(lax.dynamic_slice_in_dim(value, (1 - side) * half, half, 0), 1)
        return lax.dynamic_slice_in_dim(value, side * half, half, 0) + theirs

    def sum_over(value, move, first, size):
        rounded = value.astype(bf16)
        parts = [rounded if d == 0 else move(rounded, d) for d in range(0, size, first)]
        parts = [part.astype(f32) for part in parts]
        while len(parts) > 1:
            parts = [parts[i] + parts[i + 1] for i in range(0, len(parts), 2)]
        return parts[0]

    def digits(ids):
        lanes = features.shape[2]
        parts = [ids & 255, (ids >> 8) & 255, ids >> 16]
        rows = jnp.concatenate([part.reshape(-1, lanes) for part in parts], axis=0)
        return jnp.pad(rows, ((0, -rows.shape[0] % 16), (0, 0))).astype(bf16)

    def undo_digits(rows):
        count = own_rows // rows.shape[1]
        parts = [rows[i * count : (i + 1) * count].astype(jnp.int32) for i in range(3)]
        return (parts[0] + (parts[1] << 8) + (parts[2] << 16)).reshape(own_rows)

    member = lax.rem(blk_index, sections)
    place, count = tile_place[0, 0], tile_count[0, 0]
    width = features.shape[2]
    bundle = jnp.concatenate([features[0], digits(node_ids[0])], axis=0)
    stride = bundle.shape[0]
    arrived = to_pieces(bundle)
    tiles = tile_values[0, 0]
    next_rep = lax.rem(rep_index + 1, reps)
    where = jnp.where(member < jnp.arange(sections + 1) - 1, next_rep, rep_index)
    meta = jnp.concatenate([where, count, place.reshape(-1)])
    meta, arrived[0] = lax.optimization_barrier((meta, arrived[0]))
    dense = build_dense(tiles, meta, own_rows, group_rows, False)
    pieces = [
        half[d * stride : (d + 1) * stride] for half in to_all(arrived) for d in range(reps // 2)
    ]
    id_columns = jnp.concatenate([undo_digits(piece[own_rows:]) for piece in pieces])
    feature_columns = jnp.concatenate([piece[:own_rows] for piece in pieces], axis=0)
    units = jnp.arange(hidden_width, dtype=jnp.int32)
    kept = keep_mask(id_columns[:, None], units[None, :])
    chunks = dot(dense, feature_columns).reshape(reps, own_rows, width)
    arrived = [swap(chunks[delta], delta) for delta in range(1, reps)]
    total = chunks[0]
    for part in arrived:
        total = total + part
    z_input = total.astype(bf16)
    z_columns = jnp.concatenate(to_all(to_pieces(z_input)), axis=0)
    kept, z_columns = lax.optimization_barrier((kept, z_columns))
    third = f32(4.0 / 3.0)
    pre_act = dot(z_columns, weight_in)
    dropped = (jnp.maximum(pre_act, 0.0) * (kept.astype(f32) * third)).astype(bf16)
    dropped, z_again = lax.optimization_barrier((dropped, z_columns))
    second = dot(dense, dropped)
    mask = jnp.where(dot(z_again, weight_in) > 0, kept, jnp.zeros_like(kept))
    mask, ready = lax.optimization_barrier((mask, second))
    sent = simple_call(
        encode_kernel,
        [jax.ShapeDtypeStruct((own_rows + HEAD_ROWS, hidden_width), jnp.int16)] * (reps - 1),
        "encode", second,
    )
    arrived = [swap(sent[d - 1], d) for d in range(1, reps)]
    classes = weight_out.shape[1]
    chunk = -(-classes // (16 * reps)) * 16
    spot = jnp.stack([side, rep_index])
    logits, out_total, *sent = simple_call(
        functools.partial(head_kernel, scale, reps),
        [
            jax.ShapeDtypeStruct((own_rows, classes), f32),
            jax.ShapeDtypeStruct((chunk, hidden_width), f32),
        ]
        + [jax.ShapeDtypeStruct((own_rows + chunk, hidden_width), bf16)] * reps,
        "head",
        weight_out.T, class_bias[None], labels, train_mask,
        ready, *arrived,
        spot=(spot,),
        scratch=[pltpu.VMEM((chunk * reps, hidden_width), f32)],
    )
    arrived = [swap(sent[d], d) for d in range(reps)]
    meta, out_total = lax.optimization_barrier((meta, out_total))
    turned = build_dense(tiles, meta, own_rows, group_rows, True)
    grad_block = jnp.concatenate([part[:own_rows] for part in arrived], axis=0)
    for part in arrived[1:]:
        out_total = out_total + part[own_rows:].astype(f32)
    grad_block, mask, out_total = lax.optimization_barrier((grad_block, mask, out_total))
    back = dot(turned, grad_block)
    pre_slope = (back * (mask.astype(f32) * third)).astype(bf16)
    pre_slope, out_total = lax.optimization_barrier((pre_slope, out_total))
    in_terms = lax.dot_general(
        z_columns, pre_slope, (((0,), (0,)), ((), ())), preferred_element_type=f32
    )
    half, piece = width // 2, chunk // 2

    def halves(which):
        rows = [
            lax.dynamic_slice_in_dim(in_terms, which * half, half, 0),
            lax.dynamic_slice_in_dim(out_total, which * piece, piece, 0),
        ]
        return jnp.concatenate(rows, axis=0)

    total = halves(side) + exchange(halves(1 - side), 1)
    total = sum_over(total, exchange, 2, blks).astype(bf16)
    arrived = [swap(total, d) for d in range(reps)]
    parts = [part[:half].astype(f32) for part in arrived]
    while len(parts) > 1:
        parts = [parts[i] + parts[i + 1] for i in range(0, len(parts), 2)]
    total = jnp.concatenate(parts + [part[half:].astype(f32) for part in arrived], axis=0)
    grad_in, grad_wide = simple_call(
        functools.partial(last_kernel, chunk),
        [
            jax.ShapeDtypeStruct((width, hidden_width), f32),
            jax.ShapeDtypeStruct((classes, hidden_width), f32),
        ],
        "last", total, exchange(total, 1), spot=(spot,),
    )
    grad_out = grad_wide.T
    return (logits[None], grad_in, grad_out)


def solution(mesh):
    placed = (
        P("blk", "rep", None),
        P("blk", "rep"),
        P("blk", "rep"),
        P("blk", "rep"),
        P("blk", "rep", None, None, None, None),
        P("blk", "rep", None, None),
        P("blk", "rep", None),
        P(),
        P(),
        P(),
    )
    return jax.shard_map(
        on_device,
        mesh=mesh,
        in_specs=placed,
        out_specs=(P("blk", "rep", None), P(), P()),
        check_vma=False,
    )
```

```python
import functools
import math

import jax
import jax.numpy as jnp
from jax import lax
from jax.experimental import pallas as pl
from jax.experimental.pallas import tpu as pltpu
from jax.sharding import PartitionSpec as P


LEVELS = 32767.0
MANTISSA_BITS = 14
HEAD_ROWS = 16


def keep_mask(id_values, unit_values):
    mixed = id_values * 73244475 + unit_values * 19349663 + 12345
    mixed = mixed ^ jnp.right_shift(mixed, 15)
    mixed = mixed * 40503
    mixed = mixed ^ jnp.right_shift(mixed, 13)
    return (jnp.bitwise_and(mixed, 3) != 0).astype(jnp.bfloat16)


def eye_of(count):
    rows = lax.broadcasted_iota(jnp.int32, (count, count), 0)
    columns = lax.broadcasted_iota(jnp.int32, (count, count), 1)
    return rows == columns


def dot(left, right):
    return jnp.dot(left, right, preferred_element_type=jnp.float32)


def dot_wide(left, right):
    return lax.dot_general(
        left, right, (((1,), (1,)), ((), ())), preferred_element_type=jnp.float32
    )


def encode(values):
    rows, width = values.shape
    largest = jnp.maximum(jnp.max(jnp.abs(values), axis=1, keepdims=True), 1e-30)
    power = jnp.ceil(jnp.log2(largest))
    mantissa = jnp.ceil(largest * jnp.exp2(MANTISSA_BITS - power))
    scale = mantissa * jnp.exp2(power - MANTISSA_BITS)
    coded = jnp.clip(jnp.round(values * (LEVELS / scale)), -LEVELS, LEVELS)
    square = eye_of(width)
    index = lax.broadcasted_iota(jnp.int32, (HEAD_ROWS, width), 0)
    head = jnp.zeros((HEAD_ROWS, width), jnp.float32)
    for part in range(rows // width):
        for offset, column in enumerate((power, mantissa)):
            column = column[part * width : (part + 1) * width]
            line = jnp.sum(jnp.where(square, column, 0.0), axis=0, keepdims=True)
            head = jnp.where(index == 2 * part + offset, line, head)
    whole = jnp.concatenate([coded, head], axis=0)
    return whole.astype(jnp.int32).astype(jnp.int16)


def decode(coded):
    whole = coded.astype(jnp.int32).astype(jnp.float32)
    rows, width = whole.shape[0] - HEAD_ROWS, whole.shape[1]
    square = eye_of(width)
    columns = [[], []]
    for part in range(rows // width):
        for offset in range(2):
            start = rows + 2 * part + offset
            line = whole[start : start + 1]
            columns[offset].append(jnp.sum(jnp.where(square, line, 0.0), axis=1, keepdims=True))
    power, mantissa = (jnp.concatenate(parts, axis=0) for parts in columns)
    return whole[:rows] * (mantissa * jnp.exp2(power - MANTISSA_BITS) * (1.0 / LEVELS))


def encode_kernel(partial_ref, *coded_refs):
    own_rows = partial_ref.shape[0] // (len(coded_refs) + 1)
    for delta, coded_ref in enumerate(coded_refs, 1):
        coded_ref[...] = encode(partial_ref[delta * own_rows : (delta + 1) * own_rows, :])


def last_kernel(chunk, spot_ref, total_ref, other_ref, grad_in_ref, grad_out_ref):
    side, rep_index = spot_ref[0], spot_ref[1]
    half = grad_in_ref.shape[0] // 2
    piece = chunk // 2
    classes = grad_out_ref.shape[0]
    reps = (total_ref.shape[0] - half) // piece
    for part in range(2):

        def take(start, size):
            rows = pl.ds(start, size)
            return jnp.where(side == part, total_ref[rows, :], other_ref[rows, :])

        grad_in_ref[part * half : (part + 1) * half, :] = take(0, half)
        for r in range(reps):
            start = r * chunk + part * piece
            size = min(piece, classes - start)
            if size > 0:
                spot = pl.multiple_of(half + (r ^ rep_index) * piece, 8)
                grad_out_ref[start : start + size, :] = take(spot, piece)[:size]


def head_kernel(
    scale, reps, spot_ref, weight_ref, bias_ref, label_ref, mask_ref, own_ref, *refs
):
    coded_refs, refs = refs[: reps - 1], refs[reps - 1 :]
    logits_ref, own_terms_ref, sent_refs, terms_ref = refs[0], refs[1], refs[2:-1], refs[-1]
    own_rows, classes = logits_ref.shape
    total = own_ref[:own_rows, :]
    for coded_ref in coded_refs:
        total += decode(coded_ref[...])
    z_output = total.astype(jnp.bfloat16)
    square = eye_of(own_rows)
    label, mask = (
        jnp.sum(jnp.where(square, ref[...].astype(jnp.float32), 0.0), axis=1, keepdims=True)
        for ref in (label_ref, mask_ref)
    )
    logits = dot_wide(z_output, weight_ref[...]) + bias_ref[...]
    logits_ref[...] = logits
    shifted = jnp.exp(logits - jnp.max(logits, axis=1, keepdims=True))
    likelihood = shifted / jnp.sum(shifted, axis=1, keepdims=True)
    onehot = label.astype(jnp.int32) == lax.broadcasted_iota(jnp.int32, logits.shape, 1)
    slope = (likelihood - onehot.astype(jnp.float32)) * mask * scale
    slope = slope.astype(jnp.bfloat16)
    grad_rows = dot(slope, weight_ref[...]).astype(jnp.bfloat16)
    terms = lax.dot_general(
        slope, z_output, (((0,), (0,)), ((), ())), preferred_element_type=jnp.float32
    )
    terms_ref[:classes, :] = terms
    pad = terms_ref.shape[0] - classes
    if pad:
        terms_ref[classes:, :] = jnp.zeros((pad, terms.shape[1]), jnp.float32)
    chunk = own_terms_ref.shape[0]
    for delta, sent_ref in enumerate(sent_refs):
        start = pl.multiple_of((spot_ref[1] ^ delta) * chunk, 8)
        piece = terms_ref[pl.ds(start, chunk), :]
        sent_ref[:own_rows, :] = grad_rows
        sent_ref[own_rows:, :] = piece.astype(jnp.bfloat16)
        if delta == 0:
            own_terms_ref[...] = piece


def simple_call(body, shapes, name, *values, spot=(), scratch=()):
    smem = pl.BlockSpec(memory_space=pltpu.SMEM)
    vmem = pl.BlockSpec(memory_space=pltpu.VMEM)
    return pl.pallas_call(
        body,
        in_specs=[smem] * len(spot) + [vmem] * len(values),
        out_shape=shapes,
        scratch_shapes=scratch,
        compiler_params=pltpu.CompilerParams(vmem_limit_bytes=8 * 1024 * 1024),
        name=name,
    )(*spot, *values)


def dense_kernel(per_rep, tile_side, turn, meta_ref, tiles_ref, dense_ref):
    section = pl.program_id(0)
    rep_index, source_rep = meta_ref[section, 0], meta_ref[section, 1]
    edge = tiles_ref.shape[-1]
    dense_ref[...] = jnp.zeros_like(dense_ref)

    def put(slot, carried):
        place = meta_ref[section, 3 + slot]
        row = place // tile_side
        column = place % tile_side
        row = ((row // per_rep) ^ rep_index) * per_rep + row % per_rep
        column = ((column // per_rep) ^ source_rep) * per_rep + column % per_rep
        rows = pl.ds(pl.multiple_of(row * edge, edge), edge)
        columns = pl.ds(pl.multiple_of(column * edge, edge), edge)
        tile = tiles_ref[0, slot]
        if turn:
            dense_ref[columns, rows] = tile.T
        else:
            dense_ref[rows, columns] = tile
        return carried

    lax.fori_loop(0, meta_ref[section, 2], put, 0)


def build_dense(tiles, meta, own_rows, group_rows, turn):
    sections, slots, edge, _ = tiles.shape
    body = functools.partial(dense_kernel, own_rows // edge, group_rows // edge, turn)
    block = (group_rows, group_rows)
    shape = (sections * group_rows, group_rows) if turn else (group_rows, sections * group_rows)
    return pl.pallas_call(
        body,
        grid_spec=pltpu.PrefetchScalarGridSpec(
            num_scalar_prefetch=1,
            grid=(sections,),
            in_specs=[pl.BlockSpec((1, slots, edge, edge), lambda p, *_: (p, 0, 0, 0))],
            out_specs=pl.BlockSpec(block, lambda p, *_: (p, 0) if turn else (0, p)),
        ),
        out_shape=jax.ShapeDtypeStruct(shape, tiles.dtype),
        compiler_params=pltpu.CompilerParams(
            vmem_limit_bytes=4 * group_rows**2 + 8 * slots * edge**2 + (2 << 20)
        ),
        cost_estimate=pl.CostEstimate(
            flops=0, bytes_accessed=4 * sections * group_rows * group_rows, transcendentals=0
        ),
        name="dense_turned" if turn else "dense",
    )(meta, tiles)


def on_device(
    features,
    node_ids,
    labels,
    train_mask,
    tile_values,
    tile_place,
    tile_count,
    weight_in,
    weight_out,
    class_bias,
):
    own_rows = features.shape[1]
    reps = lax.axis_size("rep")
    blks = lax.axis_size("blk")
    rep_index = lax.axis_index("rep")
    blk_index = lax.axis_index("blk")
    sections = tile_values.shape[2]
    group_rows = own_rows * reps
    hidden_width = weight_in.shape[1]
    scale = 1.0 / math.sqrt(group_rows * blks)
    f32 = jnp.float32
    bf16 = jnp.bfloat16

    def swap(value, delta):
        if delta == 0:
            return value
        return lax.ppermute(value, "rep", [(r, r ^ delta) for r in range(reps)])

    def to_section(block, j):
        pairs = []
        for r in range(reps):
            for c in range(blks):
                member = c % sections + j
                if member < sections:
                    pairs.append((r * blks + c, r * blks + c + j))
                else:
                    pairs.append((r * blks + c, (r - 1) % reps * blks + c + j - sections))
        return lax.ppermute(block, ("rep", "blk"), pairs)

    def exchange(value, delta):
        return lax.ppermute(value, "blk", [(c, c ^ delta) for c in range(blks)])

    def to_pieces(value):
        pieces = []
        for delta in range(reps):
            pairs = []
            for r in range(reps):
                for c in range(blks):
                    target = r ^ delta
                    pairs.append((r * blks + c, target * blks + (c + sections * target) % blks))
            pieces.append(lax.ppermute(value, ("rep", "blk"), pairs))
        return pieces

    def to_all(pieces):
        cut = reps // 2
        halves = [jnp.concatenate(pieces[:cut], axis=0), jnp.concatenate(pieces[cut:], axis=0)]
        blocks = list(halves)
        for j in range(1, sections):
            blocks += [to_section(half, j) for half in halves]
        return blocks

    side = lax.rem(blk_index, 2)

    def halve(value):
        half = value.shape[0] // 2
        theirs = exchange(lax.dynamic_slice_in_dim(value, (1 - side) * half, half, 0), 1)
        return lax.dynamic_slice_in_dim(value, side * half, half, 0) + theirs

    def sum_over(value, move, first, size):
        rounded = value.astype(bf16)
        parts = [rounded if d == 0 else move(rounded, d) for d in range(0, size, first)]
        parts = [part.astype(f32) for part in parts]
        while len(parts) > 1:
            parts = [parts[i] + parts[i + 1] for i in range(0, len(parts), 2)]
        return parts[0]

    def digits(ids):
        lanes = features.shape[2]
        parts = [ids & 255, (ids >> 8) & 255, ids >> 16]
        rows = jnp.concatenate([part.reshape(-1, lanes) for part in parts], axis=0)
        return jnp.pad(rows, ((0, -rows.shape[0] % 16), (0, 0))).astype(bf16)

    def undo_digits(rows):
        count = own_rows // rows.shape[1]
        parts = [rows[i * count : (i + 1) * count].astype(jnp.int32) for i in range(3)]
        return (parts[0] + (parts[1] << 8) + (parts[2] << 16)).reshape(own_rows)

    member = lax.rem(blk_index, sections)
    place, count = tile_place[0, 0], tile_count[0, 0]
    width = features.shape[2]
    bundle = jnp.concatenate([features[0], digits(node_ids[0])], axis=0)
    stride = bundle.shape[0]
    arrived = to_pieces(bundle)
    tiles = tile_values[0, 0]
    next_rep = lax.rem(rep_index + 1, reps)
    where = jnp.where(member < jnp.arange(sections + 1) - 1, next_rep, rep_index)
    where, arrived[0] = lax.optimization_barrier((where, arrived[0]))
    columns = [jnp.broadcast_to(where[0], (sections, 1)), where[1:, None], count[:, None], place]
    meta = jnp.concatenate(columns, axis=1)
    dense = build_dense(tiles, meta, own_rows, group_rows, False)
    pieces = [
        half[d * stride : (d + 1) * stride] for half in to_all(arrived) for d in range(reps // 2)
    ]
    id_columns = jnp.concatenate([undo_digits(piece[own_rows:]) for piece in pieces])
    feature_columns = jnp.concatenate([piece[:own_rows] for piece in pieces], axis=0)
    units = jnp.arange(hidden_width, dtype=jnp.int32)
    kept = keep_mask(id_columns[:, None], units[None, :])
    chunks = dot(dense, feature_columns).reshape(reps, own_rows, width)
    arrived = [swap(chunks[delta], delta) for delta in range(1, reps)]
    kept, arrived = lax.optimization_barrier((kept, arrived))
    total = chunks[0]
    for part in arrived:
        total = total + part
    z_input = total.astype(bf16)
    z_columns = jnp.concatenate(to_all(to_pieces(z_input)), axis=0)
    kept, z_columns = lax.optimization_barrier((kept, z_columns))
    third = f32(4.0 / 3.0)
    pre_act = dot(z_columns, weight_in)
    dropped = (jnp.maximum(pre_act, 0.0) * (kept.astype(f32) * third)).astype(bf16)
    dropped, z_again = lax.optimization_barrier((dropped, z_columns))
    second = dot(dense, dropped)
    mask = jnp.where(dot(z_again, weight_in) > 0, kept, jnp.zeros_like(kept))
    mask, ready = lax.optimization_barrier((mask, second))
    sent = simple_call(
        encode_kernel,
        [jax.ShapeDtypeStruct((own_rows + HEAD_ROWS, hidden_width), jnp.int16)] * (reps - 1),
        "encode", second,
    )
    arrived = [swap(sent[d - 1], d) for d in range(1, reps)]
    classes = weight_out.shape[1]
    chunk = -(-classes // (16 * reps)) * 16
    spot = jnp.stack([side, rep_index])
    logits, out_total, *sent = simple_call(
        functools.partial(head_kernel, scale, reps),
        [
            jax.ShapeDtypeStruct((own_rows, classes), f32),
            jax.ShapeDtypeStruct((chunk, hidden_width), f32),
        ]
        + [jax.ShapeDtypeStruct((own_rows + chunk, hidden_width), bf16)] * reps,
        "head",
        weight_out.T, class_bias[None], labels, train_mask,
        ready, *arrived,
        spot=(spot,),
        scratch=[pltpu.VMEM((chunk * reps, hidden_width), f32)],
    )
    arrived = [swap(sent[d], d) for d in range(reps)]
    meta, out_total = lax.optimization_barrier((meta, out_total))
    turned = build_dense(tiles, meta, own_rows, group_rows, True)
    grad_block = jnp.concatenate([part[:own_rows] for part in arrived], axis=0)
    for part in arrived[1:]:
        out_total = out_total + part[own_rows:].astype(f32)
    grad_block, mask, out_total = lax.optimization_barrier((grad_block, mask, out_total))
    back = dot(turned, grad_block)
    pre_slope = (back * (mask.astype(f32) * third)).astype(bf16)
    pre_slope, out_total = lax.optimization_barrier((pre_slope, out_total))
    in_terms = lax.dot_general(
        z_columns, pre_slope, (((0,), (0,)), ((), ())), preferred_element_type=f32
    )
    half, piece = width // 2, chunk // 2

    def halves(which):
        rows = [
            lax.dynamic_slice_in_dim(in_terms, which * half, half, 0),
            lax.dynamic_slice_in_dim(out_total, which * piece, piece, 0),
        ]
        return jnp.concatenate(rows, axis=0)

    total = halves(side) + exchange(halves(1 - side), 1)
    total = sum_over(total, exchange, 2, blks).astype(bf16)
    arrived = [swap(total, d) for d in range(reps)]
    parts = [part[:half].astype(f32) for part in arrived]
    while len(parts) > 1:
        parts = [parts[i] + parts[i + 1] for i in range(0, len(parts), 2)]
    total = jnp.concatenate(parts + [part[half:].astype(f32) for part in arrived], axis=0)
    grad_in, grad_wide = simple_call(
        functools.partial(last_kernel, chunk),
        [
            jax.ShapeDtypeStruct((width, hidden_width), f32),
            jax.ShapeDtypeStruct((classes, hidden_width), f32),
        ],
        "last", total, exchange(total, 1), spot=(spot,),
    )
    grad_out = grad_wide.T
    return (logits[None], grad_in, grad_out)


def solution(mesh):
    placed = (
        P("blk", "rep", None),
        P("blk", "rep"),
        P("blk", "rep"),
        P("blk", "rep"),
        P("blk", "rep", None, None, None, None),
        P("blk", "rep", None, None),
        P("blk", "rep", None),
        P(),
        P(),
        P(),
    )
    return jax.shard_map(
        on_device,
        mesh=mesh,
        in_specs=placed,
        out_specs=(P("blk", "rep", None), P(), P()),
        check_vma=False,
    )
```

```python
import functools
import math

import jax
import jax.numpy as jnp
from jax import lax
from jax.experimental import pallas as pl
from jax.experimental.pallas import tpu as pltpu
from jax.sharding import PartitionSpec as P


LEVELS = 32767.0
MANTISSA_BITS = 14
HEAD_ROWS = 16


def keep_mask(id_values, unit_values):
    mixed = id_values * 73244475 + unit_values * 19349663 + 12345
    mixed = mixed ^ jnp.right_shift(mixed, 15)
    mixed = mixed * 40503
    mixed = mixed ^ jnp.right_shift(mixed, 13)
    return (jnp.bitwise_and(mixed, 3) != 0).astype(jnp.bfloat16)


def eye_of(count):
    rows = lax.broadcasted_iota(jnp.int32, (count, count), 0)
    columns = lax.broadcasted_iota(jnp.int32, (count, count), 1)
    return rows == columns


def dot(left, right):
    return jnp.dot(left, right, preferred_element_type=jnp.float32)


def dot_wide(left, right):
    return lax.dot_general(
        left, right, (((1,), (1,)), ((), ())), preferred_element_type=jnp.float32
    )


def encode(values):
    rows, width = values.shape
    largest = jnp.maximum(jnp.max(jnp.abs(values), axis=1, keepdims=True), 1e-30)
    power = jnp.ceil(jnp.log2(largest))
    mantissa = jnp.ceil(largest * jnp.exp2(MANTISSA_BITS - power))
    scale = mantissa * jnp.exp2(power - MANTISSA_BITS)
    coded = jnp.clip(jnp.round(values * (LEVELS / scale)), -LEVELS, LEVELS)
    square = eye_of(width)
    index = lax.broadcasted_iota(jnp.int32, (HEAD_ROWS, width), 0)
    head = jnp.zeros((HEAD_ROWS, width), jnp.float32)
    for part in range(rows // width):
        for offset, column in enumerate((power, mantissa)):
            column = column[part * width : (part + 1) * width]
            line = jnp.sum(jnp.where(square, column, 0.0), axis=0, keepdims=True)
            head = jnp.where(index == 2 * part + offset, line, head)
    whole = jnp.concatenate([coded, head], axis=0)
    return whole.astype(jnp.int32).astype(jnp.int16)


def decode(coded):
    whole = coded.astype(jnp.int32).astype(jnp.float32)
    rows, width = whole.shape[0] - HEAD_ROWS, whole.shape[1]
    square = eye_of(width)
    columns = [[], []]
    for part in range(rows // width):
        for offset in range(2):
            start = rows + 2 * part + offset
            line = whole[start : start + 1]
            columns[offset].append(jnp.sum(jnp.where(square, line, 0.0), axis=1, keepdims=True))
    power, mantissa = (jnp.concatenate(parts, axis=0) for parts in columns)
    return whole[:rows] * (mantissa * jnp.exp2(power - MANTISSA_BITS) * (1.0 / LEVELS))


def encode_kernel(partial_ref, *coded_refs):
    own_rows = partial_ref.shape[0] // (len(coded_refs) + 1)
    for delta, coded_ref in enumerate(coded_refs, 1):
        coded_ref[...] = encode(partial_ref[delta * own_rows : (delta + 1) * own_rows, :])


def last_kernel(chunk, spot_ref, total_ref, other_ref, grad_in_ref, grad_out_ref):
    side, rep_index = spot_ref[0], spot_ref[1]
    half = grad_in_ref.shape[0] // 2
    piece = chunk // 2
    classes = grad_out_ref.shape[0]
    reps = (total_ref.shape[0] - half) // piece
    for part in range(2):

        def take(start, size):
            rows = pl.ds(start, size)
            return jnp.where(side == part, total_ref[rows, :], other_ref[rows, :])

        grad_in_ref[part * half : (part + 1) * half, :] = take(0, half)
        for r in range(reps):
            start = r * chunk + part * piece
            size = min(piece, classes - start)
            if size > 0:
                spot = pl.multiple_of(half + (r ^ rep_index) * piece, 8)
                grad_out_ref[start : start + size, :] = take(spot, piece)[:size]


def head_kernel(
    scale, reps, spot_ref, weight_ref, bias_ref, label_ref, mask_ref, own_ref, *refs
):
    coded_refs, refs = refs[: reps - 1], refs[reps - 1 :]
    logits_ref, own_terms_ref, sent_refs, terms_ref = refs[0], refs[1], refs[2:-1], refs[-1]
    own_rows, classes = logits_ref.shape
    total = own_ref[:own_rows, :]
    for coded_ref in coded_refs:
        total += decode(coded_ref[...])
    z_output = total.astype(jnp.bfloat16)
    square = eye_of(own_rows)
    label, mask = (
        jnp.sum(jnp.where(square, ref[...].astype(jnp.float32), 0.0), axis=1, keepdims=True)
        for ref in (label_ref, mask_ref)
    )
    logits = dot_wide(z_output, weight_ref[...]) + bias_ref[...]
    logits_ref[...] = logits
    shifted = jnp.exp(logits - jnp.max(logits, axis=1, keepdims=True))
    likelihood = shifted / jnp.sum(shifted, axis=1, keepdims=True)
    onehot = label.astype(jnp.int32) == lax.broadcasted_iota(jnp.int32, logits.shape, 1)
    slope = (likelihood - onehot.astype(jnp.float32)) * mask * scale
    slope = slope.astype(jnp.bfloat16)
    grad_rows = dot(slope, weight_ref[...]).astype(jnp.bfloat16)
    terms = lax.dot_general(
        slope, z_output, (((0,), (0,)), ((), ())), preferred_element_type=jnp.float32
    )
    terms_ref[:classes, :] = terms
    pad = terms_ref.shape[0] - classes
    if pad:
        terms_ref[classes:, :] = jnp.zeros((pad, terms.shape[1]), jnp.float32)
    chunk = own_terms_ref.shape[0]
    for delta, sent_ref in enumerate(sent_refs):
        start = pl.multiple_of((spot_ref[1] ^ delta) * chunk, 8)
        piece = terms_ref[pl.ds(start, chunk), :]
        sent_ref[:own_rows, :] = grad_rows
        sent_ref[own_rows:, :] = piece.astype(jnp.bfloat16)
        if delta == 0:
            own_terms_ref[...] = piece


def simple_call(body, shapes, name, *values, spot=(), scratch=()):
    smem = pl.BlockSpec(memory_space=pltpu.SMEM)
    vmem = pl.BlockSpec(memory_space=pltpu.VMEM)
    return pl.pallas_call(
        body,
        in_specs=[smem] * len(spot) + [vmem] * len(values),
        out_shape=shapes,
        scratch_shapes=scratch,
        compiler_params=pltpu.CompilerParams(vmem_limit_bytes=8 * 1024 * 1024),
        name=name,
    )(*spot, *values)


def dense_kernel(per_rep, tile_side, turn, meta_ref, tiles_ref, dense_ref):
    section = pl.program_id(0)
    rep_index, source_rep = meta_ref[section, 0], meta_ref[section, 1]
    edge = tiles_ref.shape[-1]
    dense_ref[...] = jnp.zeros_like(dense_ref)

    def put(slot, carried):
        place = meta_ref[section, 3 + slot]
        row = place // tile_side
        column = place % tile_side
        row = ((row // per_rep) ^ rep_index) * per_rep + row % per_rep
        column = ((column // per_rep) ^ source_rep) * per_rep + column % per_rep
        rows = pl.ds(pl.multiple_of(row * edge, edge), edge)
        columns = pl.ds(pl.multiple_of(column * edge, edge), edge)
        tile = tiles_ref[0, slot]
        if turn:
            dense_ref[columns, rows] = tile.T
        else:
            dense_ref[rows, columns] = tile
        return carried

    lax.fori_loop(0, meta_ref[section, 2], put, 0)


def build_dense(tiles, meta, own_rows, group_rows, turn):
    sections, slots, edge, _ = tiles.shape
    body = functools.partial(dense_kernel, own_rows // edge, group_rows // edge, turn)
    block = (group_rows, group_rows)
    shape = (sections * group_rows, group_rows) if turn else (group_rows, sections * group_rows)
    return pl.pallas_call(
        body,
        grid_spec=pltpu.PrefetchScalarGridSpec(
            num_scalar_prefetch=1,
            grid=(sections,),
            in_specs=[pl.BlockSpec((1, slots, edge, edge), lambda p, *_: (p, 0, 0, 0))],
            out_specs=pl.BlockSpec(block, lambda p, *_: (p, 0) if turn else (0, p)),
        ),
        out_shape=jax.ShapeDtypeStruct(shape, tiles.dtype),
        compiler_params=pltpu.CompilerParams(
            vmem_limit_bytes=4 * group_rows**2 + 8 * slots * edge**2 + (2 << 20)
        ),
        cost_estimate=pl.CostEstimate(
            flops=0, bytes_accessed=4 * sections * group_rows * group_rows, transcendentals=0
        ),
        name="dense_turned" if turn else "dense",
    )(meta, tiles)


def on_device(
    features,
    node_ids,
    labels,
    train_mask,
    tile_values,
    tile_place,
    tile_count,
    weight_in,
    weight_out,
    class_bias,
):
    own_rows = features.shape[1]
    reps = lax.axis_size("rep")
    blks = lax.axis_size("blk")
    rep_index = lax.axis_index("rep")
    blk_index = lax.axis_index("blk")
    sections = tile_values.shape[2]
    group_rows = own_rows * reps
    hidden_width = weight_in.shape[1]
    scale = 1.0 / math.sqrt(group_rows * blks)
    f32 = jnp.float32
    bf16 = jnp.bfloat16

    def swap(value, delta):
        if delta == 0:
            return value
        return lax.ppermute(value, "rep", [(r, r ^ delta) for r in range(reps)])

    def to_section(block, j):
        pairs = []
        for r in range(reps):
            for c in range(blks):
                member = c % sections + j
                if member < sections:
                    pairs.append((r * blks + c, r * blks + c + j))
                else:
                    pairs.append((r * blks + c, (r - 1) % reps * blks + c + j - sections))
        return lax.ppermute(block, ("rep", "blk"), pairs)

    def exchange(value, delta):
        return lax.ppermute(value, "blk", [(c, c ^ delta) for c in range(blks)])

    def to_pieces(value):
        pieces = []
        for delta in range(reps):
            pairs = []
            for r in range(reps):
                for c in range(blks):
                    target = r ^ delta
                    pairs.append((r * blks + c, target * blks + (c + sections * target) % blks))
            pieces.append(lax.ppermute(value, ("rep", "blk"), pairs))
        return pieces

    def to_all(pieces, size):
        parts = [
            jnp.concatenate(pieces[start : start + size], axis=0)
            for start in range(0, reps, size)
        ]
        blocks = list(parts)
        for j in range(1, sections):
            blocks += [to_section(part, j) for part in parts]
        return blocks

    side = lax.rem(blk_index, 2)

    def halve(value):
        half = value.shape[0] // 2
        theirs = exchange(lax.dynamic_slice_in_dim(value, (1 - side) * half, half, 0), 1)
        return lax.dynamic_slice_in_dim(value, side * half, half, 0) + theirs

    def sum_over(value, move, first, size):
        rounded = value.astype(bf16)
        parts = [rounded if d == 0 else move(rounded, d) for d in range(0, size, first)]
        parts = [part.astype(f32) for part in parts]
        while len(parts) > 1:
            parts = [parts[i] + parts[i + 1] for i in range(0, len(parts), 2)]
        return parts[0]

    def digits(ids):
        lanes = features.shape[2]
        parts = [ids & 255, (ids >> 8) & 255, ids >> 16]
        rows = jnp.concatenate([part.reshape(-1, lanes) for part in parts], axis=0)
        return jnp.pad(rows, ((0, -rows.shape[0] % 16), (0, 0))).astype(bf16)

    def undo_digits(rows):
        count = own_rows // rows.shape[1]
        parts = [rows[i * count : (i + 1) * count].astype(jnp.int32) for i in range(3)]
        return (parts[0] + (parts[1] << 8) + (parts[2] << 16)).reshape(own_rows)

    member = lax.rem(blk_index, sections)
    place, count = tile_place[0, 0], tile_count[0, 0]
    width = features.shape[2]
    bundle = jnp.concatenate([features[0], digits(node_ids[0])], axis=0)
    stride = bundle.shape[0]
    arrived = to_pieces(bundle)
    tiles = tile_values[0, 0]
    next_rep = lax.rem(rep_index + 1, reps)
    where = jnp.where(member < jnp.arange(sections + 1) - 1, next_rep, rep_index)
    where, arrived[0] = lax.optimization_barrier((where, arrived[0]))
    columns = [jnp.broadcast_to(where[0], (sections, 1)), where[1:, None], count[:, None], place]
    meta = jnp.concatenate(columns, axis=1)
    dense = build_dense(tiles, meta, own_rows, group_rows, False)
    pieces = [
        half[d * stride : (d + 1) * stride]
        for half in to_all(arrived, reps // 2)
        for d in range(reps // 2)
    ]
    id_columns = jnp.concatenate([undo_digits(piece[own_rows:]) for piece in pieces])
    feature_columns = jnp.concatenate([piece[:own_rows] for piece in pieces], axis=0)
    units = jnp.arange(hidden_width, dtype=jnp.int32)
    kept = keep_mask(id_columns[:, None], units[None, :])
    chunks = dot(dense, feature_columns).reshape(reps, own_rows, width)
    arrived = [swap(chunks[delta], delta) for delta in range(1, reps)]
    kept, arrived = lax.optimization_barrier((kept, arrived))
    total = chunks[0]
    for part in arrived:
        total = total + part
    z_input = total.astype(bf16)
    z_columns = jnp.concatenate(to_all(to_pieces(z_input), 1), axis=0)
    kept, z_columns = lax.optimization_barrier((kept, z_columns))
    third = f32(4.0 / 3.0)
    pre_act = dot(z_columns, weight_in)
    dropped = (jnp.maximum(pre_act, 0.0) * (kept.astype(f32) * third)).astype(bf16)
    dropped, z_again = lax.optimization_barrier((dropped, z_columns))
    second = dot(dense, dropped)
    mask = jnp.where(dot(z_again, weight_in) > 0, kept, jnp.zeros_like(kept))
    mask, ready = lax.optimization_barrier((mask, second))
    sent = simple_call(
        encode_kernel,
        [jax.ShapeDtypeStruct((own_rows + HEAD_ROWS, hidden_width), jnp.int16)] * (reps - 1),
        "encode", second,
    )
    arrived = [swap(sent[d - 1], d) for d in range(1, reps)]
    classes = weight_out.shape[1]
    chunk = -(-classes // (16 * reps)) * 16
    spot = jnp.stack([side, rep_index])
    logits, out_total, *sent = simple_call(
        functools.partial(head_kernel, scale, reps),
        [
            jax.ShapeDtypeStruct((own_rows, classes), f32),
            jax.ShapeDtypeStruct((chunk, hidden_width), f32),
        ]
        + [jax.ShapeDtypeStruct((own_rows + chunk, hidden_width), bf16)] * reps,
        "head",
        weight_out.T, class_bias[None], labels, train_mask,
        ready, *arrived,
        spot=(spot,),
        scratch=[pltpu.VMEM((chunk * reps, hidden_width), f32)],
    )
    arrived = [swap(sent[d], d) for d in range(reps)]
    meta, out_total = lax.optimization_barrier((meta, out_total))
    turned = build_dense(tiles, meta, own_rows, group_rows, True)
    grad_block = jnp.concatenate([part[:own_rows] for part in arrived], axis=0)
    for part in arrived[1:]:
        out_total = out_total + part[own_rows:].astype(f32)
    grad_block, mask, out_total = lax.optimization_barrier((grad_block, mask, out_total))
    back = dot(turned, grad_block)
    pre_slope = (back * (mask.astype(f32) * third)).astype(bf16)
    pre_slope, out_total = lax.optimization_barrier((pre_slope, out_total))
    in_terms = lax.dot_general(
        z_columns, pre_slope, (((0,), (0,)), ((), ())), preferred_element_type=f32
    )
    half, piece = width // 2, chunk // 2

    def halves(which):
        rows = [
            lax.dynamic_slice_in_dim(in_terms, which * half, half, 0),
            lax.dynamic_slice_in_dim(out_total, which * piece, piece, 0),
        ]
        return jnp.concatenate(rows, axis=0)

    total = halves(side) + exchange(halves(1 - side), 1)
    total = sum_over(total, exchange, 2, blks).astype(bf16)
    arrived = [swap(total, d) for d in range(reps)]
    parts = [part[:half].astype(f32) for part in arrived]
    while len(parts) > 1:
        parts = [parts[i] + parts[i + 1] for i in range(0, len(parts), 2)]
    total = jnp.concatenate(parts + [part[half:].astype(f32) for part in arrived], axis=0)
    grad_in, grad_wide = simple_call(
        functools.partial(last_kernel, chunk),
        [
            jax.ShapeDtypeStruct((width, hidden_width), f32),
            jax.ShapeDtypeStruct((classes, hidden_width), f32),
        ],
        "last", total, exchange(total, 1), spot=(spot,),
    )
    grad_out = grad_wide.T
    return (logits[None], grad_in, grad_out)


def solution(mesh):
    placed = (
        P("blk", "rep", None),
        P("blk", "rep"),
        P("blk", "rep"),
        P("blk", "rep"),
        P("blk", "rep", None, None, None, None),
        P("blk", "rep", None, None),
        P("blk", "rep", None),
        P(),
        P(),
        P(),
    )
    return jax.shard_map(
        on_device,
        mesh=mesh,
        in_specs=placed,
        out_specs=(P("blk", "rep", None), P(), P()),
        check_vma=False,
    )
```

```python
import functools
import math

import jax
import jax.numpy as jnp
from jax import lax
from jax.experimental import pallas as pl
from jax.experimental.pallas import tpu as pltpu
from jax.sharding import PartitionSpec as P


LEVELS = 32767.0
MANTISSA_BITS = 14
HEAD_ROWS = 16


def keep_mask(id_values, unit_values):
    mixed = id_values * 73244475 + unit_values * 19349663 + 12345
    mixed = mixed ^ jnp.right_shift(mixed, 15)
    mixed = mixed * 40503
    mixed = mixed ^ jnp.right_shift(mixed, 13)
    return (jnp.bitwise_and(mixed, 3) != 0).astype(jnp.bfloat16)


def eye_of(count):
    rows = lax.broadcasted_iota(jnp.int32, (count, count), 0)
    columns = lax.broadcasted_iota(jnp.int32, (count, count), 1)
    return rows == columns


def dot(left, right):
    return jnp.dot(left, right, preferred_element_type=jnp.float32)


def dot_wide(left, right):
    return lax.dot_general(
        left, right, (((1,), (1,)), ((), ())), preferred_element_type=jnp.float32
    )


def encode(values):
    rows, width = values.shape
    largest = jnp.maximum(jnp.max(jnp.abs(values), axis=1, keepdims=True), 1e-30)
    power = jnp.ceil(jnp.log2(largest))
    mantissa = jnp.ceil(largest * jnp.exp2(MANTISSA_BITS - power))
    scale = mantissa * jnp.exp2(power - MANTISSA_BITS)
    coded = jnp.clip(jnp.round(values * (LEVELS / scale)), -LEVELS, LEVELS)
    square = eye_of(width)
    index = lax.broadcasted_iota(jnp.int32, (HEAD_ROWS, width), 0)
    head = jnp.zeros((HEAD_ROWS, width), jnp.float32)
    for part in range(rows // width):
        for offset, column in enumerate((power, mantissa)):
            column = column[part * width : (part + 1) * width]
            line = jnp.sum(jnp.where(square, column, 0.0), axis=0, keepdims=True)
            head = jnp.where(index == 2 * part + offset, line, head)
    whole = jnp.concatenate([coded, head], axis=0)
    return whole.astype(jnp.int32).astype(jnp.int16)


def decode(coded):
    whole = coded.astype(jnp.int32).astype(jnp.float32)
    rows, width = whole.shape[0] - HEAD_ROWS, whole.shape[1]
    square = eye_of(width)
    columns = [[], []]
    for part in range(rows // width):
        for offset in range(2):
            start = rows + 2 * part + offset
            line = whole[start : start + 1]
            columns[offset].append(jnp.sum(jnp.where(square, line, 0.0), axis=1, keepdims=True))
    power, mantissa = (jnp.concatenate(parts, axis=0) for parts in columns)
    return whole[:rows] * (mantissa * jnp.exp2(power - MANTISSA_BITS) * (1.0 / LEVELS))


def encode_kernel(partial_ref, *coded_refs):
    own_rows = partial_ref.shape[0] // (len(coded_refs) + 1)
    for delta, coded_ref in enumerate(coded_refs, 1):
        coded_ref[...] = encode(partial_ref[delta * own_rows : (delta + 1) * own_rows, :])


def last_kernel(chunk, spot_ref, total_ref, other_ref, grad_in_ref, grad_out_ref):
    side, rep_index = spot_ref[0], spot_ref[1]
    half = grad_in_ref.shape[0] // 2
    piece = chunk // 2
    classes = grad_out_ref.shape[0]
    reps = (total_ref.shape[0] - half) // piece
    for part in range(2):

        def take(start, size):
            rows = pl.ds(start, size)
            return jnp.where(side == part, total_ref[rows, :], other_ref[rows, :])

        grad_in_ref[part * half : (part + 1) * half, :] = take(0, half)
        for r in range(reps):
            start = r * chunk + part * piece
            size = min(piece, classes - start)
            if size > 0:
                spot = pl.multiple_of(half + (r ^ rep_index) * piece, 8)
                grad_out_ref[start : start + size, :] = take(spot, piece)[:size]


def head_kernel(
    scale, reps, spot_ref, weight_ref, bias_ref, label_ref, mask_ref, own_ref, *refs
):
    coded_refs, refs = refs[: reps - 1], refs[reps - 1 :]
    logits_ref, own_terms_ref, sent_refs, terms_ref = refs[0], refs[1], refs[2:-1], refs[-1]
    own_rows, classes = logits_ref.shape
    total = own_ref[:own_rows, :]
    for coded_ref in coded_refs:
        total += decode(coded_ref[...])
    z_output = total.astype(jnp.bfloat16)
    square = eye_of(own_rows)
    label, mask = (
        jnp.sum(jnp.where(square, ref[...].astype(jnp.float32), 0.0), axis=1, keepdims=True)
        for ref in (label_ref, mask_ref)
    )
    logits = dot_wide(z_output, weight_ref[...]) + bias_ref[...]
    logits_ref[...] = logits
    shifted = jnp.exp(logits - jnp.max(logits, axis=1, keepdims=True))
    likelihood = shifted / jnp.sum(shifted, axis=1, keepdims=True)
    onehot = label.astype(jnp.int32) == lax.broadcasted_iota(jnp.int32, logits.shape, 1)
    slope = (likelihood - onehot.astype(jnp.float32)) * mask * scale
    slope = slope.astype(jnp.bfloat16)
    grad_rows = dot(slope, weight_ref[...]).astype(jnp.bfloat16)
    terms = lax.dot_general(
        slope, z_output, (((0,), (0,)), ((), ())), preferred_element_type=jnp.float32
    )
    terms_ref[:classes, :] = terms
    pad = terms_ref.shape[0] - classes
    if pad:
        terms_ref[classes:, :] = jnp.zeros((pad, terms.shape[1]), jnp.float32)
    chunk = own_terms_ref.shape[0]
    for delta, sent_ref in enumerate(sent_refs):
        start = pl.multiple_of((spot_ref[1] ^ delta) * chunk, 8)
        piece = terms_ref[pl.ds(start, chunk), :]
        sent_ref[:own_rows, :] = grad_rows
        sent_ref[own_rows:, :] = piece.astype(jnp.bfloat16)
        if delta == 0:
            own_terms_ref[...] = piece


def simple_call(body, shapes, name, *values, spot=(), scratch=()):
    smem = pl.BlockSpec(memory_space=pltpu.SMEM)
    vmem = pl.BlockSpec(memory_space=pltpu.VMEM)
    return pl.pallas_call(
        body,
        in_specs=[smem] * len(spot) + [vmem] * len(values),
        out_shape=shapes,
        scratch_shapes=scratch,
        compiler_params=pltpu.CompilerParams(vmem_limit_bytes=8 * 1024 * 1024),
        name=name,
    )(*spot, *values)


def dense_kernel(per_rep, tile_side, turn, meta_ref, tiles_ref, dense_ref):
    section = pl.program_id(0)
    rep_index, source_rep = meta_ref[section, 0], meta_ref[section, 1]
    edge = tiles_ref.shape[-1]
    dense_ref[...] = jnp.zeros_like(dense_ref)

    def put(slot, carried):
        place = meta_ref[section, 3 + slot]
        row = place // tile_side
        column = place % tile_side
        row = ((row // per_rep) ^ rep_index) * per_rep + row % per_rep
        column = ((column // per_rep) ^ source_rep) * per_rep + column % per_rep
        rows = pl.ds(pl.multiple_of(row * edge, edge), edge)
        columns = pl.ds(pl.multiple_of(column * edge, edge), edge)
        tile = tiles_ref[0, slot]
        if turn:
            dense_ref[columns, rows] = tile.T
        else:
            dense_ref[rows, columns] = tile
        return carried

    lax.fori_loop(0, meta_ref[section, 2], put, 0)


def build_dense(tiles, meta, own_rows, group_rows, turn):
    sections, slots, edge, _ = tiles.shape
    body = functools.partial(dense_kernel, own_rows // edge, group_rows // edge, turn)
    block = (group_rows, group_rows)
    shape = (sections * group_rows, group_rows) if turn else (group_rows, sections * group_rows)
    return pl.pallas_call(
        body,
        grid_spec=pltpu.PrefetchScalarGridSpec(
            num_scalar_prefetch=1,
            grid=(sections,),
            in_specs=[pl.BlockSpec((1, slots, edge, edge), lambda p, *_: (p, 0, 0, 0))],
            out_specs=pl.BlockSpec(block, lambda p, *_: (p, 0) if turn else (0, p)),
        ),
        out_shape=jax.ShapeDtypeStruct(shape, tiles.dtype),
        compiler_params=pltpu.CompilerParams(
            vmem_limit_bytes=4 * group_rows**2 + 8 * slots * edge**2 + (2 << 20)
        ),
        cost_estimate=pl.CostEstimate(
            flops=0, bytes_accessed=4 * sections * group_rows * group_rows, transcendentals=0
        ),
        name="dense_turned" if turn else "dense",
    )(meta, tiles)


def on_device(
    features,
    node_ids,
    labels,
    train_mask,
    tile_values,
    tile_place,
    tile_count,
    weight_in,
    weight_out,
    class_bias,
):
    own_rows = features.shape[1]
    reps = lax.axis_size("rep")
    blks = lax.axis_size("blk")
    rep_index = lax.axis_index("rep")
    blk_index = lax.axis_index("blk")
    sections = tile_values.shape[2]
    group_rows = own_rows * reps
    hidden_width = weight_in.shape[1]
    scale = 1.0 / math.sqrt(group_rows * blks)
    f32 = jnp.float32
    bf16 = jnp.bfloat16

    def swap(value, delta):
        if delta == 0:
            return value
        return lax.ppermute(value, "rep", [(r, r ^ delta) for r in range(reps)])

    def to_section(block, j):
        pairs = []
        for r in range(reps):
            for c in range(blks):
                member = c % sections + j
                if member < sections:
                    pairs.append((r * blks + c, r * blks + c + j))
                else:
                    pairs.append((r * blks + c, (r - 1) % reps * blks + c + j - sections))
        return lax.ppermute(block, ("rep", "blk"), pairs)

    def exchange(value, delta):
        return lax.ppermute(value, "blk", [(c, c ^ delta) for c in range(blks)])

    def to_pieces(value):
        pieces = []
        for delta in range(reps):
            pairs = []
            for r in range(reps):
                for c in range(blks):
                    target = r ^ delta
                    pairs.append((r * blks + c, target * blks + (c + sections * target) % blks))
            pieces.append(lax.ppermute(value, ("rep", "blk"), pairs))
        return pieces

    def to_all(pieces, size):
        parts = [
            jnp.concatenate(pieces[start : start + size], axis=0)
            for start in range(0, reps, size)
        ]
        blocks = list(parts)
        for j in range(1, sections):
            blocks += [to_section(part, j) for part in parts]
        return blocks

    side = lax.rem(blk_index, 2)

    def halve(value):
        half = value.shape[0] // 2
        theirs = exchange(lax.dynamic_slice_in_dim(value, (1 - side) * half, half, 0), 1)
        return lax.dynamic_slice_in_dim(value, side * half, half, 0) + theirs

    def sum_over(value, move, first, size):
        rounded = value.astype(bf16)
        parts = [rounded if d == 0 else move(rounded, d) for d in range(0, size, first)]
        parts = [part.astype(f32) for part in parts]
        while len(parts) > 1:
            parts = [parts[i] + parts[i + 1] for i in range(0, len(parts), 2)]
        return parts[0]

    def digits(ids):
        lanes = features.shape[2]
        parts = [ids & 255, (ids >> 8) & 255, ids >> 16]
        rows = jnp.concatenate([part.reshape(-1, lanes) for part in parts], axis=0)
        return jnp.pad(rows, ((0, -rows.shape[0] % 16), (0, 0))).astype(bf16)

    def undo_digits(rows):
        count = own_rows // rows.shape[1]
        parts = [rows[i * count : (i + 1) * count].astype(jnp.int32) for i in range(3)]
        return (parts[0] + (parts[1] << 8) + (parts[2] << 16)).reshape(own_rows)

    member = lax.rem(blk_index, sections)
    place, count = tile_place[0, 0], tile_count[0, 0]
    width = features.shape[2]
    arrived = to_pieces(features[0])
    tiles = tile_values[0, 0]
    next_rep = lax.rem(rep_index + 1, reps)
    where = jnp.where(member < jnp.arange(sections + 1) - 1, next_rep, rep_index)
    where, arrived[0] = lax.optimization_barrier((where, arrived[0]))
    columns = [jnp.broadcast_to(where[0], (sections, 1)), where[1:, None], count[:, None], place]
    meta = jnp.concatenate(columns, axis=1)
    dense = build_dense(tiles, meta, own_rows, group_rows, False)
    feature_columns = jnp.concatenate(to_all(arrived, reps // 2), axis=0)
    chunks = dot(dense, feature_columns).reshape(reps, own_rows, width)
    arrived = [swap(chunks[delta], delta) for delta in range(1, reps)]
    total = chunks[0]
    for part in arrived:
        total = total + part
    z_input = total.astype(bf16)
    z_bundle = jnp.concatenate([z_input, digits(node_ids[0])], axis=0)
    pieces = to_all(to_pieces(z_bundle), 1)
    units = jnp.arange(hidden_width, dtype=jnp.int32)
    id_columns = jnp.concatenate([undo_digits(part[own_rows:]) for part in pieces])
    kept = keep_mask(id_columns[:, None], units[None, :])
    z_columns = jnp.concatenate([part[:own_rows] for part in pieces], axis=0)
    third = f32(4.0 / 3.0)
    pre_act = dot(z_columns, weight_in)
    dropped = (jnp.maximum(pre_act, 0.0) * (kept.astype(f32) * third)).astype(bf16)
    dropped, z_again = lax.optimization_barrier((dropped, z_columns))
    second = dot(dense, dropped)
    mask = jnp.where(dot(z_again, weight_in) > 0, kept, jnp.zeros_like(kept))
    mask, ready = lax.optimization_barrier((mask, second))
    sent = simple_call(
        encode_kernel,
        [jax.ShapeDtypeStruct((own_rows + HEAD_ROWS, hidden_width), jnp.int16)] * (reps - 1),
        "encode", second,
    )
    arrived = [swap(sent[d - 1], d) for d in range(1, reps)]
    classes = weight_out.shape[1]
    chunk = -(-classes // (16 * reps)) * 16
    spot = jnp.stack([side, rep_index])
    logits, out_total, *sent = simple_call(
        functools.partial(head_kernel, scale, reps),
        [
            jax.ShapeDtypeStruct((own_rows, classes), f32),
            jax.ShapeDtypeStruct((chunk, hidden_width), f32),
        ]
        + [jax.ShapeDtypeStruct((own_rows + chunk, hidden_width), bf16)] * reps,
        "head",
        weight_out.T, class_bias[None], labels, train_mask,
        ready, *arrived,
        spot=(spot,),
        scratch=[pltpu.VMEM((chunk * reps, hidden_width), f32)],
    )
    arrived = [swap(sent[d], d) for d in range(reps)]
    meta, out_total = lax.optimization_barrier((meta, out_total))
    turned = build_dense(tiles, meta, own_rows, group_rows, True)
    grad_block = jnp.concatenate([part[:own_rows] for part in arrived], axis=0)
    for part in arrived[1:]:
        out_total = out_total + part[own_rows:].astype(f32)
    grad_block, mask, out_total = lax.optimization_barrier((grad_block, mask, out_total))
    back = dot(turned, grad_block)
    pre_slope = (back * (mask.astype(f32) * third)).astype(bf16)
    pre_slope, out_total = lax.optimization_barrier((pre_slope, out_total))
    in_terms = lax.dot_general(
        z_columns, pre_slope, (((0,), (0,)), ((), ())), preferred_element_type=f32
    )
    half, piece = width // 2, chunk // 2

    def halves(which):
        rows = [
            lax.dynamic_slice_in_dim(in_terms, which * half, half, 0),
            lax.dynamic_slice_in_dim(out_total, which * piece, piece, 0),
        ]
        return jnp.concatenate(rows, axis=0)

    total = halves(side) + exchange(halves(1 - side), 1)
    total = sum_over(total, exchange, 2, blks).astype(bf16)
    arrived = [swap(total, d) for d in range(reps)]
    parts = [part[:half].astype(f32) for part in arrived]
    while len(parts) > 1:
        parts = [parts[i] + parts[i + 1] for i in range(0, len(parts), 2)]
    total = jnp.concatenate(parts + [part[half:].astype(f32) for part in arrived], axis=0)
    grad_in, grad_wide = simple_call(
        functools.partial(last_kernel, chunk),
        [
            jax.ShapeDtypeStruct((width, hidden_width), f32),
            jax.ShapeDtypeStruct((classes, hidden_width), f32),
        ],
        "last", total, exchange(total, 1), spot=(spot,),
    )
    grad_out = grad_wide.T
    return (logits[None], grad_in, grad_out)


def solution(mesh):
    placed = (
        P("blk", "rep", None),
        P("blk", "rep"),
        P("blk", "rep"),
        P("blk", "rep"),
        P("blk", "rep", None, None, None, None),
        P("blk", "rep", None, None),
        P("blk", "rep", None),
        P(),
        P(),
        P(),
    )
    return jax.shard_map(
        on_device,
        mesh=mesh,
        in_specs=placed,
        out_specs=(P("blk", "rep", None), P(), P()),
        check_vma=False,
    )
```

```python
import functools
import math

import jax
import jax.numpy as jnp
from jax import lax
from jax.experimental import pallas as pl
from jax.experimental.pallas import tpu as pltpu
from jax.sharding import PartitionSpec as P


LEVELS = 32767.0
MANTISSA_BITS = 14
HEAD_ROWS = 16


def keep_mask(id_values, unit_values):
    mixed = id_values * 73244475 + unit_values * 19349663 + 12345
    mixed = mixed ^ jnp.right_shift(mixed, 15)
    mixed = mixed * 40503
    mixed = mixed ^ jnp.right_shift(mixed, 13)
    return (jnp.bitwise_and(mixed, 3) != 0).astype(jnp.bfloat16)


def eye_of(count):
    rows = lax.broadcasted_iota(jnp.int32, (count, count), 0)
    columns = lax.broadcasted_iota(jnp.int32, (count, count), 1)
    return rows == columns


def dot(left, right):
    return jnp.dot(left, right, preferred_element_type=jnp.float32)


def dot_wide(left, right):
    return lax.dot_general(
        left, right, (((1,), (1,)), ((), ())), preferred_element_type=jnp.float32
    )


def encode(values):
    rows, width = values.shape
    largest = jnp.maximum(jnp.max(jnp.abs(values), axis=1, keepdims=True), 1e-30)
    power = jnp.ceil(jnp.log2(largest))
    mantissa = jnp.ceil(largest * jnp.exp2(MANTISSA_BITS - power))
    scale = mantissa * jnp.exp2(power - MANTISSA_BITS)
    coded = jnp.clip(jnp.round(values * (LEVELS / scale)), -LEVELS, LEVELS)
    square = eye_of(width)
    index = lax.broadcasted_iota(jnp.int32, (HEAD_ROWS, width), 0)
    head = jnp.zeros((HEAD_ROWS, width), jnp.float32)
    for part in range(rows // width):
        for offset, column in enumerate((power, mantissa)):
            column = column[part * width : (part + 1) * width]
            line = jnp.sum(jnp.where(square, column, 0.0), axis=0, keepdims=True)
            head = jnp.where(index == 2 * part + offset, line, head)
    whole = jnp.concatenate([coded, head], axis=0)
    return whole.astype(jnp.int32).astype(jnp.int16)


def decode(coded):
    whole = coded.astype(jnp.int32).astype(jnp.float32)
    rows, width = whole.shape[0] - HEAD_ROWS, whole.shape[1]
    square = eye_of(width)
    columns = [[], []]
    for part in range(rows // width):
        for offset in range(2):
            start = rows + 2 * part + offset
            line = whole[start : start + 1]
            columns[offset].append(jnp.sum(jnp.where(square, line, 0.0), axis=1, keepdims=True))
    power, mantissa = (jnp.concatenate(parts, axis=0) for parts in columns)
    return whole[:rows] * (mantissa * jnp.exp2(power - MANTISSA_BITS) * (1.0 / LEVELS))


def encode_kernel(partial_ref, *coded_refs):
    own_rows = partial_ref.shape[0] // (len(coded_refs) + 1)
    for delta, coded_ref in enumerate(coded_refs, 1):
        coded_ref[...] = encode(partial_ref[delta * own_rows : (delta + 1) * own_rows, :])


def last_kernel(chunk, spot_ref, total_ref, other_ref, grad_in_ref, grad_out_ref):
    side, rep_index = spot_ref[0], spot_ref[1]
    half = grad_in_ref.shape[0] // 2
    piece = chunk // 2
    classes = grad_out_ref.shape[0]
    reps = (total_ref.shape[0] - half) // piece
    for part in range(2):

        def take(start, size):
            rows = pl.ds(start, size)
            return jnp.where(side == part, total_ref[rows, :], other_ref[rows, :])

        grad_in_ref[part * half : (part + 1) * half, :] = take(0, half)
        for r in range(reps):
            start = r * chunk + part * piece
            size = min(piece, classes - start)
            if size > 0:
                spot = pl.multiple_of(half + (r ^ rep_index) * piece, 8)
                grad_out_ref[start : start + size, :] = take(spot, piece)[:size]


def head_kernel(
    scale, reps, spot_ref, weight_ref, bias_ref, label_ref, mask_ref, own_ref, *refs
):
    coded_refs, refs = refs[: reps - 1], refs[reps - 1 :]
    logits_ref, own_terms_ref, sent_refs, terms_ref = refs[0], refs[1], refs[2:-1], refs[-1]
    own_rows, classes = logits_ref.shape
    total = own_ref[:own_rows, :]
    for coded_ref in coded_refs:
        total += decode(coded_ref[...])
    z_output = total.astype(jnp.bfloat16)
    square = eye_of(own_rows)
    label, mask = (
        jnp.sum(jnp.where(square, ref[...].astype(jnp.float32), 0.0), axis=1, keepdims=True)
        for ref in (label_ref, mask_ref)
    )
    logits = dot_wide(z_output, weight_ref[...]) + bias_ref[...]
    logits_ref[...] = logits
    shifted = jnp.exp(logits - jnp.max(logits, axis=1, keepdims=True))
    likelihood = shifted / jnp.sum(shifted, axis=1, keepdims=True)
    onehot = label.astype(jnp.int32) == lax.broadcasted_iota(jnp.int32, logits.shape, 1)
    slope = (likelihood - onehot.astype(jnp.float32)) * mask * scale
    slope = slope.astype(jnp.bfloat16)
    grad_rows = dot(slope, weight_ref[...]).astype(jnp.bfloat16)
    terms = lax.dot_general(
        slope, z_output, (((0,), (0,)), ((), ())), preferred_element_type=jnp.float32
    )
    terms_ref[:classes, :] = terms
    pad = terms_ref.shape[0] - classes
    if pad:
        terms_ref[classes:, :] = jnp.zeros((pad, terms.shape[1]), jnp.float32)
    chunk = own_terms_ref.shape[0]
    for delta, sent_ref in enumerate(sent_refs):
        start = pl.multiple_of((spot_ref[1] ^ delta) * chunk, 8)
        piece = terms_ref[pl.ds(start, chunk), :]
        sent_ref[:own_rows, :] = grad_rows
        sent_ref[own_rows:, :] = piece.astype(jnp.bfloat16)
        if delta == 0:
            own_terms_ref[...] = piece


def simple_call(body, shapes, name, *values, spot=(), scratch=()):
    smem = pl.BlockSpec(memory_space=pltpu.SMEM)
    vmem = pl.BlockSpec(memory_space=pltpu.VMEM)
    return pl.pallas_call(
        body,
        in_specs=[smem] * len(spot) + [vmem] * len(values),
        out_shape=shapes,
        scratch_shapes=scratch,
        compiler_params=pltpu.CompilerParams(vmem_limit_bytes=8 * 1024 * 1024),
        name=name,
    )(*spot, *values)


def dense_kernel(per_rep, tile_side, turn, meta_ref, tiles_ref, dense_ref):
    section = pl.program_id(0)
    rep_index, source_rep = meta_ref[section, 0], meta_ref[section, 1]
    edge = tiles_ref.shape[-1]
    dense_ref[...] = jnp.zeros_like(dense_ref)

    def put(slot, carried):
        place = meta_ref[section, 3 + slot]
        row = place // tile_side
        column = place % tile_side
        row = ((row // per_rep) ^ rep_index) * per_rep + row % per_rep
        column = ((column // per_rep) ^ source_rep) * per_rep + column % per_rep
        rows = pl.ds(pl.multiple_of(row * edge, edge), edge)
        columns = pl.ds(pl.multiple_of(column * edge, edge), edge)
        tile = tiles_ref[0, slot]
        if turn:
            dense_ref[columns, rows] = tile.T
        else:
            dense_ref[rows, columns] = tile
        return carried

    lax.fori_loop(0, meta_ref[section, 2], put, 0)


def build_dense(tiles, meta, own_rows, group_rows, turn):
    sections, slots, edge, _ = tiles.shape
    body = functools.partial(dense_kernel, own_rows // edge, group_rows // edge, turn)
    block = (group_rows, group_rows)
    shape = (sections * group_rows, group_rows) if turn else (group_rows, sections * group_rows)
    return pl.pallas_call(
        body,
        grid_spec=pltpu.PrefetchScalarGridSpec(
            num_scalar_prefetch=1,
            grid=(sections,),
            in_specs=[pl.BlockSpec((1, slots, edge, edge), lambda p, *_: (p, 0, 0, 0))],
            out_specs=pl.BlockSpec(block, lambda p, *_: (p, 0) if turn else (0, p)),
        ),
        out_shape=jax.ShapeDtypeStruct(shape, tiles.dtype),
        compiler_params=pltpu.CompilerParams(
            vmem_limit_bytes=4 * group_rows**2 + 8 * slots * edge**2 + (2 << 20)
        ),
        cost_estimate=pl.CostEstimate(
            flops=0, bytes_accessed=4 * sections * group_rows * group_rows, transcendentals=0
        ),
        name="dense_turned" if turn else "dense",
    )(meta, tiles)


def on_device(
    features,
    node_ids,
    labels,
    train_mask,
    tile_values,
    tile_place,
    tile_count,
    weight_in,
    weight_out,
    class_bias,
):
    own_rows = features.shape[1]
    reps = lax.axis_size("rep")
    blks = lax.axis_size("blk")
    rep_index = lax.axis_index("rep")
    blk_index = lax.axis_index("blk")
    sections = tile_values.shape[2]
    group_rows = own_rows * reps
    hidden_width = weight_in.shape[1]
    scale = 1.0 / math.sqrt(group_rows * blks)
    f32 = jnp.float32
    bf16 = jnp.bfloat16

    def swap(value, delta):
        if delta == 0:
            return value
        return lax.ppermute(value, "rep", [(r, r ^ delta) for r in range(reps)])

    def to_section(block, j):
        pairs = []
        for r in range(reps):
            for c in range(blks):
                member = c % sections + j
                if member < sections:
                    pairs.append((r * blks + c, r * blks + c + j))
                else:
                    pairs.append((r * blks + c, (r - 1) % reps * blks + c + j - sections))
        return lax.ppermute(block, ("rep", "blk"), pairs)

    def exchange(value, delta):
        return lax.ppermute(value, "blk", [(c, c ^ delta) for c in range(blks)])

    def to_pieces(value):
        pieces = []
        for delta in range(reps):
            pairs = []
            for r in range(reps):
                for c in range(blks):
                    target = r ^ delta
                    pairs.append((r * blks + c, target * blks + (c + sections * target) % blks))
            pieces.append(lax.ppermute(value, ("rep", "blk"), pairs))
        return pieces

    def to_all(pieces, size):
        parts = [
            jnp.concatenate(pieces[start : start + size], axis=0)
            for start in range(0, reps, size)
        ]
        blocks = list(parts)
        for j in range(1, sections):
            blocks += [to_section(part, j) for part in parts]
        return blocks

    side = lax.rem(blk_index, 2)

    def halve(value):
        half = value.shape[0] // 2
        theirs = exchange(lax.dynamic_slice_in_dim(value, (1 - side) * half, half, 0), 1)
        return lax.dynamic_slice_in_dim(value, side * half, half, 0) + theirs

    def sum_over(value, move, first, size):
        rounded = value.astype(bf16)
        parts = [rounded if d == 0 else move(rounded, d) for d in range(0, size, first)]
        parts = [part.astype(f32) for part in parts]
        while len(parts) > 1:
            parts = [parts[i] + parts[i + 1] for i in range(0, len(parts), 2)]
        return parts[0]

    def digits(ids):
        lanes = features.shape[2]
        parts = [ids & 255, (ids >> 8) & 255, ids >> 16]
        rows = jnp.concatenate([part.reshape(-1, lanes) for part in parts], axis=0)
        return jnp.pad(rows, ((0, -rows.shape[0] % 16), (0, 0))).astype(bf16)

    def undo_digits(rows):
        count = own_rows // rows.shape[1]
        parts = [rows[i * count : (i + 1) * count].astype(jnp.int32) for i in range(3)]
        return (parts[0] + (parts[1] << 8) + (parts[2] << 16)).reshape(own_rows)

    member = lax.rem(blk_index, sections)
    place, count = tile_place[0, 0], tile_count[0, 0]
    width = features.shape[2]
    arrived = to_pieces(features[0])
    tiles = tile_values[0, 0]
    next_rep = lax.rem(rep_index + 1, reps)
    where = jnp.where(member < jnp.arange(sections + 1) - 1, next_rep, rep_index)
    where, arrived[0] = lax.optimization_barrier((where, arrived[0]))
    columns = [jnp.broadcast_to(where[0], (sections, 1)), where[1:, None], count[:, None], place]
    meta = jnp.concatenate(columns, axis=1)
    dense = build_dense(tiles, meta, own_rows, group_rows, False)
    feature_columns = jnp.concatenate(to_all(arrived, reps // 2), axis=0)
    chunks = dot(dense, feature_columns).reshape(reps, own_rows, width)
    arrived = [swap(chunks[delta], delta) for delta in range(1, reps)]
    total = chunks[0]
    for part in arrived:
        total = total + part
    z_input = total.astype(bf16)
    z_bundle = jnp.concatenate([z_input, digits(node_ids[0])], axis=0)
    pieces = to_all(to_pieces(z_bundle), 1)
    units = jnp.arange(hidden_width, dtype=jnp.int32)

    def kept_of(parts):
        ids = jnp.concatenate([undo_digits(part) for part in parts])
        return keep_mask(ids[:, None], units[None, :])

    rows = [part[own_rows:] for part in pieces]
    rows[:reps], pieces[reps] = lax.optimization_barrier((rows[:reps], pieces[reps]))
    kept_own, rows[-1] = lax.optimization_barrier((kept_of(rows[:reps]), rows[-1]))
    kept = jnp.concatenate([kept_own, kept_of(rows[reps:])], axis=0)
    z_columns = jnp.concatenate([part[:own_rows] for part in pieces], axis=0)
    kept, z_columns = lax.optimization_barrier((kept, z_columns))
    third = f32(4.0 / 3.0)
    pre_act = dot(z_columns, weight_in)
    dropped = (jnp.maximum(pre_act, 0.0) * (kept.astype(f32) * third)).astype(bf16)
    dropped, z_again = lax.optimization_barrier((dropped, z_columns))
    second = dot(dense, dropped)
    mask = jnp.where(dot(z_again, weight_in) > 0, kept, jnp.zeros_like(kept))
    mask, ready = lax.optimization_barrier((mask, second))
    sent = simple_call(
        encode_kernel,
        [jax.ShapeDtypeStruct((own_rows + HEAD_ROWS, hidden_width), jnp.int16)] * (reps - 1),
        "encode", second,
    )
    arrived = [swap(sent[d - 1], d) for d in range(1, reps)]
    classes = weight_out.shape[1]
    chunk = -(-classes // (16 * reps)) * 16
    spot = jnp.stack([side, rep_index])
    logits, out_total, *sent = simple_call(
        functools.partial(head_kernel, scale, reps),
        [
            jax.ShapeDtypeStruct((own_rows, classes), f32),
            jax.ShapeDtypeStruct((chunk, hidden_width), f32),
        ]
        + [jax.ShapeDtypeStruct((own_rows + chunk, hidden_width), bf16)] * reps,
        "head",
        weight_out.T, class_bias[None], labels, train_mask,
        ready, *arrived,
        spot=(spot,),
        scratch=[pltpu.VMEM((chunk * reps, hidden_width), f32)],
    )
    arrived = [swap(sent[d], d) for d in range(reps)]
    meta, out_total = lax.optimization_barrier((meta, out_total))
    turned = build_dense(tiles, meta, own_rows, group_rows, True)
    grad_block = jnp.concatenate([part[:own_rows] for part in arrived], axis=0)
    for part in arrived[1:]:
        out_total = out_total + part[own_rows:].astype(f32)
    grad_block, mask, out_total = lax.optimization_barrier((grad_block, mask, out_total))
    back = dot(turned, grad_block)
    pre_slope = (back * (mask.astype(f32) * third)).astype(bf16)
    pre_slope, out_total = lax.optimization_barrier((pre_slope, out_total))
    in_terms = lax.dot_general(
        z_columns, pre_slope, (((0,), (0,)), ((), ())), preferred_element_type=f32
    )
    half, piece = width // 2, chunk // 2

    def halves(which):
        rows = [
            lax.dynamic_slice_in_dim(in_terms, which * half, half, 0),
            lax.dynamic_slice_in_dim(out_total, which * piece, piece, 0),
        ]
        return jnp.concatenate(rows, axis=0)

    total = halves(side) + exchange(halves(1 - side), 1)
    total = sum_over(total, exchange, 2, blks).astype(bf16)
    arrived = [swap(total, d) for d in range(reps)]
    parts = [part[:half].astype(f32) for part in arrived]
    while len(parts) > 1:
        parts = [parts[i] + parts[i + 1] for i in range(0, len(parts), 2)]
    total = jnp.concatenate(parts + [part[half:].astype(f32) for part in arrived], axis=0)
    grad_in, grad_wide = simple_call(
        functools.partial(last_kernel, chunk),
        [
            jax.ShapeDtypeStruct((width, hidden_width), f32),
            jax.ShapeDtypeStruct((classes, hidden_width), f32),
        ],
        "last", total, exchange(total, 1), spot=(spot,),
    )
    grad_out = grad_wide.T
    return (logits[None], grad_in, grad_out)


def solution(mesh):
    placed = (
        P("blk", "rep", None),
        P("blk", "rep"),
        P("blk", "rep"),
        P("blk", "rep"),
        P("blk", "rep", None, None, None, None),
        P("blk", "rep", None, None),
        P("blk", "rep", None),
        P(),
        P(),
        P(),
    )
    return jax.shard_map(
        on_device,
        mesh=mesh,
        in_specs=placed,
        out_specs=(P("blk", "rep", None), P(), P()),
        check_vma=False,
    )
```

```python
import functools
import math

import jax
import jax.numpy as jnp
from jax import lax
from jax.experimental import pallas as pl
from jax.experimental.pallas import tpu as pltpu
from jax.sharding import PartitionSpec as P


LEVELS = 32767.0
MANTISSA_BITS = 14
HEAD_ROWS = 16


def keep_mask(id_values, unit_values):
    mixed = id_values * 73244475 + unit_values * 19349663 + 12345
    mixed = mixed ^ jnp.right_shift(mixed, 15)
    mixed = mixed * 40503
    mixed = mixed ^ jnp.right_shift(mixed, 13)
    return (jnp.bitwise_and(mixed, 3) != 0).astype(jnp.bfloat16)


def eye_of(count):
    rows = lax.broadcasted_iota(jnp.int32, (count, count), 0)
    columns = lax.broadcasted_iota(jnp.int32, (count, count), 1)
    return rows == columns


def dot(left, right):
    return jnp.dot(left, right, preferred_element_type=jnp.float32)


def dot_wide(left, right):
    return lax.dot_general(
        left, right, (((1,), (1,)), ((), ())), preferred_element_type=jnp.float32
    )


def encode(values):
    rows, width = values.shape
    largest = jnp.maximum(jnp.max(jnp.abs(values), axis=1, keepdims=True), 1e-30)
    power = jnp.ceil(jnp.log2(largest))
    mantissa = jnp.ceil(largest * jnp.exp2(MANTISSA_BITS - power))
    scale = mantissa * jnp.exp2(power - MANTISSA_BITS)
    coded = jnp.clip(jnp.round(values * (LEVELS / scale)), -LEVELS, LEVELS)
    square = eye_of(width)
    index = lax.broadcasted_iota(jnp.int32, (HEAD_ROWS, width), 0)
    head = jnp.zeros((HEAD_ROWS, width), jnp.float32)
    for part in range(rows // width):
        for offset, column in enumerate((power, mantissa)):
            column = column[part * width : (part + 1) * width]
            line = jnp.sum(jnp.where(square, column, 0.0), axis=0, keepdims=True)
            head = jnp.where(index == 2 * part + offset, line, head)
    whole = jnp.concatenate([coded, head], axis=0)
    return whole.astype(jnp.int32).astype(jnp.int16)


def decode(coded):
    whole = coded.astype(jnp.int32).astype(jnp.float32)
    rows, width = whole.shape[0] - HEAD_ROWS, whole.shape[1]
    square = eye_of(width)
    columns = [[], []]
    for part in range(rows // width):
        for offset in range(2):
            start = rows + 2 * part + offset
            line = whole[start : start + 1]
            columns[offset].append(jnp.sum(jnp.where(square, line, 0.0), axis=1, keepdims=True))
    power, mantissa = (jnp.concatenate(parts, axis=0) for parts in columns)
    return whole[:rows] * (mantissa * jnp.exp2(power - MANTISSA_BITS) * (1.0 / LEVELS))


def encode_kernel(partial_ref, *coded_refs):
    own_rows = partial_ref.shape[0] // (len(coded_refs) + 1)
    for delta, coded_ref in enumerate(coded_refs, 1):
        coded_ref[...] = encode(partial_ref[delta * own_rows : (delta + 1) * own_rows, :])


def last_kernel(chunk, spot_ref, total_ref, other_ref, grad_in_ref, grad_out_ref):
    side, rep_index = spot_ref[0], spot_ref[1]
    half = grad_in_ref.shape[0] // 2
    piece = chunk // 2
    classes = grad_out_ref.shape[0]
    reps = (total_ref.shape[0] - half) // piece
    for part in range(2):

        def take(start, size):
            rows = pl.ds(start, size)
            return jnp.where(side == part, total_ref[rows, :], other_ref[rows, :])

        grad_in_ref[part * half : (part + 1) * half, :] = take(0, half)
        for r in range(reps):
            start = r * chunk + part * piece
            size = min(piece, classes - start)
            if size > 0:
                spot = pl.multiple_of(half + (r ^ rep_index) * piece, 8)
                grad_out_ref[start : start + size, :] = take(spot, piece)[:size]


def head_kernel(
    scale, reps, spot_ref, weight_ref, bias_ref, label_ref, mask_ref, own_ref, *refs
):
    coded_refs, refs = refs[: reps - 1], refs[reps - 1 :]
    logits_ref, own_terms_ref, sent_refs, terms_ref = refs[0], refs[1], refs[2:-1], refs[-1]
    own_rows, classes = logits_ref.shape
    total = own_ref[:own_rows, :]
    for coded_ref in coded_refs:
        total += decode(coded_ref[...])
    z_output = total.astype(jnp.bfloat16)
    square = eye_of(own_rows)
    label, mask = (
        jnp.sum(jnp.where(square, ref[...].astype(jnp.float32), 0.0), axis=1, keepdims=True)
        for ref in (label_ref, mask_ref)
    )
    logits = dot_wide(z_output, weight_ref[...]) + bias_ref[...]
    logits_ref[...] = logits
    shifted = jnp.exp(logits - jnp.max(logits, axis=1, keepdims=True))
    likelihood = shifted / jnp.sum(shifted, axis=1, keepdims=True)
    onehot = label.astype(jnp.int32) == lax.broadcasted_iota(jnp.int32, logits.shape, 1)
    slope = (likelihood - onehot.astype(jnp.float32)) * mask * scale
    slope = slope.astype(jnp.bfloat16)
    grad_rows = dot(slope, weight_ref[...]).astype(jnp.bfloat16)
    terms = lax.dot_general(
        slope, z_output, (((0,), (0,)), ((), ())), preferred_element_type=jnp.float32
    )
    terms_ref[:classes, :] = terms
    pad = terms_ref.shape[0] - classes
    if pad:
        terms_ref[classes:, :] = jnp.zeros((pad, terms.shape[1]), jnp.float32)
    chunk = own_terms_ref.shape[0]
    for delta, sent_ref in enumerate(sent_refs):
        start = pl.multiple_of((spot_ref[1] ^ delta) * chunk, 8)
        piece = terms_ref[pl.ds(start, chunk), :]
        sent_ref[:own_rows, :] = grad_rows
        sent_ref[own_rows:, :] = piece.astype(jnp.bfloat16)
        if delta == 0:
            own_terms_ref[...] = piece


def simple_call(body, shapes, name, *values, spot=(), scratch=()):
    smem = pl.BlockSpec(memory_space=pltpu.SMEM)
    vmem = pl.BlockSpec(memory_space=pltpu.VMEM)
    return pl.pallas_call(
        body,
        in_specs=[smem] * len(spot) + [vmem] * len(values),
        out_shape=shapes,
        scratch_shapes=scratch,
        compiler_params=pltpu.CompilerParams(vmem_limit_bytes=8 * 1024 * 1024),
        name=name,
    )(*spot, *values)


def dense_kernel(per_rep, tile_side, turn, meta_ref, tiles_ref, dense_ref):
    section = pl.program_id(0)
    rep_index, source_rep = meta_ref[section, 0], meta_ref[section, 1]
    edge = tiles_ref.shape[-1]
    dense_ref[...] = jnp.zeros_like(dense_ref)

    def put(slot, carried):
        place = meta_ref[section, 3 + slot]
        row = place // tile_side
        column = place % tile_side
        row = ((row // per_rep) ^ rep_index) * per_rep + row % per_rep
        column = ((column // per_rep) ^ source_rep) * per_rep + column % per_rep
        rows = pl.ds(pl.multiple_of(row * edge, edge), edge)
        columns = pl.ds(pl.multiple_of(column * edge, edge), edge)
        tile = tiles_ref[0, slot]
        if turn:
            dense_ref[columns, rows] = tile.T
        else:
            dense_ref[rows, columns] = tile
        return carried

    lax.fori_loop(0, meta_ref[section, 2], put, 0)


def build_dense(tiles, meta, own_rows, group_rows, turn):
    sections, slots, edge, _ = tiles.shape
    body = functools.partial(dense_kernel, own_rows // edge, group_rows // edge, turn)
    block = (group_rows, group_rows)
    shape = (sections * group_rows, group_rows) if turn else (group_rows, sections * group_rows)
    return pl.pallas_call(
        body,
        grid_spec=pltpu.PrefetchScalarGridSpec(
            num_scalar_prefetch=1,
            grid=(sections,),
            in_specs=[pl.BlockSpec((1, slots, edge, edge), lambda p, *_: (p, 0, 0, 0))],
            out_specs=pl.BlockSpec(block, lambda p, *_: (p, 0) if turn else (0, p)),
        ),
        out_shape=jax.ShapeDtypeStruct(shape, tiles.dtype),
        compiler_params=pltpu.CompilerParams(
            vmem_limit_bytes=4 * group_rows**2 + 8 * slots * edge**2 + (2 << 20)
        ),
        cost_estimate=pl.CostEstimate(
            flops=0, bytes_accessed=4 * sections * group_rows * group_rows, transcendentals=0
        ),
        name="dense_turned" if turn else "dense",
    )(meta, tiles)


def on_device(
    features,
    node_ids,
    labels,
    train_mask,
    tile_values,
    tile_place,
    tile_count,
    weight_in,
    weight_out,
    class_bias,
):
    own_rows = features.shape[1]
    reps = lax.axis_size("rep")
    blks = lax.axis_size("blk")
    rep_index = lax.axis_index("rep")
    blk_index = lax.axis_index("blk")
    sections = tile_values.shape[2]
    group_rows = own_rows * reps
    hidden_width = weight_in.shape[1]
    scale = 1.0 / math.sqrt(group_rows * blks)
    f32 = jnp.float32
    bf16 = jnp.bfloat16

    def swap(value, delta):
        if delta == 0:
            return value
        return lax.ppermute(value, "rep", [(r, r ^ delta) for r in range(reps)])

    def to_section(block, j):
        pairs = []
        for r in range(reps):
            for c in range(blks):
                member = c % sections + j
                if member < sections:
                    pairs.append((r * blks + c, r * blks + c + j))
                else:
                    pairs.append((r * blks + c, (r - 1) % reps * blks + c + j - sections))
        return lax.ppermute(block, ("rep", "blk"), pairs)

    def exchange(value, delta):
        return lax.ppermute(value, "blk", [(c, c ^ delta) for c in range(blks)])

    def to_pieces(value):
        pieces = []
        for delta in range(reps):
            pairs = []
            for r in range(reps):
                for c in range(blks):
                    target = r ^ delta
                    pairs.append((r * blks + c, target * blks + (c + sections * target) % blks))
            pieces.append(lax.ppermute(value, ("rep", "blk"), pairs))
        return pieces

    def to_all(pieces, size):
        parts = [
            jnp.concatenate(pieces[start : start + size], axis=0)
            for start in range(0, reps, size)
        ]
        blocks = list(parts)
        for j in range(1, sections):
            blocks += [to_section(part, j) for part in parts]
        return blocks

    side = lax.rem(blk_index, 2)

    def halve(value):
        half = value.shape[0] // 2
        theirs = exchange(lax.dynamic_slice_in_dim(value, (1 - side) * half, half, 0), 1)
        return lax.dynamic_slice_in_dim(value, side * half, half, 0) + theirs

    def sum_over(value, move, first, size):
        rounded = value.astype(bf16)
        parts = [rounded if d == 0 else move(rounded, d) for d in range(0, size, first)]
        parts = [part.astype(f32) for part in parts]
        while len(parts) > 1:
            parts = [parts[i] + parts[i + 1] for i in range(0, len(parts), 2)]
        return parts[0]

    def digits(ids):
        lanes = features.shape[2]
        parts = [ids & 255, (ids >> 8) & 255, ids >> 16]
        rows = jnp.concatenate([part.reshape(-1, lanes) for part in parts], axis=0)
        return jnp.pad(rows, ((0, -rows.shape[0] % 16), (0, 0))).astype(bf16)

    def undo_digits(rows):
        count = own_rows // rows.shape[1]
        parts = [rows[i * count : (i + 1) * count].astype(jnp.int32) for i in range(3)]
        return (parts[0] + (parts[1] << 8) + (parts[2] << 16)).reshape(own_rows)

    member = lax.rem(blk_index, sections)
    place, count = tile_place[0, 0], tile_count[0, 0]
    width = features.shape[2]
    arrived = to_pieces(features[0])
    tiles = tile_values[0, 0]
    next_rep = lax.rem(rep_index + 1, reps)
    where = jnp.where(member < jnp.arange(sections + 1) - 1, next_rep, rep_index)
    where, count, arrived[0] = lax.optimization_barrier((where, count, arrived[0]))
    columns = [jnp.broadcast_to(where[0], (sections, 1)), where[1:, None], count[:, None], place]
    meta, late_ids = lax.optimization_barrier((jnp.concatenate(columns, axis=1), node_ids[0]))
    dense = build_dense(tiles, meta, own_rows, group_rows, False)
    feature_columns = jnp.concatenate(to_all(arrived, reps // 2), axis=0)
    chunks = dot(dense, feature_columns).reshape(reps, own_rows, width)
    arrived = [swap(chunks[delta], delta) for delta in range(1, reps)]
    total = chunks[0]
    for part in arrived:
        total = total + part
    z_input = total.astype(bf16)
    z_bundle = jnp.concatenate([z_input, digits(late_ids)], axis=0)
    pieces = to_all(to_pieces(z_bundle), 1)
    units = jnp.arange(hidden_width, dtype=jnp.int32)

    def kept_of(parts):
        ids = jnp.concatenate([undo_digits(part) for part in parts])
        return keep_mask(ids[:, None], units[None, :])

    rows = [part[own_rows:] for part in pieces]
    rows[:reps], pieces[reps] = lax.optimization_barrier((rows[:reps], pieces[reps]))
    kept_own, rows[-1] = lax.optimization_barrier((kept_of(rows[:reps]), rows[-1]))
    kept = jnp.concatenate([kept_own, kept_of(rows[reps:])], axis=0)
    z_columns = jnp.concatenate([part[:own_rows] for part in pieces], axis=0)
    kept, z_columns = lax.optimization_barrier((kept, z_columns))
    third = f32(4.0 / 3.0)
    pre_act = dot(z_columns, weight_in)
    dropped = (jnp.maximum(pre_act, 0.0) * (kept.astype(f32) * third)).astype(bf16)
    dropped, z_again = lax.optimization_barrier((dropped, z_columns))
    second = dot(dense, dropped)
    mask = jnp.where(dot(z_again, weight_in) > 0, kept, jnp.zeros_like(kept))
    mask, ready = lax.optimization_barrier((mask, second))
    sent = simple_call(
        encode_kernel,
        [jax.ShapeDtypeStruct((own_rows + HEAD_ROWS, hidden_width), jnp.int16)] * (reps - 1),
        "encode", second,
    )
    arrived = [swap(sent[d - 1], d) for d in range(1, reps)]
    classes = weight_out.shape[1]
    chunk = -(-classes // (16 * reps)) * 16
    spot = jnp.stack([side, rep_index])
    logits, out_total, *sent = simple_call(
        functools.partial(head_kernel, scale, reps),
        [
            jax.ShapeDtypeStruct((own_rows, classes), f32),
            jax.ShapeDtypeStruct((chunk, hidden_width), f32),
        ]
        + [jax.ShapeDtypeStruct((own_rows + chunk, hidden_width), bf16)] * reps,
        "head",
        weight_out.T, class_bias[None], labels, train_mask,
        ready, *arrived,
        spot=(spot,),
        scratch=[pltpu.VMEM((chunk * reps, hidden_width), f32)],
    )
    arrived = [swap(sent[d], d) for d in range(reps)]
    meta, out_total = lax.optimization_barrier((meta, out_total))
    turned = build_dense(tiles, meta, own_rows, group_rows, True)
    grad_block = jnp.concatenate([part[:own_rows] for part in arrived], axis=0)
    for part in arrived[1:]:
        out_total = out_total + part[own_rows:].astype(f32)
    grad_block, mask, out_total = lax.optimization_barrier((grad_block, mask, out_total))
    back = dot(turned, grad_block)
    pre_slope = (back * (mask.astype(f32) * third)).astype(bf16)
    pre_slope, out_total = lax.optimization_barrier((pre_slope, out_total))
    in_terms = lax.dot_general(
        z_columns, pre_slope, (((0,), (0,)), ((), ())), preferred_element_type=f32
    )
    half, piece = width // 2, chunk // 2

    def halves(which):
        rows = [
            lax.dynamic_slice_in_dim(in_terms, which * half, half, 0),
            lax.dynamic_slice_in_dim(out_total, which * piece, piece, 0),
        ]
        return jnp.concatenate(rows, axis=0)

    total = halves(side) + exchange(halves(1 - side), 1)
    total = sum_over(total, exchange, 2, blks).astype(bf16)
    arrived = [swap(total, d) for d in range(reps)]
    parts = [part[:half].astype(f32) for part in arrived]
    while len(parts) > 1:
        parts = [parts[i] + parts[i + 1] for i in range(0, len(parts), 2)]
    total = jnp.concatenate(parts + [part[half:].astype(f32) for part in arrived], axis=0)
    grad_in, grad_wide = simple_call(
        functools.partial(last_kernel, chunk),
        [
            jax.ShapeDtypeStruct((width, hidden_width), f32),
            jax.ShapeDtypeStruct((classes, hidden_width), f32),
        ],
        "last", total, exchange(total, 1), spot=(spot,),
    )
    grad_out = grad_wide.T
    return (logits[None], grad_in, grad_out)


def solution(mesh):
    placed = (
        P("blk", "rep", None),
        P("blk", "rep"),
        P("blk", "rep"),
        P("blk", "rep"),
        P("blk", "rep", None, None, None, None),
        P("blk", "rep", None, None),
        P("blk", "rep", None),
        P(),
        P(),
        P(),
    )
    return jax.shard_map(
        on_device,
        mesh=mesh,
        in_specs=placed,
        out_specs=(P("blk", "rep", None), P(), P()),
        check_vma=False,
    )
```

```python
import functools
import math

import jax
import jax.numpy as jnp
from jax import lax
from jax.experimental import pallas as pl
from jax.experimental.pallas import tpu as pltpu
from jax.sharding import PartitionSpec as P


LEVELS = 32767.0
MANTISSA_BITS = 14
HEAD_ROWS = 16


def keep_mask(id_values, unit_values):
    mixed = id_values * 73244475 + unit_values * 19349663 + 12345
    mixed = mixed ^ jnp.right_shift(mixed, 15)
    mixed = mixed * 40503
    mixed = mixed ^ jnp.right_shift(mixed, 13)
    return (jnp.bitwise_and(mixed, 3) != 0).astype(jnp.bfloat16)


def eye_of(count):
    rows = lax.broadcasted_iota(jnp.int32, (count, count), 0)
    columns = lax.broadcasted_iota(jnp.int32, (count, count), 1)
    return rows == columns


def dot(left, right):
    return jnp.dot(left, right, preferred_element_type=jnp.float32)


def dot_wide(left, right):
    return lax.dot_general(
        left, right, (((1,), (1,)), ((), ())), preferred_element_type=jnp.float32
    )


def encode(values):
    rows, width = values.shape
    largest = jnp.maximum(jnp.max(jnp.abs(values), axis=1, keepdims=True), 1e-30)
    power = jnp.ceil(jnp.log2(largest))
    mantissa = jnp.ceil(largest * jnp.exp2(MANTISSA_BITS - power))
    scale = mantissa * jnp.exp2(power - MANTISSA_BITS)
    coded = jnp.clip(jnp.round(values * (LEVELS / scale)), -LEVELS, LEVELS)
    square = eye_of(width)
    index = lax.broadcasted_iota(jnp.int32, (HEAD_ROWS, width), 0)
    head = jnp.zeros((HEAD_ROWS, width), jnp.float32)
    for part in range(rows // width):
        for offset, column in enumerate((power, mantissa)):
            column = column[part * width : (part + 1) * width]
            line = jnp.sum(jnp.where(square, column, 0.0), axis=0, keepdims=True)
            head = jnp.where(index == 2 * part + offset, line, head)
    whole = jnp.concatenate([coded, head], axis=0)
    return whole.astype(jnp.int32).astype(jnp.int16)


def decode(coded):
    whole = coded.astype(jnp.int32).astype(jnp.float32)
    rows, width = whole.shape[0] - HEAD_ROWS, whole.shape[1]
    square = eye_of(width)
    columns = [[], []]
    for part in range(rows // width):
        for offset in range(2):
            start = rows + 2 * part + offset
            line = whole[start : start + 1]
            columns[offset].append(jnp.sum(jnp.where(square, line, 0.0), axis=1, keepdims=True))
    power, mantissa = (jnp.concatenate(parts, axis=0) for parts in columns)
    return whole[:rows] * (mantissa * jnp.exp2(power - MANTISSA_BITS) * (1.0 / LEVELS))


def encode_kernel(partial_ref, *coded_refs):
    own_rows = partial_ref.shape[0] // (len(coded_refs) + 1)
    for delta, coded_ref in enumerate(coded_refs, 1):
        coded_ref[...] = encode(partial_ref[delta * own_rows : (delta + 1) * own_rows, :])


def last_kernel(chunk, spot_ref, total_ref, other_ref, grad_in_ref, grad_out_ref):
    side, rep_index = spot_ref[0], spot_ref[1]
    half = grad_in_ref.shape[0] // 2
    piece = chunk // 2
    classes = grad_out_ref.shape[0]
    reps = (total_ref.shape[0] - half) // piece
    for part in range(2):

        def take(start, size):
            rows = pl.ds(start, size)
            return jnp.where(side == part, total_ref[rows, :], other_ref[rows, :])

        grad_in_ref[part * half : (part + 1) * half, :] = take(0, half)
        for r in range(reps):
            start = r * chunk + part * piece
            size = min(piece, classes - start)
            if size > 0:
                spot = pl.multiple_of(half + (r ^ rep_index) * piece, 8)
                grad_out_ref[start : start + size, :] = take(spot, piece)[:size]


def head_kernel(
    scale, reps, spot_ref, weight_ref, bias_ref, label_ref, mask_ref, own_ref, *refs
):
    coded_refs, refs = refs[: reps - 1], refs[reps - 1 :]
    logits_ref, own_terms_ref, sent_refs, terms_ref = refs[0], refs[1], refs[2:-1], refs[-1]
    own_rows, classes = logits_ref.shape
    total = own_ref[:own_rows, :]
    for coded_ref in coded_refs:
        total += decode(coded_ref[...])
    z_output = total.astype(jnp.bfloat16)
    square = eye_of(own_rows)
    label, mask = (
        jnp.sum(jnp.where(square, ref[...].astype(jnp.float32), 0.0), axis=1, keepdims=True)
        for ref in (label_ref, mask_ref)
    )
    logits = dot_wide(z_output, weight_ref[...]) + bias_ref[...]
    logits_ref[...] = logits
    shifted = jnp.exp(logits - jnp.max(logits, axis=1, keepdims=True))
    likelihood = shifted / jnp.sum(shifted, axis=1, keepdims=True)
    onehot = label.astype(jnp.int32) == lax.broadcasted_iota(jnp.int32, logits.shape, 1)
    slope = (likelihood - onehot.astype(jnp.float32)) * mask * scale
    slope = slope.astype(jnp.bfloat16)
    grad_rows = dot(slope, weight_ref[...]).astype(jnp.bfloat16)
    terms = lax.dot_general(
        slope, z_output, (((0,), (0,)), ((), ())), preferred_element_type=jnp.float32
    )
    terms_ref[:classes, :] = terms
    pad = terms_ref.shape[0] - classes
    if pad:
        terms_ref[classes:, :] = jnp.zeros((pad, terms.shape[1]), jnp.float32)
    chunk = own_terms_ref.shape[0]
    for delta, sent_ref in enumerate(sent_refs):
        start = pl.multiple_of((spot_ref[1] ^ delta) * chunk, 8)
        piece = terms_ref[pl.ds(start, chunk), :]
        sent_ref[:own_rows, :] = grad_rows
        sent_ref[own_rows:, :] = piece.astype(jnp.bfloat16)
        if delta == 0:
            own_terms_ref[...] = piece


def simple_call(body, shapes, name, *values, spot=(), scratch=()):
    smem = pl.BlockSpec(memory_space=pltpu.SMEM)
    vmem = pl.BlockSpec(memory_space=pltpu.VMEM)
    return pl.pallas_call(
        body,
        in_specs=[smem] * len(spot) + [vmem] * len(values),
        out_shape=shapes,
        scratch_shapes=scratch,
        compiler_params=pltpu.CompilerParams(vmem_limit_bytes=8 * 1024 * 1024),
        name=name,
    )(*spot, *values)


def dense_kernel(per_rep, tile_side, turn, meta_ref, tiles_ref, dense_ref):
    section = pl.program_id(0)
    rep_index, source_rep = meta_ref[section, 0], meta_ref[section, 1]
    edge = tiles_ref.shape[-1]
    dense_ref[...] = jnp.zeros_like(dense_ref)

    def put(slot, carried):
        place = meta_ref[section, 3 + slot]
        row = place // tile_side
        column = place % tile_side
        row = ((row // per_rep) ^ rep_index) * per_rep + row % per_rep
        column = ((column // per_rep) ^ source_rep) * per_rep + column % per_rep
        rows = pl.ds(pl.multiple_of(row * edge, edge), edge)
        columns = pl.ds(pl.multiple_of(column * edge, edge), edge)
        tile = tiles_ref[0, slot]
        if turn:
            dense_ref[columns, rows] = tile.T
        else:
            dense_ref[rows, columns] = tile
        return carried

    lax.fori_loop(0, meta_ref[section, 2], put, 0)


def build_dense(tiles, meta, own_rows, group_rows, turn):
    sections, slots, edge, _ = tiles.shape
    body = functools.partial(dense_kernel, own_rows // edge, group_rows // edge, turn)
    block = (group_rows, group_rows)
    shape = (sections * group_rows, group_rows) if turn else (group_rows, sections * group_rows)
    return pl.pallas_call(
        body,
        grid_spec=pltpu.PrefetchScalarGridSpec(
            num_scalar_prefetch=1,
            grid=(sections,),
            in_specs=[pl.BlockSpec((1, slots, edge, edge), lambda p, *_: (p, 0, 0, 0))],
            out_specs=pl.BlockSpec(block, lambda p, *_: (p, 0) if turn else (0, p)),
        ),
        out_shape=jax.ShapeDtypeStruct(shape, tiles.dtype),
        compiler_params=pltpu.CompilerParams(
            vmem_limit_bytes=4 * group_rows**2 + 8 * slots * edge**2 + (2 << 20)
        ),
        cost_estimate=pl.CostEstimate(
            flops=0, bytes_accessed=4 * sections * group_rows * group_rows, transcendentals=0
        ),
        name="dense_turned" if turn else "dense",
    )(meta, tiles)


def on_device(
    features,
    node_ids,
    labels,
    train_mask,
    tile_values,
    tile_place,
    tile_count,
    weight_in,
    weight_out,
    class_bias,
):
    own_rows = features.shape[1]
    reps = lax.axis_size("rep")
    blks = lax.axis_size("blk")
    rep_index = lax.axis_index("rep")
    blk_index = lax.axis_index("blk")
    sections = tile_values.shape[2]
    group_rows = own_rows * reps
    hidden_width = weight_in.shape[1]
    scale = 1.0 / math.sqrt(group_rows * blks)
    f32 = jnp.float32
    bf16 = jnp.bfloat16

    def swap(value, delta):
        if delta == 0:
            return value
        return lax.ppermute(value, "rep", [(r, r ^ delta) for r in range(reps)])

    def to_section(block, j):
        pairs = []
        for r in range(reps):
            for c in range(blks):
                member = c % sections + j
                if member < sections:
                    pairs.append((r * blks + c, r * blks + c + j))
                else:
                    pairs.append((r * blks + c, (r - 1) % reps * blks + c + j - sections))
        return lax.ppermute(block, ("rep", "blk"), pairs)

    def exchange(value, delta):
        return lax.ppermute(value, "blk", [(c, c ^ delta) for c in range(blks)])

    def to_pieces(value):
        pieces = []
        for delta in range(reps):
            pairs = []
            for r in range(reps):
                for c in range(blks):
                    target = r ^ delta
                    pairs.append((r * blks + c, target * blks + (c + sections * target) % blks))
            pieces.append(lax.ppermute(value, ("rep", "blk"), pairs))
        return pieces

    def to_all(pieces, size):
        parts = [
            jnp.concatenate(pieces[start : start + size], axis=0)
            for start in range(0, reps, size)
        ]
        blocks = list(parts)
        for j in range(1, sections):
            blocks += [to_section(part, j) for part in parts]
        return blocks

    side = lax.rem(blk_index, 2)

    def halve(value):
        half = value.shape[0] // 2
        theirs = exchange(lax.dynamic_slice_in_dim(value, (1 - side) * half, half, 0), 1)
        return lax.dynamic_slice_in_dim(value, side * half, half, 0) + theirs

    def sum_over(value, move, first, size):
        rounded = value.astype(bf16)
        parts = [rounded if d == 0 else move(rounded, d) for d in range(0, size, first)]
        parts = [part.astype(f32) for part in parts]
        while len(parts) > 1:
            parts = [parts[i] + parts[i + 1] for i in range(0, len(parts), 2)]
        return parts[0]

    def digits(ids):
        lanes = features.shape[2]
        parts = [ids & 255, (ids >> 8) & 255, ids >> 16]
        rows = jnp.concatenate([part.reshape(-1, lanes) for part in parts], axis=0)
        return jnp.pad(rows, ((0, -rows.shape[0] % 16), (0, 0))).astype(bf16)

    def undo_digits(rows):
        count = own_rows // rows.shape[1]
        parts = [rows[i * count : (i + 1) * count].astype(jnp.int32) for i in range(3)]
        return (parts[0] + (parts[1] << 8) + (parts[2] << 16)).reshape(own_rows)

    member = lax.rem(blk_index, sections)
    place, count = tile_place[0, 0], tile_count[0, 0]
    width = features.shape[2]
    arrived = to_pieces(features[0])
    tiles = tile_values[0, 0]
    next_rep = lax.rem(rep_index + 1, reps)
    where = jnp.where(member < jnp.arange(sections + 1) - 1, next_rep, rep_index)
    where, count, arrived[0] = lax.optimization_barrier((where, count, arrived[0]))
    columns = [jnp.broadcast_to(where[0], (sections, 1)), where[1:, None], count[:, None], place]
    meta, late_ids = lax.optimization_barrier((jnp.concatenate(columns, axis=1), node_ids[0]))
    dense = build_dense(tiles, meta, own_rows, group_rows, False)
    feature_columns = jnp.concatenate(to_all(arrived, reps // 2), axis=0)
    chunks = dot(dense, feature_columns).reshape(reps, own_rows, width)
    far_first = range(reps - 1, 0, -1)
    arrived = [swap(chunks[delta], delta) for delta in far_first]
    total = chunks[0]
    for part in arrived:
        total = total + part
    z_input = total.astype(bf16)
    z_bundle = jnp.concatenate([z_input, digits(late_ids)], axis=0)
    pieces = to_all(to_pieces(z_bundle), 1)
    units = jnp.arange(hidden_width, dtype=jnp.int32)

    def kept_of(parts):
        ids = jnp.concatenate([undo_digits(part) for part in parts])
        return keep_mask(ids[:, None], units[None, :])

    rows = [part[own_rows:] for part in pieces]
    rows[:reps], pieces[reps] = lax.optimization_barrier((rows[:reps], pieces[reps]))
    kept_own, rows[-1] = lax.optimization_barrier((kept_of(rows[:reps]), rows[-1]))
    kept = jnp.concatenate([kept_own, kept_of(rows[reps:])], axis=0)
    z_columns = jnp.concatenate([part[:own_rows] for part in pieces], axis=0)
    kept, z_columns = lax.optimization_barrier((kept, z_columns))
    third = f32(4.0 / 3.0)
    pre_act = dot(z_columns, weight_in)
    dropped = (jnp.maximum(pre_act, 0.0) * (kept.astype(f32) * third)).astype(bf16)
    dropped, z_again = lax.optimization_barrier((dropped, z_columns))
    second = dot(dense, dropped)
    mask = jnp.where(dot(z_again, weight_in) > 0, kept, jnp.zeros_like(kept))
    mask, ready = lax.optimization_barrier((mask, second))
    sent = simple_call(
        encode_kernel,
        [jax.ShapeDtypeStruct((own_rows + HEAD_ROWS, hidden_width), jnp.int16)] * (reps - 1),
        "encode", second,
    )
    arrived = [swap(sent[d - 1], d) for d in far_first]
    classes = weight_out.shape[1]
    chunk = -(-classes // (16 * reps)) * 16
    spot = jnp.stack([side, rep_index])
    logits, out_total, *sent = simple_call(
        functools.partial(head_kernel, scale, reps),
        [
            jax.ShapeDtypeStruct((own_rows, classes), f32),
            jax.ShapeDtypeStruct((chunk, hidden_width), f32),
        ]
        + [jax.ShapeDtypeStruct((own_rows + chunk, hidden_width), bf16)] * reps,
        "head",
        weight_out.T, class_bias[None], labels, train_mask,
        ready, *arrived,
        spot=(spot,),
        scratch=[pltpu.VMEM((chunk * reps, hidden_width), f32)],
    )
    arrived = [swap(sent[d], d) for d in range(reps - 1, -1, -1)][::-1]
    meta, out_total = lax.optimization_barrier((meta, out_total))
    turned = build_dense(tiles, meta, own_rows, group_rows, True)
    grad_block = jnp.concatenate([part[:own_rows] for part in arrived], axis=0)
    for part in arrived[1:]:
        out_total = out_total + part[own_rows:].astype(f32)
    grad_block, mask, out_total = lax.optimization_barrier((grad_block, mask, out_total))
    back = dot(turned, grad_block)
    pre_slope = (back * (mask.astype(f32) * third)).astype(bf16)
    pre_slope, out_total = lax.optimization_barrier((pre_slope, out_total))
    in_terms = lax.dot_general(
        z_columns, pre_slope, (((0,), (0,)), ((), ())), preferred_element_type=f32
    )
    half, piece = width // 2, chunk // 2

    def halves(which):
        rows = [
            lax.dynamic_slice_in_dim(in_terms, which * half, half, 0),
            lax.dynamic_slice_in_dim(out_total, which * piece, piece, 0),
        ]
        return jnp.concatenate(rows, axis=0)

    total = halves(side) + exchange(halves(1 - side), 1)
    total = sum_over(total, exchange, 2, blks).astype(bf16)
    arrived = [swap(total, d) for d in range(reps - 1, -1, -1)][::-1]
    parts = [part[:half].astype(f32) for part in arrived]
    while len(parts) > 1:
        parts = [parts[i] + parts[i + 1] for i in range(0, len(parts), 2)]
    total = jnp.concatenate(parts + [part[half:].astype(f32) for part in arrived], axis=0)
    grad_in, grad_wide = simple_call(
        functools.partial(last_kernel, chunk),
        [
            jax.ShapeDtypeStruct((width, hidden_width), f32),
            jax.ShapeDtypeStruct((classes, hidden_width), f32),
        ],
        "last", total, exchange(total, 1), spot=(spot,),
    )
    grad_out = grad_wide.T
    return (logits[None], grad_in, grad_out)


def solution(mesh):
    placed = (
        P("blk", "rep", None),
        P("blk", "rep"),
        P("blk", "rep"),
        P("blk", "rep"),
        P("blk", "rep", None, None, None, None),
        P("blk", "rep", None, None),
        P("blk", "rep", None),
        P(),
        P(),
        P(),
    )
    return jax.shard_map(
        on_device,
        mesh=mesh,
        in_specs=placed,
        out_specs=(P("blk", "rep", None), P(), P()),
        check_vma=False,
    )
```

```python
import functools
import math

import jax
import jax.numpy as jnp
from jax import lax
from jax.experimental import pallas as pl
from jax.experimental.pallas import tpu as pltpu
from jax.sharding import PartitionSpec as P


LEVELS = 32767.0
MANTISSA_BITS = 14
HEAD_ROWS = 16


def keep_mask(id_values, unit_values):
    mixed = id_values * 73244475 + unit_values * 19349663 + 12345
    mixed = mixed ^ jnp.right_shift(mixed, 15)
    mixed = mixed * 40503
    mixed = mixed ^ jnp.right_shift(mixed, 13)
    return (jnp.bitwise_and(mixed, 3) != 0).astype(jnp.bfloat16)


def eye_of(count):
    rows = lax.broadcasted_iota(jnp.int32, (count, count), 0)
    columns = lax.broadcasted_iota(jnp.int32, (count, count), 1)
    return rows == columns


def dot(left, right):
    return jnp.dot(left, right, preferred_element_type=jnp.float32)


def dot_wide(left, right):
    return lax.dot_general(
        left, right, (((1,), (1,)), ((), ())), preferred_element_type=jnp.float32
    )


def encode(values):
    rows, width = values.shape
    largest = jnp.maximum(jnp.max(jnp.abs(values), axis=1, keepdims=True), 1e-30)
    power = jnp.ceil(jnp.log2(largest))
    mantissa = jnp.ceil(largest * jnp.exp2(MANTISSA_BITS - power))
    scale = mantissa * jnp.exp2(power - MANTISSA_BITS)
    coded = jnp.clip(jnp.round(values * (LEVELS / scale)), -LEVELS, LEVELS)
    square = eye_of(width)
    index = lax.broadcasted_iota(jnp.int32, (HEAD_ROWS, width), 0)
    head = jnp.zeros((HEAD_ROWS, width), jnp.float32)
    for part in range(rows // width):
        for offset, column in enumerate((power, mantissa)):
            column = column[part * width : (part + 1) * width]
            line = jnp.sum(jnp.where(square, column, 0.0), axis=0, keepdims=True)
            head = jnp.where(index == 2 * part + offset, line, head)
    whole = jnp.concatenate([coded, head], axis=0)
    return whole.astype(jnp.int32).astype(jnp.int16)


def decode(coded):
    whole = coded.astype(jnp.int32).astype(jnp.float32)
    rows, width = whole.shape[0] - HEAD_ROWS, whole.shape[1]
    square = eye_of(width)
    columns = [[], []]
    for part in range(rows // width):
        for offset in range(2):
            start = rows + 2 * part + offset
            line = whole[start : start + 1]
            columns[offset].append(jnp.sum(jnp.where(square, line, 0.0), axis=1, keepdims=True))
    power, mantissa = (jnp.concatenate(parts, axis=0) for parts in columns)
    return whole[:rows] * (mantissa * jnp.exp2(power - MANTISSA_BITS) * (1.0 / LEVELS))


def encode_kernel(partial_ref, *coded_refs):
    own_rows = partial_ref.shape[0] // (len(coded_refs) + 1)
    for delta, coded_ref in enumerate(coded_refs, 1):
        coded_ref[...] = encode(partial_ref[delta * own_rows : (delta + 1) * own_rows, :])


def last_kernel(chunk, spot_ref, total_ref, other_ref, grad_in_ref, grad_out_ref):
    side, rep_index = spot_ref[0], spot_ref[1]
    half = grad_in_ref.shape[0] // 2
    piece = chunk // 2
    classes = grad_out_ref.shape[0]
    reps = (total_ref.shape[0] - half) // piece
    for part in range(2):

        def take(start, size):
            rows = pl.ds(start, size)
            return jnp.where(side == part, total_ref[rows, :], other_ref[rows, :])

        grad_in_ref[part * half : (part + 1) * half, :] = take(0, half)
        for r in range(reps):
            start = r * chunk + part * piece
            size = min(piece, classes - start)
            if size > 0:
                spot = pl.multiple_of(half + (r ^ rep_index) * piece, 8)
                grad_out_ref[start : start + size, :] = take(spot, piece)[:size]


def head_kernel(
    scale, reps, spot_ref, weight_ref, bias_ref, label_ref, mask_ref, own_ref, *refs
):
    coded_refs, refs = refs[: reps - 1], refs[reps - 1 :]
    logits_ref, own_terms_ref, sent_refs, terms_ref = refs[0], refs[1], refs[2:-1], refs[-1]
    own_rows, classes = logits_ref.shape
    total = own_ref[:own_rows, :]
    for coded_ref in coded_refs:
        total += decode(coded_ref[...])
    z_output = total.astype(jnp.bfloat16)
    square = eye_of(own_rows)
    label, mask = (
        jnp.sum(jnp.where(square, ref[...].astype(jnp.float32), 0.0), axis=1, keepdims=True)
        for ref in (label_ref, mask_ref)
    )
    logits = dot_wide(z_output, weight_ref[...]) + bias_ref[...]
    logits_ref[...] = logits
    shifted = jnp.exp(logits - jnp.max(logits, axis=1, keepdims=True))
    likelihood = shifted / jnp.sum(shifted, axis=1, keepdims=True)
    onehot = label.astype(jnp.int32) == lax.broadcasted_iota(jnp.int32, logits.shape, 1)
    slope = (likelihood - onehot.astype(jnp.float32)) * mask * scale
    slope = slope.astype(jnp.bfloat16)
    grad_rows = dot(slope, weight_ref[...]).astype(jnp.bfloat16)
    terms = lax.dot_general(
        slope, z_output, (((0,), (0,)), ((), ())), preferred_element_type=jnp.float32
    )
    terms_ref[:classes, :] = terms
    pad = terms_ref.shape[0] - classes
    if pad:
        terms_ref[classes:, :] = jnp.zeros((pad, terms.shape[1]), jnp.float32)
    chunk = own_terms_ref.shape[0]
    for delta, sent_ref in enumerate(sent_refs):
        start = pl.multiple_of((spot_ref[1] ^ delta) * chunk, 8)
        piece = terms_ref[pl.ds(start, chunk), :]
        sent_ref[:own_rows, :] = grad_rows
        sent_ref[own_rows:, :] = piece.astype(jnp.bfloat16)
        if delta == 0:
            own_terms_ref[...] = piece


def simple_call(body, shapes, name, *values, spot=(), scratch=()):
    smem = pl.BlockSpec(memory_space=pltpu.SMEM)
    vmem = pl.BlockSpec(memory_space=pltpu.VMEM)
    return pl.pallas_call(
        body,
        in_specs=[smem] * len(spot) + [vmem] * len(values),
        out_shape=shapes,
        scratch_shapes=scratch,
        compiler_params=pltpu.CompilerParams(vmem_limit_bytes=8 * 1024 * 1024),
        name=name,
    )(*spot, *values)


def dense_kernel(per_rep, tile_side, turn, meta_ref, tiles_ref, dense_ref):
    section = pl.program_id(0)
    rep_index, source_rep = meta_ref[section, 0], meta_ref[section, 1]
    edge = tiles_ref.shape[-1]
    dense_ref[...] = jnp.zeros_like(dense_ref)

    def put(slot, carried):
        place = meta_ref[section, 3 + slot]
        row = place // tile_side
        column = place % tile_side
        row = ((row // per_rep) ^ rep_index) * per_rep + row % per_rep
        column = ((column // per_rep) ^ source_rep) * per_rep + column % per_rep
        rows = pl.ds(pl.multiple_of(row * edge, edge), edge)
        columns = pl.ds(pl.multiple_of(column * edge, edge), edge)
        tile = tiles_ref[0, slot]
        if turn:
            dense_ref[columns, rows] = tile.T
        else:
            dense_ref[rows, columns] = tile
        return carried

    lax.fori_loop(0, meta_ref[section, 2], put, 0)


def build_dense(tiles, meta, own_rows, group_rows, turn):
    sections, slots, edge, _ = tiles.shape
    body = functools.partial(dense_kernel, own_rows // edge, group_rows // edge, turn)
    block = (group_rows, group_rows)
    shape = (sections * group_rows, group_rows) if turn else (group_rows, sections * group_rows)
    return pl.pallas_call(
        body,
        grid_spec=pltpu.PrefetchScalarGridSpec(
            num_scalar_prefetch=1,
            grid=(sections,),
            in_specs=[pl.BlockSpec((1, slots, edge, edge), lambda p, *_: (p, 0, 0, 0))],
            out_specs=pl.BlockSpec(block, lambda p, *_: (p, 0) if turn else (0, p)),
        ),
        out_shape=jax.ShapeDtypeStruct(shape, tiles.dtype),
        compiler_params=pltpu.CompilerParams(
            vmem_limit_bytes=4 * group_rows**2 + 8 * slots * edge**2 + (2 << 20)
        ),
        cost_estimate=pl.CostEstimate(
            flops=0, bytes_accessed=4 * sections * group_rows * group_rows, transcendentals=0
        ),
        name="dense_turned" if turn else "dense",
    )(meta, tiles)


def on_device(
    features,
    node_ids,
    labels,
    train_mask,
    tile_values,
    tile_place,
    tile_count,
    weight_in,
    weight_out,
    class_bias,
):
    own_rows = features.shape[1]
    reps = lax.axis_size("rep")
    blks = lax.axis_size("blk")
    rep_index = lax.axis_index("rep")
    blk_index = lax.axis_index("blk")
    sections = tile_values.shape[2]
    group_rows = own_rows * reps
    hidden_width = weight_in.shape[1]
    scale = 1.0 / math.sqrt(group_rows * blks)
    f32 = jnp.float32
    bf16 = jnp.bfloat16

    def swap(value, delta):
        if delta == 0:
            return value
        return lax.ppermute(value, "rep", [(r, r ^ delta) for r in range(reps)])

    def to_section(block, j):
        pairs = []
        for r in range(reps):
            for c in range(blks):
                member = c % sections + j
                if member < sections:
                    pairs.append((r * blks + c, r * blks + c + j))
                else:
                    pairs.append((r * blks + c, (r - 1) % reps * blks + c + j - sections))
        return lax.ppermute(block, ("rep", "blk"), pairs)

    def exchange(value, delta):
        return lax.ppermute(value, "blk", [(c, c ^ delta) for c in range(blks)])

    def to_pieces(value):
        pieces = []
        for delta in range(reps):
            pairs = []
            for r in range(reps):
                for c in range(blks):
                    target = r ^ delta
                    pairs.append((r * blks + c, target * blks + (c + sections * target) % blks))
            pieces.append(lax.ppermute(value, ("rep", "blk"), pairs))
        return pieces

    def to_all(pieces, size):
        parts = [
            jnp.concatenate(pieces[start : start + size], axis=0)
            for start in range(0, reps, size)
        ]
        blocks = list(parts)
        for j in range(1, sections):
            blocks += [to_section(part, j) for part in parts]
        return blocks

    side = lax.rem(blk_index, 2)

    def halve(value):
        half = value.shape[0] // 2
        theirs = exchange(lax.dynamic_slice_in_dim(value, (1 - side) * half, half, 0), 1)
        return lax.dynamic_slice_in_dim(value, side * half, half, 0) + theirs

    def sum_over(value, move, first, size):
        rounded = value.astype(bf16)
        parts = [rounded if d == 0 else move(rounded, d) for d in range(0, size, first)]
        parts = [part.astype(f32) for part in parts]
        while len(parts) > 1:
            parts = [parts[i] + parts[i + 1] for i in range(0, len(parts), 2)]
        return parts[0]

    def digits(ids):
        lanes = features.shape[2]
        parts = [ids & 255, (ids >> 8) & 255, ids >> 16]
        rows = jnp.concatenate([part.reshape(-1, lanes) for part in parts], axis=0)
        return jnp.pad(rows, ((0, -rows.shape[0] % 16), (0, 0))).astype(bf16)

    def undo_digits(rows):
        count = own_rows // rows.shape[1]
        parts = [rows[i * count : (i + 1) * count].astype(jnp.int32) for i in range(3)]
        return (parts[0] + (parts[1] << 8) + (parts[2] << 16)).reshape(own_rows)

    member = lax.rem(blk_index, sections)
    place, count = tile_place[0, 0], tile_count[0, 0]
    width = features.shape[2]
    arrived = to_pieces(features[0])
    tiles = tile_values[0, 0]
    next_rep = lax.rem(rep_index + 1, reps)
    where = jnp.where(member < jnp.arange(sections + 1) - 1, next_rep, rep_index)
    where, count, arrived[0] = lax.optimization_barrier((where, count, arrived[0]))
    columns = [jnp.broadcast_to(where[0], (sections, 1)), where[1:, None], count[:, None], place]
    meta, late_ids = lax.optimization_barrier((jnp.concatenate(columns, axis=1), node_ids[0]))
    dense = build_dense(tiles, meta, own_rows, group_rows, False)
    feature_columns = jnp.concatenate(to_all(arrived, reps // 2), axis=0)
    chunks = dot(dense, feature_columns).reshape(reps, own_rows, width)
    far_first = range(reps - 1, 0, -1)
    arrived = [swap(chunks[delta], delta) for delta in far_first]
    total = chunks[0]
    for part in arrived:
        total = total + part
    z_input = total.astype(bf16)
    z_bundle = jnp.concatenate([z_input, digits(late_ids)], axis=0)
    pieces = to_all(to_pieces(z_bundle), 1)
    units = jnp.arange(hidden_width, dtype=jnp.int32)

    def kept_of(parts):
        ids = jnp.concatenate([undo_digits(part) for part in parts])
        return keep_mask(ids[:, None], units[None, :])

    rows = [part[own_rows:] for part in pieces]
    rows[:reps], pieces[reps] = lax.optimization_barrier((rows[:reps], pieces[reps]))
    kept_own, rows[-1] = lax.optimization_barrier((kept_of(rows[:reps]), rows[-1]))
    kept = jnp.concatenate([kept_own, kept_of(rows[reps:])], axis=0)
    z_columns = jnp.concatenate([part[:own_rows] for part in pieces], axis=0)
    kept, z_columns = lax.optimization_barrier((kept, z_columns))
    third = f32(4.0 / 3.0)
    pre_act = dot(z_columns, weight_in)
    dropped = (jnp.maximum(pre_act, 0.0) * (kept.astype(f32) * third)).astype(bf16)
    dropped, z_again = lax.optimization_barrier((dropped, z_columns))
    second = dot(dense, dropped)
    mask = jnp.where(dot(z_again, weight_in) > 0, kept, jnp.zeros_like(kept))
    mask, ready = lax.optimization_barrier((mask, second))
    sent = simple_call(
        encode_kernel,
        [jax.ShapeDtypeStruct((own_rows + HEAD_ROWS, hidden_width), jnp.int16)] * (reps - 1),
        "encode", second,
    )
    arrived = [swap(sent[d - 1], d) for d in far_first]
    classes = weight_out.shape[1]
    chunk = -(-classes // (16 * reps)) * 16
    spot = jnp.stack([side, rep_index])
    logits, out_total, *sent = simple_call(
        functools.partial(head_kernel, scale, reps),
        [
            jax.ShapeDtypeStruct((own_rows, classes), f32),
            jax.ShapeDtypeStruct((chunk, hidden_width), f32),
        ]
        + [jax.ShapeDtypeStruct((own_rows + chunk, hidden_width), bf16)] * reps,
        "head",
        weight_out.T, class_bias[None], labels, train_mask,
        ready, *arrived,
        spot=(spot,),
        scratch=[pltpu.VMEM((chunk * reps, hidden_width), f32)],
    )
    arrived = lax.optimization_barrier([swap(sent[d], d) for d in far_first]) + [sent[0]]
    arrived = arrived[::-1]
    meta, out_total = lax.optimization_barrier((meta, out_total))
    turned = build_dense(tiles, meta, own_rows, group_rows, True)
    grad_block = jnp.concatenate([part[:own_rows] for part in arrived], axis=0)
    for part in arrived[1:]:
        out_total = out_total + part[own_rows:].astype(f32)
    grad_block, mask, out_total = lax.optimization_barrier((grad_block, mask, out_total))
    back = dot(turned, grad_block)
    pre_slope = (back * (mask.astype(f32) * third)).astype(bf16)
    pre_slope, out_total = lax.optimization_barrier((pre_slope, out_total))
    in_terms = lax.dot_general(
        z_columns, pre_slope, (((0,), (0,)), ((), ())), preferred_element_type=f32
    )
    half, piece = width // 2, chunk // 2

    def halves(which):
        rows = [
            lax.dynamic_slice_in_dim(in_terms, which * half, half, 0),
            lax.dynamic_slice_in_dim(out_total, which * piece, piece, 0),
        ]
        return jnp.concatenate(rows, axis=0)

    total = halves(side) + exchange(halves(1 - side), 1)
    total = sum_over(total, exchange, 2, blks).astype(bf16)
    arrived = lax.optimization_barrier([swap(total, d) for d in far_first]) + [total]
    arrived = arrived[::-1]
    parts = [part[:half].astype(f32) for part in arrived]
    while len(parts) > 1:
        parts = [parts[i] + parts[i + 1] for i in range(0, len(parts), 2)]
    total = jnp.concatenate(parts + [part[half:].astype(f32) for part in arrived], axis=0)
    grad_in, grad_wide = simple_call(
        functools.partial(last_kernel, chunk),
        [
            jax.ShapeDtypeStruct((width, hidden_width), f32),
            jax.ShapeDtypeStruct((classes, hidden_width), f32),
        ],
        "last", total, exchange(total, 1), spot=(spot,),
    )
    grad_out = grad_wide.T
    return (logits[None], grad_in, grad_out)


def solution(mesh):
    placed = (
        P("blk", "rep", None),
        P("blk", "rep"),
        P("blk", "rep"),
        P("blk", "rep"),
        P("blk", "rep", None, None, None, None),
        P("blk", "rep", None, None),
        P("blk", "rep", None),
        P(),
        P(),
        P(),
    )
    return jax.shard_map(
        on_device,
        mesh=mesh,
        in_specs=placed,
        out_specs=(P("blk", "rep", None), P(), P()),
        check_vma=False,
    )
```

```python
import functools
import math

import jax
import jax.numpy as jnp
from jax import lax
from jax.experimental import pallas as pl
from jax.experimental.pallas import tpu as pltpu
from jax.sharding import PartitionSpec as P


LEVELS = 32767.0
MANTISSA_BITS = 14
HEAD_ROWS = 16


def keep_mask(id_values, unit_values):
    mixed = id_values * 73244475 + unit_values * 19349663 + 12345
    mixed = mixed ^ jnp.right_shift(mixed, 15)
    mixed = mixed * 40503
    mixed = mixed ^ jnp.right_shift(mixed, 13)
    return (jnp.bitwise_and(mixed, 3) != 0).astype(jnp.bfloat16)


def eye_of(count):
    rows = lax.broadcasted_iota(jnp.int32, (count, count), 0)
    columns = lax.broadcasted_iota(jnp.int32, (count, count), 1)
    return rows == columns


def dot(left, right):
    return jnp.dot(left, right, preferred_element_type=jnp.float32)


def dot_wide(left, right):
    return lax.dot_general(
        left, right, (((1,), (1,)), ((), ())), preferred_element_type=jnp.float32
    )


def encode(values):
    rows, width = values.shape
    largest = jnp.maximum(jnp.max(jnp.abs(values), axis=1, keepdims=True), 1e-30)
    power = jnp.ceil(jnp.log2(largest))
    mantissa = jnp.ceil(largest * jnp.exp2(MANTISSA_BITS - power))
    scale = mantissa * jnp.exp2(power - MANTISSA_BITS)
    coded = jnp.clip(jnp.round(values * (LEVELS / scale)), -LEVELS, LEVELS)
    square = eye_of(width)
    index = lax.broadcasted_iota(jnp.int32, (HEAD_ROWS, width), 0)
    head = jnp.zeros((HEAD_ROWS, width), jnp.float32)
    for part in range(rows // width):
        for offset, column in enumerate((power, mantissa)):
            column = column[part * width : (part + 1) * width]
            line = jnp.sum(jnp.where(square, column, 0.0), axis=0, keepdims=True)
            head = jnp.where(index == 2 * part + offset, line, head)
    whole = jnp.concatenate([coded, head], axis=0)
    return whole.astype(jnp.int32).astype(jnp.int16)


def decode(coded):
    whole = coded.astype(jnp.int32).astype(jnp.float32)
    rows, width = whole.shape[0] - HEAD_ROWS, whole.shape[1]
    square = eye_of(width)
    columns = [[], []]
    for part in range(rows // width):
        for offset in range(2):
            start = rows + 2 * part + offset
            line = whole[start : start + 1]
            columns[offset].append(jnp.sum(jnp.where(square, line, 0.0), axis=1, keepdims=True))
    power, mantissa = (jnp.concatenate(parts, axis=0) for parts in columns)
    return whole[:rows] * (mantissa * jnp.exp2(power - MANTISSA_BITS) * (1.0 / LEVELS))


def encode_kernel(partial_ref, *coded_refs):
    own_rows = partial_ref.shape[0] // (len(coded_refs) + 1)
    for delta, coded_ref in enumerate(coded_refs, 1):
        coded_ref[...] = encode(partial_ref[delta * own_rows : (delta + 1) * own_rows, :])


def last_kernel(chunk, spot_ref, total_ref, other_ref, grad_in_ref, grad_out_ref):
    side, rep_index = spot_ref[0], spot_ref[1]
    half = grad_in_ref.shape[0] // 2
    piece = chunk // 2
    classes = grad_out_ref.shape[0]
    reps = (total_ref.shape[0] - half) // piece
    for part in range(2):

        def take(start, size):
            rows = pl.ds(start, size)
            return jnp.where(side == part, total_ref[rows, :], other_ref[rows, :])

        grad_in_ref[part * half : (part + 1) * half, :] = take(0, half)
        for r in range(reps):
            start = r * chunk + part * piece
            size = min(piece, classes - start)
            if size > 0:
                spot = pl.multiple_of(half + (r ^ rep_index) * piece, 8)
                grad_out_ref[start : start + size, :] = take(spot, piece)[:size]


def head_kernel(
    scale, reps, spot_ref, weight_ref, bias_ref, label_ref, mask_ref, own_ref, *refs
):
    coded_refs, refs = refs[: reps - 1], refs[reps - 1 :]
    logits_ref, own_terms_ref, sent_refs, terms_ref = refs[0], refs[1], refs[2:-1], refs[-1]
    own_rows, classes = logits_ref.shape
    total = own_ref[:own_rows, :]
    for coded_ref in coded_refs:
        total += decode(coded_ref[...])
    z_output = total.astype(jnp.bfloat16)
    square = eye_of(own_rows)
    label, mask = (
        jnp.sum(jnp.where(square, ref[...].astype(jnp.float32), 0.0), axis=1, keepdims=True)
        for ref in (label_ref, mask_ref)
    )
    logits = dot_wide(z_output, weight_ref[...]) + bias_ref[...]
    logits_ref[...] = logits
    shifted = jnp.exp(logits - jnp.max(logits, axis=1, keepdims=True))
    likelihood = shifted / jnp.sum(shifted, axis=1, keepdims=True)
    onehot = label.astype(jnp.int32) == lax.broadcasted_iota(jnp.int32, logits.shape, 1)
    slope = (likelihood - onehot.astype(jnp.float32)) * mask * scale
    slope = slope.astype(jnp.bfloat16)
    grad_rows = dot(slope, weight_ref[...]).astype(jnp.bfloat16)
    terms = lax.dot_general(
        slope, z_output, (((0,), (0,)), ((), ())), preferred_element_type=jnp.float32
    )
    terms_ref[:classes, :] = terms
    pad = terms_ref.shape[0] - classes
    if pad:
        terms_ref[classes:, :] = jnp.zeros((pad, terms.shape[1]), jnp.float32)
    chunk = own_terms_ref.shape[0]
    for delta, sent_ref in enumerate(sent_refs):
        start = pl.multiple_of((spot_ref[1] ^ delta) * chunk, 8)
        piece = terms_ref[pl.ds(start, chunk), :]
        sent_ref[:own_rows, :] = grad_rows
        sent_ref[own_rows:, :] = piece.astype(jnp.bfloat16)
        if delta == 0:
            own_terms_ref[...] = piece


def simple_call(body, shapes, name, *values, spot=(), scratch=()):
    smem = pl.BlockSpec(memory_space=pltpu.SMEM)
    vmem = pl.BlockSpec(memory_space=pltpu.VMEM)
    return pl.pallas_call(
        body,
        in_specs=[smem] * len(spot) + [vmem] * len(values),
        out_shape=shapes,
        scratch_shapes=scratch,
        compiler_params=pltpu.CompilerParams(vmem_limit_bytes=8 * 1024 * 1024),
        name=name,
    )(*spot, *values)


def dense_kernel(per_rep, tile_side, turn, meta_ref, tiles_ref, dense_ref):
    section = pl.program_id(0)
    rep_index, source_rep = meta_ref[section, 0], meta_ref[section, 1]
    edge = tiles_ref.shape[-1]
    dense_ref[...] = jnp.zeros_like(dense_ref)

    def put(slot, carried):
        place = meta_ref[section, 3 + slot]
        row = place // tile_side
        column = place % tile_side
        row = ((row // per_rep) ^ rep_index) * per_rep + row % per_rep
        column = ((column // per_rep) ^ source_rep) * per_rep + column % per_rep
        rows = pl.ds(pl.multiple_of(row * edge, edge), edge)
        columns = pl.ds(pl.multiple_of(column * edge, edge), edge)
        tile = tiles_ref[0, slot]
        if turn:
            dense_ref[columns, rows] = tile.T
        else:
            dense_ref[rows, columns] = tile
        return carried

    lax.fori_loop(0, meta_ref[section, 2], put, 0)


def build_dense(tiles, meta, own_rows, group_rows, turn):
    sections, slots, edge, _ = tiles.shape
    body = functools.partial(dense_kernel, own_rows // edge, group_rows // edge, turn)
    block = (group_rows, group_rows)
    shape = (sections * group_rows, group_rows) if turn else (group_rows, sections * group_rows)
    return pl.pallas_call(
        body,
        grid_spec=pltpu.PrefetchScalarGridSpec(
            num_scalar_prefetch=1,
            grid=(sections,),
            in_specs=[pl.BlockSpec((1, slots, edge, edge), lambda p, *_: (p, 0, 0, 0))],
            out_specs=pl.BlockSpec(block, lambda p, *_: (p, 0) if turn else (0, p)),
        ),
        out_shape=jax.ShapeDtypeStruct(shape, tiles.dtype),
        compiler_params=pltpu.CompilerParams(
            vmem_limit_bytes=4 * group_rows**2 + 8 * slots * edge**2 + (2 << 20)
        ),
        cost_estimate=pl.CostEstimate(
            flops=0, bytes_accessed=4 * sections * group_rows * group_rows, transcendentals=0
        ),
        name="dense_turned" if turn else "dense",
    )(meta, tiles)


def on_device(
    features,
    node_ids,
    labels,
    train_mask,
    tile_values,
    tile_place,
    tile_count,
    weight_in,
    weight_out,
    class_bias,
):
    own_rows = features.shape[1]
    reps = lax.axis_size("rep")
    blks = lax.axis_size("blk")
    rep_index = lax.axis_index("rep")
    blk_index = lax.axis_index("blk")
    sections = tile_values.shape[2]
    group_rows = own_rows * reps
    hidden_width = weight_in.shape[1]
    scale = 1.0 / math.sqrt(group_rows * blks)
    f32 = jnp.float32
    bf16 = jnp.bfloat16

    def swap(value, delta):
        if delta == 0:
            return value
        return lax.ppermute(value, "rep", [(r, r ^ delta) for r in range(reps)])

    def to_section(block, j):
        pairs = []
        for r in range(reps):
            for c in range(blks):
                member = c % sections + j
                if member < sections:
                    pairs.append((r * blks + c, r * blks + c + j))
                else:
                    pairs.append((r * blks + c, (r - 1) % reps * blks + c + j - sections))
        return lax.ppermute(block, ("rep", "blk"), pairs)

    def exchange(value, delta):
        return lax.ppermute(value, "blk", [(c, c ^ delta) for c in range(blks)])

    def to_pieces(value):
        pieces = []
        for delta in range(reps):
            pairs = []
            for r in range(reps):
                for c in range(blks):
                    target = r ^ delta
                    pairs.append((r * blks + c, target * blks + (c + sections * target) % blks))
            pieces.append(lax.ppermute(value, ("rep", "blk"), pairs))
        return pieces

    def to_all(pieces, size):
        parts = [
            jnp.concatenate(pieces[start : start + size], axis=0)
            for start in range(0, reps, size)
        ]
        blocks = list(parts)
        for j in range(1, sections):
            blocks += [to_section(part, j) for part in parts]
        return blocks

    side = lax.rem(blk_index, 2)

    def halve(value):
        half = value.shape[0] // 2
        theirs = exchange(lax.dynamic_slice_in_dim(value, (1 - side) * half, half, 0), 1)
        return lax.dynamic_slice_in_dim(value, side * half, half, 0) + theirs

    def sum_over(value, move, first, size):
        rounded = value.astype(bf16)
        moved = [move(rounded, d) for d in range(first, size, first)][::-1]
        parts = [rounded] + lax.optimization_barrier(moved)[::-1]
        parts = [part.astype(f32) for part in parts]
        while len(parts) > 1:
            parts = [parts[i] + parts[i + 1] for i in range(0, len(parts), 2)]
        return parts[0]

    def digits(ids):
        lanes = features.shape[2]
        parts = [ids & 255, (ids >> 8) & 255, ids >> 16]
        rows = jnp.concatenate([part.reshape(-1, lanes) for part in parts], axis=0)
        return jnp.pad(rows, ((0, -rows.shape[0] % 16), (0, 0))).astype(bf16)

    def undo_digits(rows):
        count = own_rows // rows.shape[1]
        parts = [rows[i * count : (i + 1) * count].astype(jnp.int32) for i in range(3)]
        return (parts[0] + (parts[1] << 8) + (parts[2] << 16)).reshape(own_rows)

    member = lax.rem(blk_index, sections)
    place, count = tile_place[0, 0], tile_count[0, 0]
    width = features.shape[2]
    arrived = to_pieces(features[0])
    tiles = tile_values[0, 0]
    next_rep = lax.rem(rep_index + 1, reps)
    where = jnp.where(member < jnp.arange(sections + 1) - 1, next_rep, rep_index)
    where, count, arrived[0] = lax.optimization_barrier((where, count, arrived[0]))
    columns = [jnp.broadcast_to(where[0], (sections, 1)), where[1:, None], count[:, None], place]
    meta, late_ids = lax.optimization_barrier((jnp.concatenate(columns, axis=1), node_ids[0]))
    dense = build_dense(tiles, meta, own_rows, group_rows, False)
    feature_columns = jnp.concatenate(to_all(arrived, reps // 2), axis=0)
    chunks = dot(dense, feature_columns).reshape(reps, own_rows, width)
    far_first = range(reps - 1, 0, -1)
    arrived = [swap(chunks[delta], delta) for delta in far_first]
    total = chunks[0]
    for part in arrived:
        total = total + part
    z_input = total.astype(bf16)
    z_bundle = jnp.concatenate([z_input, digits(late_ids)], axis=0)
    pieces = to_all(to_pieces(z_bundle), 1)
    units = jnp.arange(hidden_width, dtype=jnp.int32)

    def kept_of(parts):
        ids = jnp.concatenate([undo_digits(part) for part in parts])
        return keep_mask(ids[:, None], units[None, :])

    rows = [part[own_rows:] for part in pieces]
    rows[:reps], pieces[reps] = lax.optimization_barrier((rows[:reps], pieces[reps]))
    kept_own, rows[-1] = lax.optimization_barrier((kept_of(rows[:reps]), rows[-1]))
    kept = jnp.concatenate([kept_own, kept_of(rows[reps:])], axis=0)
    z_columns = jnp.concatenate([part[:own_rows] for part in pieces], axis=0)
    kept, z_columns = lax.optimization_barrier((kept, z_columns))
    third = f32(4.0 / 3.0)
    pre_act = dot(z_columns, weight_in)
    dropped = (jnp.maximum(pre_act, 0.0) * (kept.astype(f32) * third)).astype(bf16)
    dropped, z_again = lax.optimization_barrier((dropped, z_columns))
    second = dot(dense, dropped)
    mask = jnp.where(dot(z_again, weight_in) > 0, kept, jnp.zeros_like(kept))
    mask, ready = lax.optimization_barrier((mask, second))
    sent = simple_call(
        encode_kernel,
        [jax.ShapeDtypeStruct((own_rows + HEAD_ROWS, hidden_width), jnp.int16)] * (reps - 1),
        "encode", second,
    )
    arrived = [swap(sent[d - 1], d) for d in far_first]
    classes = weight_out.shape[1]
    chunk = -(-classes // (16 * reps)) * 16
    spot = jnp.stack([side, rep_index])
    logits, out_total, *sent = simple_call(
        functools.partial(head_kernel, scale, reps),
        [
            jax.ShapeDtypeStruct((own_rows, classes), f32),
            jax.ShapeDtypeStruct((chunk, hidden_width), f32),
        ]
        + [jax.ShapeDtypeStruct((own_rows + chunk, hidden_width), bf16)] * reps,
        "head",
        weight_out.T, class_bias[None], labels, train_mask,
        ready, *arrived,
        spot=(spot,),
        scratch=[pltpu.VMEM((chunk * reps, hidden_width), f32)],
    )
    arrived = [swap(sent[d], d) for d in range(reps - 1, -1, -1)][::-1]
    meta, out_total = lax.optimization_barrier((meta, out_total))
    turned = build_dense(tiles, meta, own_rows, group_rows, True)
    grad_block = jnp.concatenate([part[:own_rows] for part in arrived], axis=0)
    for part in arrived[1:]:
        out_total = out_total + part[own_rows:].astype(f32)
    grad_block, mask, out_total = lax.optimization_barrier((grad_block, mask, out_total))
    back = dot(turned, grad_block)
    pre_slope = (back * (mask.astype(f32) * third)).astype(bf16)
    pre_slope, out_total = lax.optimization_barrier((pre_slope, out_total))
    in_terms = lax.dot_general(
        z_columns, pre_slope, (((0,), (0,)), ((), ())), preferred_element_type=f32
    )
    half, piece = width // 2, chunk // 2

    def halves(which):
        rows = [
            lax.dynamic_slice_in_dim(in_terms, which * half, half, 0),
            lax.dynamic_slice_in_dim(out_total, which * piece, piece, 0),
        ]
        return jnp.concatenate(rows, axis=0)

    total = halves(side) + exchange(halves(1 - side), 1)
    total = sum_over(total, exchange, 2, blks).astype(bf16)
    arrived = [swap(total, d) for d in range(reps - 1, -1, -1)][::-1]
    parts = [part[:half].astype(f32) for part in arrived]
    while len(parts) > 1:
        parts = [parts[i] + parts[i + 1] for i in range(0, len(parts), 2)]
    total = jnp.concatenate(parts + [part[half:].astype(f32) for part in arrived], axis=0)
    grad_in, grad_wide = simple_call(
        functools.partial(last_kernel, chunk),
        [
            jax.ShapeDtypeStruct((width, hidden_width), f32),
            jax.ShapeDtypeStruct((classes, hidden_width), f32),
        ],
        "last", total, exchange(total, 1), spot=(spot,),
    )
    grad_out = grad_wide.T
    return (logits[None], grad_in, grad_out)


def solution(mesh):
    placed = (
        P("blk", "rep", None),
        P("blk", "rep"),
        P("blk", "rep"),
        P("blk", "rep"),
        P("blk", "rep", None, None, None, None),
        P("blk", "rep", None, None),
        P("blk", "rep", None),
        P(),
        P(),
        P(),
    )
    return jax.shard_map(
        on_device,
        mesh=mesh,
        in_specs=placed,
        out_specs=(P("blk", "rep", None), P(), P()),
        check_vma=False,
    )
```
